128 devices in a mesh: dp: 8 (over z_hi, x), tensor: 16 (over y, z_lo, core).
Axes of the slice: x: 4, y: 4, z: 4 (z_hi: 2, z_lo: 2; z = z_hi * 2 + z_lo), core: 2. Of those that a mesh axis runs over, the one named last changes fastest.
Arguments:
- inputs: bfloat16 [16, 1024, 2048], P('dp', 'tensor'), may hold values from -6 to 6
- teacher: bfloat16 [16, 1024, 2048], P('dp', 'tensor'), may hold values from -6 to 6
- segment_ids: int32 [16, 1024], P('dp'), may hold values from 0 to 3, never falling along the last dimension, each value on 1 to 512 neighbouring positions
- padding: int32 [16, 1024], P('dp', 'tensor'), may hold values from 0 to 1, as said below
- attn_gain: float32 [2048], replicated, may hold values from 0.5 to 1.5
- qkv_weight: bfloat16 [2048, 3, 2048], P('dp', None, 'tensor'), may hold values from -0.125 to 0.125
- beta_weight: bfloat16 [2048, 16], P('dp', 'tensor'), may hold values from -0.125 to 0.125
- conv_taps: bfloat16 [4, 3, 16, 128], P(None, None, 'tensor', 'dp'), may hold values from -4 to 4
- head_gain: bfloat16 [16, 128], P('tensor', 'dp'), may hold values from 0.5 to 1.5
- out_weight: bfloat16 [2048, 2048], P('tensor', 'dp'), may hold values from -0.125 to 0.125
- mlp_gain: float32 [2048], replicated, may hold values from 0.5 to 1.5
- gate_weight: bfloat16 [2048, 5632], P('dp', 'tensor'), may hold values from -0.125 to 0.125
- up_weight: bfloat16 [2048, 5632], P('dp', 'tensor'), may hold values from -0.125 to 0.125
- down_weight: bfloat16 [5632, 2048], P('tensor', 'dp'), may hold values from -0.15625 to 0.15625
Outputs:
- block_out: bfloat16 [16, 1024, 2048], P('dp', 'tensor')
- loss: float32 [], replicated
- input_grad: float32 [16, 1024, 2048], P('dp', 'tensor')
- attn_gain_grad: float32 [2048], replicated
- qkv_grad: float32 [2048, 3, 2048], P('dp', None, 'tensor')
- beta_grad: float32 [2048, 16], P('dp', 'tensor')
- taps_grad: float32 [4, 3, 16, 128], P(None, None, 'tensor', 'dp')
- head_gain_grad: float32 [16, 128], P('tensor', 'dp')
- out_grad: float32 [2048, 2048], P('tensor', 'dp')
- mlp_gain_grad: float32 [2048], replicated
- gate_grad: float32 [2048, 5632], P('dp', 'tensor')
- up_grad: float32 [2048, 5632], P('dp', 'tensor')
- down_grad: float32 [5632, 2048], P('tensor', 'dp')
The draws below stay inside these ranges and needn't reach their ends.
Inputs may be any that keep to these rules, and one draw needn't show every extreme that they name: `padding`: in each sequence the tokens that count form a leading run of 256 to 767 tokens; the rest are 0. `segment_ids`: document numbers never fall along a sequence; a document has 1 to 512 tokens.
All inputs are finite; a program needn't handle non-finite values.
Results may differ from the reference program's by a relative error of at most 0.029.
Values may be sent and summed in bfloat16 or wider, within the bound.
A program may use at most 192 MiB of HBM per device.

```python
import math
import jax
import jax.numpy as jnp
import numpy as np
from jax import lax

D = 2048
H = 16
HEAD = 128
FF = 5632
GROUP = 64
TAPS = 4
SEQ = 1024
DOCS = 4
SEQS = 16


def draw_padding(key, part):
    key = jax.random.fold_in(key, 7)
    lengths = jax.random.randint(key, (SEQS, 1), SEQ // 4, 3 * SEQ // 4)
    positions = jnp.arange(SEQ, dtype=jnp.int32)[None, :]
    return (positions < lengths).astype(jnp.int32)


def steps_of(stream_key, shape, pieces, smallest, largest):
    def one(position, shards_of):
        steps = jax.random.uniform(jax.random.fold_in(jax.random.fold_in(stream_key, 6), position), (shards_of,), jnp.float32, smallest / len(pieces), largest / len(pieces))
        return jnp.repeat(jnp.exp(steps), shape[position] // shards_of).reshape((-1,) + (1,) * (len(shape) - position - 1))

    level = one(*pieces[0])
    for cut in pieces[1:]:
        level = level * one(*cut)
    return level


def length_profile(count, total, bound, skew):
    loads = [(1 << 20) // math.isqrt(rank ** skew) + 1 for rank in range(2, count + 1)]
    spare, counts = total - bound - (count - 1), [1] * (count - 1)
    while spare > 0:
        candidates = [i for i in range(count - 1) if counts[i] < bound]
        whole, remaining = sum([loads[i] for i in candidates]), spare
        for i in candidates:
            more = min(bound - counts[i], max(1, remaining * loads[i] // whole), spare)
            counts[i] = counts[i] + more
            spare = spare - more
    return np.array([bound] + counts)


def ragged_sizes(own_key, number_of, total, limit, lean):
    if number_of == 2:
        one = jax.random.randint(own_key, (), max(1, total - limit), min(limit, total - 1) + 1)
        return jnp.stack([one, total - one])
    tallies = jnp.asarray(length_profile(number_of, total, limit, lean), jnp.int32)
    couples = (number_of - 1) // 2
    giver, taker = tallies[1:1 + 2 * couples:2], tallies[2:2 + 2 * couples:2]
    slack = jnp.minimum(giver - 1, limit - taker)
    passed = jax.random.randint(jax.random.fold_in(own_key, 1), (couples,), 0, 1 << 20) % (slack + 1)
    tallies = tallies.at[1:1 + 2 * couples:2].set(giver - passed).at[2:2 + 2 * couples:2].set(taker + passed)
    return tallies[jax.random.permutation(jax.random.fold_in(own_key, 2), number_of)]


def noise(own_key, dims, scale, most, pieces=(), kind=jnp.bfloat16):
    entries = jax.random.normal(own_key, dims, jnp.float32) * scale
    if len(pieces) > 0:
        entries = steps_of(own_key, dims, pieces, -0.22, 0.18) * entries
    return jnp.clip(entries, min=-most, max=most).astype(kind)


def setup_inputs(seed: int = 0) -> dict:
    key_list = jax.random.split(jax.random.key(seed), 15)
    return {
        "inputs": noise(key_list[0], (SEQS, SEQ, D), 1.0, 6.0, ((0, 8), (1, 16))),
        "teacher": noise(key_list[1], (SEQS, SEQ, D), 1.0, 6.0, ((0, 8), (1, 16))),
        "segment_ids": jax.vmap(lambda own: jnp.searchsorted(jnp.cumsum(ragged_sizes(own, DOCS, SEQ, SEQ // 2, 0)), jnp.arange(SEQ), side="right"))(jax.random.split(key_list[2], SEQS)).reshape((SEQS, SEQ)).astype(jnp.int32),
        "padding": draw_padding(jax.random.fold_in(key_list[14], 71), 0),
        "attn_gain": jnp.clip(1.0 + 0.1 * jax.random.normal(key_list[4], (D,), jnp.float32), 0.5, 1.5),
        "qkv_weight": noise(key_list[5], (D, 3, D), D ** -0.5, 0.125, ((0, 8), (2, 16))),
        "beta_weight": noise(key_list[6], (D, H), D ** -0.5, 0.125, ((0, 8), (1, 16))),
        "conv_taps": noise(key_list[7], (TAPS, 3, H, HEAD), 2 ** -0.5, 4.0, ((2, 16), (3, 8))),
        "head_gain": jnp.clip(1.0 + 0.1 * jax.random.normal(key_list[8], (H, HEAD), jnp.float32), 0.5, 1.5).astype(jnp.bfloat16),
        "out_weight": noise(key_list[9], (D, D), D ** -0.5, 0.125, ((0, 16), (1, 8))),
        "mlp_gain": jnp.clip(1.0 + 0.1 * jax.random.normal(key_list[10], (D,), jnp.float32), 0.5, 1.5),
        "gate_weight": noise(key_list[11], (D, FF), D ** -0.5, 0.125, ((0, 8), (1, 16))),
        "up_weight": noise(key_list[12], (D, FF), D ** -0.5, 0.125, ((0, 8), (1, 16))),
        "down_weight": noise(key_list[13], (FF, D), (FF // 4) ** -0.5, 0.15625, ((0, 16), (1, 8))),
    }


highest = lax.Precision.HIGHEST

@jax.custom_vjp
def low(v):
    return lax.optimization_barrier(v.astype(jnp.bfloat16)).astype(jnp.float32)

@jax.custom_vjp
def low_back(v):
    return v

def low_keep(v):
    return (low(v), None)

def low_pass(kept, grad):
    return (grad,)

def back_keep(v):
    return (v, None)

def back_low(kept, grad):
    return (low(grad),)
low.defvjp(low_keep, low_pass)
low_back.defvjp(back_keep, back_low)

def rms_norm(values, epsilon):
    return values * lax.rsqrt(lax.optimization_barrier(jnp.mean(values * values, -1, keepdims=True)) + epsilon)

def unit_norm(values):
    return values * lax.rsqrt(lax.optimization_barrier(jnp.sum(values * values, -1, keepdims=True)) + 1e-06)

def short_conv(fields, taps, segment):
    length = fields.shape[0]
    total = fields * taps[0]
    for offset in range(1, taps.shape[0]):
        blank_rows = jnp.zeros((offset,) + fields.shape[1:], fields.dtype)
        moved = jnp.concatenate([blank_rows, fields[:length - offset]], 0)
        earlier = jnp.concatenate([jnp.full((offset,), -1, jnp.int32), segment[:length - offset].astype(jnp.int32)], 0)
        keep = (earlier == segment.astype(jnp.int32)).astype(fields.dtype)
        total = total + moved * keep[:, None, None, None] * taps[offset]
    return total

def delta_block(carry, block):
    state, previous = carry
    query, keys, values, beta, segment = block
    size = segment.shape[0]
    dtype = state.dtype
    carried = (segment == previous).astype(dtype)
    same = (segment[:, None] == segment[None, :]).astype(dtype)
    strict = jnp.tril(jnp.ones((size, size), dtype), -1)
    within = jnp.tril(jnp.ones((size, size), dtype))
    gram = jnp.einsum('htk,hsk->hts', keys, keys, precision=highest)
    mixing = gram * beta[:, None, :] * (same * strict)
    recalled = jnp.einsum('htk,hvk->htv', keys, state, precision=highest)
    target = values - carried[None, :, None] * recalled
    system = jnp.eye(size, dtype=dtype)[None] + mixing
    updates = jax.vmap(lambda matrix, right: jax.scipy.linalg.solve_triangular(matrix, right, lower=True, unit_diagonal=True))(system, target)
    weighted = updates * beta[:, :, None]
    scores = jnp.einsum('htk,hsk->hts', query, keys, precision=highest) * (same * within)
    output = carried[None, :, None] * jnp.einsum('htk,hvk->htv', query, state, precision=highest)
    output = output + jnp.einsum('hts,hsv->htv', scores, weighted, precision=highest)
    closing = (segment == segment[size - 1]).astype(dtype)
    new_state = carried[size - 1] * state + jnp.einsum('hsv,hsk->hvk', weighted * closing[None, :, None], keys, precision=highest)
    return ((new_state, segment[size - 1]), output)

def mixer(projected, beta_logit, taps, head_gain, segment):
    length = projected.shape[0]
    heads = beta_logit.shape[1]
    width = taps.shape[-1]
    fields = projected.reshape(length, 3, heads, width)
    mixed = jax.nn.silu(short_conv(fields, taps, segment))
    query = unit_norm(mixed[:, 0]) * width ** (-0.5)
    keys = unit_norm(mixed[:, 1])
    values = mixed[:, 2]
    beta = jax.nn.sigmoid(beta_logit)
    blocks = length // GROUP

    def arrange(array):
        return jnp.transpose(array.reshape(blocks, GROUP, heads, width), (0, 2, 1, 3))
    beta_blocks = jnp.transpose(beta.reshape(blocks, GROUP, heads), (0, 2, 1))
    segment_blocks = segment.astype(jnp.int32).reshape(blocks, GROUP)
    start = (jnp.zeros((heads, width, width), projected.dtype), jnp.int32(-1))
    final, outputs = lax.scan(jax.checkpoint(delta_block), start, (arrange(query), arrange(keys), arrange(values), beta_blocks, segment_blocks))
    raw = jnp.transpose(outputs, (0, 2, 1, 3)).reshape(length, heads, width)
    normed = rms_norm(raw, 1e-05) * head_gain
    return normed.reshape(length, heads * width)

def layer(params, inputs, segment):
    attn_gain, qkv_weight, beta_weight, conv_taps, head_gain, out_weight, mlp_gain, gate_weight, up_weight, down_weight = params
    normed = low(rms_norm(inputs, 1e-06) * attn_gain)
    projected = low_back(jnp.einsum('sd,dcf->scf', normed, qkv_weight, precision=highest))
    beta_logit = low_back(jnp.dot(normed, beta_weight, precision=highest))
    heads = low(mixer(projected, beta_logit, conv_taps, head_gain, segment))
    attention = low_back(jnp.dot(heads, out_weight, precision=highest))
    hidden = inputs + attention
    ffn_in = low(rms_norm(hidden, 1e-06) * mlp_gain)
    gate = low_back(jnp.dot(ffn_in, gate_weight, precision=highest))
    up = low_back(jnp.dot(ffn_in, up_weight, precision=highest))
    act = low(jax.nn.silu(gate) * up)
    ffn_out = low_back(jnp.dot(act, down_weight, precision=highest))
    return hidden + ffn_out

def reference(inputs, teacher, segment_ids, padding, attn_gain, qkv_weight, beta_weight, conv_taps, head_gain, out_weight, mlp_gain, gate_weight, up_weight, down_weight):
    params = tuple((weight.astype(jnp.float32) for weight in (attn_gain, qkv_weight, beta_weight, conv_taps, head_gain, out_weight, mlp_gain, gate_weight, up_weight, down_weight)))
    valid = jnp.sum(padding).astype(jnp.float32)
    scale = SEQS * SEQ / valid

    def per_sequence(carry, item):
        totals, squares = carry
        tokens, target, segment, mask = item
        target32 = target.astype(jnp.float32)
        weights32 = mask.astype(jnp.float32)

        def objective(weights, values):
            result = layer(weights, values, segment)
            diff = result - target32
            errors = lax.optimization_barrier(jnp.sum(diff * diff, -1)) * weights32
            return (0.5 * scale * jnp.sum(errors), (result, jnp.sum(errors)))
        value, pullback, extra = jax.vjp(objective, params, tokens.astype(jnp.float32), has_aux=True)
        result, error_sum = extra
        weight_grads, token_grad = pullback(jnp.ones_like(value))
        totals = tuple((old + new for old, new in zip(totals, weight_grads)))
        return ((totals, squares + error_sum), (result.astype(jnp.bfloat16), token_grad))
    start = (tuple((jnp.zeros_like(weight) for weight in params)), jnp.zeros((), jnp.float32))
    finals, outputs = lax.scan(per_sequence, start, (inputs, teacher, segment_ids, padding))
    totals, squares = finals
    block_out, input_grad = outputs
    loss = squares / (valid * D)
    return (block_out, loss, input_grad, totals[0], totals[1], totals[2], totals[3], totals[4], totals[5], totals[6], totals[7], totals[8], totals[9])
```

```python
import jax
import jax.numpy as jnp
from jax import lax
from jax.experimental import pallas as pl
from jax.experimental.pallas import tpu as pltpu
from jax.sharding import PartitionSpec as P

CHUNK = 128
WIDE = 512
PARAMS = pltpu.CompilerParams(vmem_limit_bytes=56 << 20)


def nn(a, b):
    return jnp.dot(a, b, preferred_element_type=jnp.float32)


def nt(a, b):
    return lax.dot_general(a, b, (((1,), (1,)), ((), ())), preferred_element_type=jnp.float32)


def tn(a, b):
    return lax.dot_general(a, b, (((0,), (0,)), ((), ())), preferred_element_type=jnp.float32)


def low(value):
    return value.astype(jnp.bfloat16)


def split(value):
    high = low(value)
    return high, low(value - high.astype(jnp.float32))


def fine(product, a, b):
    a_high, a_rest = a
    b_high, b_rest = b
    return product(a_high, b_high) + (product(a_high, b_rest) + product(a_rest, b_high))


def grid_masks():
    row = lax.broadcasted_iota(jnp.int32, (CHUNK, CHUNK), 0)
    column = lax.broadcasted_iota(jnp.int32, (CHUNK, CHUNK), 1)
    return row, column


def rows_of(index, sequence):
    first = pl.multiple_of(index * 256 + sequence * 64, 64)
    second = pl.multiple_of(index * 256 + 128 + sequence * 64, 64)
    return first, second


def load(ref, index, sequence, lanes=slice(None)):
    first, second = rows_of(index, sequence)
    return jnp.concatenate([ref[pl.ds(first, 64), lanes], ref[pl.ds(second, 64), lanes]], 0)


def store(ref, index, sequence, value, lanes=slice(None)):
    first, second = rows_of(index, sequence)
    ref[pl.ds(first, 64), lanes] = value[:64]
    ref[pl.ds(second, 64), lanes] = value[64:]


def columns_of(pos_ref, index, sequence):
    line = pos_ref[pl.ds(index * 2 + sequence, 1), :]
    return line, jnp.broadcast_to(line, (CHUNK, CHUNK)).T


def convolve(proj_ref, taps_ref, index, sequence, place):
    fields = slice(0, 384)
    current = load(proj_ref, index, sequence, fields)
    before = pl.multiple_of(jnp.maximum(index * 256 - 128 + sequence * 64 + 56, 0), 8)
    window = jnp.concatenate([proj_ref[pl.ds(before, 8), fields], current], 0)
    total = current * taps_ref[0:1, :]
    moved = [current]
    for offset in range(1, 4):
        keep = (place[:, 0:1] >= offset).astype(jnp.float32)
        shifted = window[8 - offset : 8 - offset + CHUNK] * keep
        moved.append(shifted)
        total = total + shifted * taps_ref[offset : offset + 1, :]
    return total, moved


def activate(total):
    sigma = jax.nn.sigmoid(total)
    act = total * sigma
    query, keys, values = act[:, :128], act[:, 128:256], act[:, 256:]
    query_scale = lax.rsqrt(jnp.sum(query * query, -1, keepdims=True) + 1e-06)
    key_scale = lax.rsqrt(jnp.sum(keys * keys, -1, keepdims=True) + 1e-06)
    return sigma, query * query_scale, query_scale, keys * key_scale, key_scale, values


def inverse(mixing, row, column):
    eye = (row == column).astype(jnp.float32)
    total = eye - jnp.where((row // 2) == (column // 2), mixing, 0.0)
    size = 2
    while size < CHUNK:
        corner = (
            ((row // (2 * size)) == (column // (2 * size)))
            & (((row // size) % 2) == 1)
            & (((column // size) % 2) == 0)
        )
        held = split(total)
        inner = split(fine(nn, held, split(jnp.where(corner, mixing, 0.0))))
        total = total - fine(nn, inner, held)
        size *= 2
    return total


def mixer_forward(
    proj_ref, pos_ref, taps_ref, gain_ref,
    heads_ref, query_ref, key_ref, inv_ref, kc_ref, score_ref, step_ref, state_ref, update_ref, raw_ref,
    free_ref, shift_ref,
):
    row, column = grid_masks()
    depth = row - column

    def prepare(index, carry):
        for sequence in range(2):
            line, place = columns_of(pos_ref, index, sequence)
            total, _ = convolve(proj_ref, taps_ref, index, sequence, place)
            beta = jax.nn.sigmoid(load(proj_ref, index, sequence, slice(384, 512)))
            _, query, _, keys, _, values = activate(total)
            query = query * 128 ** (-0.5)
            last = line[:, 127:128]
            within = (depth >= 0) & (depth.astype(jnp.float32) <= place)
            carried = place > row.astype(jnp.float32)
            closing = (127 - row).astype(jnp.float32) <= last
            gram = fine(nt, split(keys), split(keys * beta))
            solved = low(inverse(jnp.where(within & (depth > 0), gram, 0.0), row, column))
            right = jnp.concatenate([low(jnp.where(carried, keys, 0.0)), low(values)], 1)
            both = nn(solved, right)
            key_low = low(keys)
            query_low = low(query)
            score = jnp.where(within, nt(query_low, key_low), 0.0)
            weight = jnp.where(closing, beta, 0.0)
            ends = tn(key_low, low(jnp.concatenate([weight, weight], 1) * both))
            through = jnp.where((row == column) & (last > 127.0), 1.0, 0.0)
            block = index * 2 + sequence
            store(query_ref, index, sequence, query_low)
            store(key_ref, index, sequence, key_low)
            inv_ref[block] = solved
            kc_ref[block] = low(both[:, :128])
            free_ref[block] = both[:, 128:]
            score_ref[block] = low(score)
            step_ref[block] = low(through - ends[:, :128])
            shift_ref[block] = ends[:, 128:]
        return carry

    lax.fori_loop(0, 8, prepare, 0)

    def advance(index, states):
        new = []
        for sequence in range(2):
            block = index * 2 + sequence
            state_low = low(states[sequence])
            state_ref[block] = state_low
            new.append(nn(step_ref[block], state_low) + shift_ref[block])
        return tuple(new)

    zero = jnp.zeros((CHUNK, CHUNK), jnp.float32)
    states = (zero, zero)
    for index in range(8):
        states = advance(index, states)

    def finish(index, carry):
        for sequence in range(2):
            block = index * 2 + sequence
            _, place = columns_of(pos_ref, index, sequence)
            carried = place > row.astype(jnp.float32)
            beta = jax.nn.sigmoid(load(proj_ref, index, sequence, slice(384, 512)))
            state = state_ref[block]
            update = free_ref[block] - nn(kc_ref[block], state)
            output = jnp.where(carried, nn(load(query_ref, index, sequence), state), 0.0)
            output = output + nn(score_ref[block], low(beta * update))
            scale = lax.rsqrt(jnp.mean(output * output, -1, keepdims=True) + 1e-05)
            update_ref[block] = update
            raw_ref[block] = output
            store(heads_ref, index, sequence, low(output * scale * gain_ref[0:1, :]))
        return carry

    lax.fori_loop(0, 8, finish, 0)


def mixer_backward(
    grad_ref, proj_ref, pos_ref, taps_ref, gain_ref,
    query_ref, key_ref, inv_ref, kc_ref, score_ref, step_ref, state_ref, update_ref, raw_ref,
    out_ref, taps_grad_ref, gain_grad_ref,
    back_ref, pull_ref, flow_ref, enter_ref, pre_ref, place_ref,
):
    row, column = grid_masks()
    depth = row - column
    taps_grad_ref[...] = jnp.zeros_like(taps_grad_ref)
    gain_grad_ref[...] = jnp.zeros_like(gain_grad_ref)

    def prepare(index, carry):
        for sequence in range(2):
            block = index * 2 + sequence
            _, place = columns_of(pos_ref, index, sequence)
            carried = place > row.astype(jnp.float32)
            beta = jax.nn.sigmoid(load(proj_ref, index, sequence, slice(384, 512)))
            grad = load(grad_ref, index, sequence)
            output = raw_ref[block]
            scale = lax.rsqrt(jnp.mean(output * output, -1, keepdims=True) + 1e-05)
            unit = output * scale
            inner = grad * gain_ref[0:1, :]
            gain_grad_ref[0:1, :] += jnp.sum(grad * unit, 0, keepdims=True)
            back = scale * (inner - unit * jnp.mean(inner * unit, -1, keepdims=True))
            back_low = low(back)
            pull = tn(score_ref[block], back_low)
            left = jnp.concatenate([load(query_ref, index, sequence), kc_ref[block]], 0)
            right = jnp.concatenate([jnp.where(carried, back_low, 0.0), low(-beta * pull)], 0)
            enter_ref[block] = tn(left, right)
            back_ref[block] = back_low
            pull_ref[block] = pull
        return carry

    lax.fori_loop(0, 8, prepare, 0)

    def retreat(step, flows):
        index = 7 - step
        new = []
        for sequence in range(2):
            block = index * 2 + sequence
            flow_low = low(flows[sequence])
            flow_ref[block] = flow_low
            new.append(tn(step_ref[block], flow_low) + enter_ref[block])
        return tuple(new)

    zero = jnp.zeros((CHUNK, CHUNK), jnp.float32)
    flows = (zero, zero)
    for step in range(8):
        flows = retreat(step, flows)

    def collect(index, carry):
        for sequence in range(2):
            block = index * 2 + sequence
            line, place = columns_of(pos_ref, index, sequence)
            total, moved = convolve(proj_ref, taps_ref, index, sequence, place)
            sigma, query, query_scale, keys, key_scale, values = activate(total)
            beta = jax.nn.sigmoid(load(proj_ref, index, sequence, slice(384, 512)))
            last = line[:, 127:128]
            within = (depth >= 0) & (depth.astype(jnp.float32) <= place)
            later = (depth < 0) & ((-depth).astype(jnp.float32) <= line)
            carried = place > row.astype(jnp.float32)
            closing = (127 - row).astype(jnp.float32) <= last
            query_low = load(query_ref, index, sequence)
            key_low = load(key_ref, index, sequence)
            update = update_ref[block]
            weighted = beta * update
            flow = flow_ref[block]
            state = state_ref[block]
            back = back_ref[block]
            weight_grad = pull_ref[block] + jnp.where(closing, nn(key_low, flow), 0.0)
            score_grad = low(jnp.where(within, nt(back, low(weighted)), 0.0))
            right_grad = tn(inv_ref[block], low(beta * weight_grad))
            right_low = low(right_grad)
            mixing_grad = jnp.where(later, -nt(low(update), right_low), 0.0)
            gram = nt(key_low, key_low)
            beta_grad = jnp.sum(weight_grad * update + mixing_grad * gram, -1, keepdims=True)
            gram_grad = low(beta * mixing_grad)
            key_grad = nt(
                jnp.concatenate(
                    [low(jnp.where(closing, weighted, 0.0)), low(jnp.where(carried, -right_grad, 0.0))], 1
                ),
                jnp.concatenate([flow, state], 1),
            )
            key_grad = key_grad + tn(
                jnp.concatenate([score_grad, gram_grad], 0), jnp.concatenate([query_low, key_low], 0)
            )
            key_grad = key_grad + nn(gram_grad, key_low)
            query_grad = nt(jnp.where(carried, back, 0.0), state) + nn(score_grad, key_low)
            query_grad = query_grad * 128 ** (-0.5)
            query_act = query_scale * (
                query_grad - query * jnp.sum(query * query_grad, -1, keepdims=True)
            )
            key_act = key_scale * (key_grad - keys * jnp.sum(keys * key_grad, -1, keepdims=True))
            act_grad = jnp.concatenate([query_act, key_act, right_grad], 1)
            pre_grad = act_grad * (sigma * (1.0 + total * (1.0 - sigma)))
            for offset in range(4):
                taps_grad_ref[offset : offset + 1, :] += jnp.sum(
                    pre_grad * moved[offset], 0, keepdims=True
                )
            store(pre_ref, index, sequence, pre_grad)
            store(place_ref, index, sequence, place)
            logit_grad = jnp.where(column == 0, beta_grad * beta * (1.0 - beta), 0.0)
            store(out_ref, index, sequence, low(logit_grad), slice(384, 512))
        return carry

    lax.fori_loop(0, 8, collect, 0)

    def spread(index, carry):
        for sequence in range(2):
            after = pl.multiple_of(jnp.minimum(index * 256 + 256, 1792) + sequence * 64, 64)
            live = jnp.where(index == 7, 0.0, 1.0)
            current = load(pre_ref, index, sequence)
            window = jnp.concatenate([current, pre_ref[pl.ds(after, 8), :] * live], 0)
            place = load(place_ref, index, sequence)
            places = jnp.concatenate([place, place_ref[pl.ds(after, 8), :]], 0)[:, 0:1]
            total = current * taps_ref[0:1, :]
            for offset in range(1, 4):
                masked = window * (places >= offset).astype(jnp.float32)
                total = total + masked[offset : offset + CHUNK] * taps_ref[offset : offset + 1, :]
            store(out_ref, index, sequence, low(total), slice(0, 384))
        return carry

    lax.fori_loop(0, 8, spread, 0)


def saved_shapes():
    rows = jax.ShapeDtypeStruct((2048, CHUNK), jnp.bfloat16)
    small = jax.ShapeDtypeStruct((16, CHUNK, CHUNK), jnp.bfloat16)
    wide = jax.ShapeDtypeStruct((16, CHUNK, CHUNK), jnp.float32)
    return (rows, rows, small, small, small, small, small, wide, wide)


def run_forward(proj, pos, taps, gain):
    heads = jax.ShapeDtypeStruct((2048, CHUNK), jnp.bfloat16)
    return pl.pallas_call(
        mixer_forward,
        out_shape=(heads,) + saved_shapes(),
        in_specs=[pl.BlockSpec(memory_space=pltpu.VMEM)] * 4,
        out_specs=[pl.BlockSpec(memory_space=pltpu.VMEM)] * 10,
        scratch_shapes=[
            pltpu.VMEM((16, CHUNK, CHUNK), jnp.float32),
            pltpu.VMEM((16, CHUNK, CHUNK), jnp.float32),
        ],
        compiler_params=PARAMS,
        cost_estimate=pl.CostEstimate(flops=16 << 30, bytes_accessed=16 << 20, transcendentals=0),
        name="mixer_forward",
    )(proj, pos, taps, gain)


def run_backward(grad, proj, pos, taps, gain, saved):
    return pl.pallas_call(
        mixer_backward,
        out_shape=(
            jax.ShapeDtypeStruct((2048, WIDE), jnp.bfloat16),
            jax.ShapeDtypeStruct((8, 384), jnp.float32),
            jax.ShapeDtypeStruct((8, CHUNK), jnp.float32),
        ),
        in_specs=[pl.BlockSpec(memory_space=pltpu.VMEM)] * 14,
        out_specs=[pl.BlockSpec(memory_space=pltpu.VMEM)] * 3,
        scratch_shapes=[
            pltpu.VMEM((16, CHUNK, CHUNK), jnp.bfloat16),
            pltpu.VMEM((16, CHUNK, CHUNK), jnp.float32),
            pltpu.VMEM((16, CHUNK, CHUNK), jnp.bfloat16),
            pltpu.VMEM((16, CHUNK, CHUNK), jnp.float32),
            pltpu.VMEM((2048, 384), jnp.float32),
            pltpu.VMEM((2048, CHUNK), jnp.float32),
        ],
        compiler_params=PARAMS,
        cost_estimate=pl.CostEstimate(flops=32 << 30, bytes_accessed=16 << 20, transcendentals=0),
        name="mixer_backward",
    )(grad, proj, pos, taps, gain, *saved)


def token_places(segment):
    length = segment.shape[1]
    before = jnp.sum((segment[:, None, :] < segment[:, :, None]).astype(jnp.int32), -1)
    place = jnp.arange(length, dtype=jnp.int32)[None, :] - before
    return jnp.transpose(place.reshape(2, 8, CHUNK), (1, 0, 2)).reshape(16, CHUNK).astype(jnp.float32)


def pad_lanes(array, width):
    return jnp.pad(array, ((0, 0), (0, width - array.shape[1])))


def f32(value):
    return value.astype(jnp.float32)


def body(
    inputs, teacher, segment_ids, padding, attn_gain, qkv_weight, beta_weight, conv_taps, head_gain,
    out_weight, mlp_gain, gate_weight, up_weight, down_weight,
):
    hidden_units = gate_weight.shape[1]
    rows = 128
    features = inputs.shape[2]
    valid = f32(lax.psum(jnp.sum(padding), ("dp", "tensor")))
    scale = 16 * 1024 / valid

    small = jnp.concatenate([conv_taps.reshape(12, 16), head_gain.reshape(1, 16)], 0).reshape(1, 208)
    small = jnp.pad(small, ((0, 7), (0, WIDE - 208)))
    mix_shard = jnp.concatenate(
        [qkv_weight.reshape(256, 384), jnp.broadcast_to(beta_weight, (256, CHUNK))], 1
    )
    mix_all = lax.all_gather(jnp.concatenate([mix_shard, small], 0), "dp", axis=0)
    mix_full = mix_all[:, :256].reshape(2048, WIDE)
    small_all = f32(jnp.transpose(mix_all[:, 256, :208].reshape(8, 13, 16), (1, 0, 2)).reshape(13, CHUNK))
    taps = jnp.pad(small_all[:12].reshape(4, 384), ((0, 4), (0, 0)))
    gain = jnp.pad(small_all[12:], ((0, 7), (0, 0)))

    tokens = f32(inputs.reshape(rows, features))
    attn_scale = lax.rsqrt(jnp.mean(tokens * tokens, -1, keepdims=True) + 1e-06)
    attn_unit = tokens * attn_scale
    normed = (attn_unit * attn_gain).astype(jnp.bfloat16)
    gathered = lax.all_gather(normed, "tensor", axis=0, tiled=True)

    ffn_shard = jnp.concatenate(
        [pad_lanes(gate_weight, 384), pad_lanes(up_weight, 384), pad_lanes(jnp.transpose(down_weight), 384)], 1
    )
    ffn_full = lax.all_gather(ffn_shard, "dp", axis=0, tiled=True)
    gate_up, down_t = ffn_full[:, :768], ffn_full[:, 768:]
    out_all = lax.all_gather(lax.all_gather(jnp.transpose(out_weight), "dp", axis=0, tiled=True), "tensor", axis=1, tiled=True)

    proj = nn(gathered, mix_full)
    pos = token_places(segment_ids)
    heads, *saved = run_forward(proj, pos, taps, gain)
    spread = lax.all_to_all(heads.reshape(16, rows, CHUNK), "tensor", 0, 0, tiled=True)
    heads_rows = jnp.transpose(spread, (1, 0, 2)).reshape(rows, features)
    hidden = tokens + nt(heads_rows, out_all)

    mlp_scale = lax.rsqrt(jnp.mean(hidden * hidden, -1, keepdims=True) + 1e-06)
    mlp_unit = hidden * mlp_scale
    ffn_in = (mlp_unit * mlp_gain).astype(jnp.bfloat16)
    ffn_all = lax.all_gather(ffn_in, "tensor", axis=0, tiled=True)
    both = nn(ffn_all, gate_up)
    gate, up = both[:, :384], both[:, 384:]
    sigma = jax.nn.sigmoid(gate)
    act = (gate * sigma * up).astype(jnp.bfloat16)
    output = hidden + f32(
        lax.psum_scatter(nt(act, down_t).astype(jnp.bfloat16), "tensor", scatter_dimension=0, tiled=True)
    )
    diff = output - f32(teacher.reshape(rows, features))
    mask = f32(padding.reshape(rows, 1))
    squares = jnp.sum(jnp.sum(diff * diff, -1, keepdims=True) * mask)
    block_grad = scale * mask * diff

    ffn_grad_all = lax.all_gather(block_grad.astype(jnp.bfloat16), "tensor", axis=0, tiled=True)
    act_grad = nn(ffn_grad_all, down_t)
    gate_low = (act_grad * up * sigma * (1.0 + gate * (1.0 - sigma))).astype(jnp.bfloat16)
    up_low = (act_grad * gate * sigma).astype(jnp.bfloat16)
    both_low = jnp.concatenate([gate_low, up_low], 1)
    mlp_grad = f32(
        lax.psum_scatter(nt(both_low, gate_up).astype(jnp.bfloat16), "tensor", scatter_dimension=0, tiled=True)
    )
    ffn_part = jnp.concatenate([tn(ffn_all, both_low), tn(ffn_grad_all, act)], 1).astype(jnp.bfloat16)
    ffn_grads = f32(lax.psum_scatter(ffn_part, "dp", scatter_dimension=0, tiled=True))

    mlp_sum = jnp.sum(mlp_grad * mlp_unit, 0)
    mlp_inner = mlp_grad * mlp_gain
    hidden_grad = block_grad + mlp_scale * (
        mlp_inner - mlp_unit * jnp.mean(mlp_inner * mlp_unit, -1, keepdims=True)
    )
    attention_low = hidden_grad.astype(jnp.bfloat16)
    heads_grad_rows = nn(attention_low, out_all).astype(jnp.bfloat16)
    heads_grad = lax.all_to_all(
        jnp.transpose(heads_grad_rows.reshape(rows, 16, CHUNK), (1, 0, 2)), "tensor", 0, 0, tiled=True
    ).reshape(2048, CHUNK)
    attention_all = lax.all_gather(attention_low, "tensor", axis=0, tiled=True)
    out_part = tn(attention_all, heads).astype(jnp.bfloat16)

    proj_low, taps_part, gain_part = run_backward(f32(heads_grad), proj, pos, taps, gain, saved)
    attn_grad = f32(
        lax.psum_scatter(
            nt(proj_low, jnp.where(jnp.arange(WIDE) <= 384, mix_full, 0)).astype(jnp.bfloat16),
            "tensor", scatter_dimension=0, tiled=True,
        )
    )
    mix_part = tn(gathered, proj_low)[:, :385]
    small_part = jnp.concatenate([taps_part[:4].reshape(12, CHUNK), gain_part[:1]], 0)
    small_part = jnp.transpose(small_part.reshape(13, 8, 16), (1, 0, 2)).reshape(8, 208)
    small_part = jnp.pad(small_part, ((0, 0), (0, 48))).reshape(2048, 1)
    mix_part = jnp.concatenate([mix_part, small_part, jnp.zeros((2048, 126), jnp.float32)], 1)
    mix_part = jnp.concatenate([mix_part.astype(jnp.bfloat16), out_part], 1)
    mix_grads = f32(lax.psum_scatter(mix_part, "dp", scatter_dimension=0, tiled=True))

    attn_sum = jnp.sum(attn_grad * attn_unit, 0)
    attn_inner = attn_grad * attn_gain
    input_grad = hidden_grad + attn_scale * (
        attn_inner - attn_unit * jnp.mean(attn_inner * attn_unit, -1, keepdims=True)
    )
    attn_total, mlp_total, square_total = lax.psum((attn_sum, mlp_sum, squares), ("dp", "tensor"))
    loss = square_total / (valid * features)
    small_grad = mix_grads[:208, 385].reshape(13, 16)
    shape = (2, 64, features)
    return (
        output.astype(jnp.bfloat16).reshape(shape),
        loss,
        input_grad.reshape(shape),
        attn_total,
        mix_grads[:, :384].reshape(256, 3, CHUNK),
        mix_grads[:, 384:385],
        small_grad[:12].reshape(4, 3, 1, 16),
        small_grad[12:].reshape(1, 16),
        jnp.transpose(mix_grads[:, 512:]),
        mlp_total,
        ffn_grads[:, :hidden_units],
        ffn_grads[:, 384 : 384 + hidden_units],
        jnp.transpose(ffn_grads[:, 768 : 768 + hidden_units]),
    )


def solution(mesh):
    in_specs = (
        P("dp", "tensor", None),
        P("dp", "tensor", None),
        P("dp", None),
        P("dp", "tensor"),
        P(),
        P("dp", None, "tensor"),
        P("dp", "tensor"),
        P(None, None, "tensor", "dp"),
        P("tensor", "dp"),
        P("tensor", "dp"),
        P(),
        P("dp", "tensor"),
        P("dp", "tensor"),
        P("tensor", "dp"),
    )
    out_specs = (
        P("dp", "tensor", None),
        P(),
        P("dp", "tensor", None),
        P(),
        P("dp", None, "tensor"),
        P("dp", "tensor"),
        P(None, None, "tensor", "dp"),
        P("tensor", "dp"),
        P("tensor", "dp"),
        P(),
        P("dp", "tensor"),
        P("dp", "tensor"),
        P("tensor", "dp"),
    )
    return jax.shard_map(body, mesh=mesh, in_specs=in_specs, out_specs=out_specs, check_vma=False)
```

```python
import jax
import jax.numpy as jnp
from jax import lax
from jax.experimental import pallas as pl
from jax.experimental.pallas import tpu as pltpu
from jax.sharding import PartitionSpec as P

MESH = pl.DeviceIdType.MESH
CHUNK = 128
WIDE = 512
PARAMS = pltpu.CompilerParams(vmem_limit_bytes=56 << 20)


def nn(a, b):
    return jnp.dot(a, b, preferred_element_type=jnp.float32)


def nt(a, b):
    return lax.dot_general(a, b, (((1,), (1,)), ((), ())), preferred_element_type=jnp.float32)


def tn(a, b):
    return lax.dot_general(a, b, (((0,), (0,)), ((), ())), preferred_element_type=jnp.float32)


def low(value):
    return value.astype(jnp.bfloat16)


def split(value):
    high = low(value)
    return high, low(value - high.astype(jnp.float32))


def fine(product, a, b):
    a_high, a_rest = a
    b_high, b_rest = b
    return product(a_high, b_high) + (product(a_high, b_rest) + product(a_rest, b_high))


def grid_masks():
    row = lax.broadcasted_iota(jnp.int32, (CHUNK, CHUNK), 0)
    column = lax.broadcasted_iota(jnp.int32, (CHUNK, CHUNK), 1)
    return row, column


def rows_of(index, sequence):
    first = pl.multiple_of(index * 256 + sequence * 64, 64)
    second = pl.multiple_of(index * 256 + 128 + sequence * 64, 64)
    return first, second


def load(ref, index, sequence, lanes=slice(None)):
    first, second = rows_of(index, sequence)
    return jnp.concatenate([ref[pl.ds(first, 64), lanes], ref[pl.ds(second, 64), lanes]], 0)


def store(ref, index, sequence, value, lanes=slice(None)):
    first, second = rows_of(index, sequence)
    ref[pl.ds(first, 64), lanes] = value[:64]
    ref[pl.ds(second, 64), lanes] = value[64:]


def columns_of(pos_ref, index, sequence):
    line = pos_ref[pl.ds(index * 2 + sequence, 1), :]
    return line, jnp.broadcast_to(line, (CHUNK, CHUNK)).T


def convolve(proj_ref, taps_ref, index, sequence, place):
    fields = slice(0, 384)
    current = load(proj_ref, index, sequence, fields)
    before = pl.multiple_of(jnp.maximum(index * 256 - 128 + sequence * 64 + 56, 0), 8)
    window = jnp.concatenate([proj_ref[pl.ds(before, 8), fields], current], 0)
    total = current * taps_ref[0:1, :]
    moved = [current]
    for offset in range(1, 4):
        keep = (place[:, 0:1] >= offset).astype(jnp.float32)
        shifted = window[8 - offset : 8 - offset + CHUNK] * keep
        moved.append(shifted)
        total = total + shifted * taps_ref[offset : offset + 1, :]
    return total, moved


def activate(total):
    sigma = jax.nn.sigmoid(total)
    act = total * sigma
    query, keys, values = act[:, :128], act[:, 128:256], act[:, 256:]
    query_scale = lax.rsqrt(jnp.sum(query * query, -1, keepdims=True) + 1e-06)
    key_scale = lax.rsqrt(jnp.sum(keys * keys, -1, keepdims=True) + 1e-06)
    return sigma, query * query_scale, query_scale, keys * key_scale, key_scale, values


def inverse(mixing, row, column):
    eye = (row == column).astype(jnp.float32)
    total = eye - jnp.where((row // 2) == (column // 2), mixing, 0.0)
    size = 2
    while size < CHUNK:
        corner = (
            ((row // (2 * size)) == (column // (2 * size)))
            & (((row // size) % 2) == 1)
            & (((column // size) % 2) == 0)
        )
        held = split(total)
        inner = split(fine(nn, held, split(jnp.where(corner, mixing, 0.0))))
        total = total - fine(nn, inner, held)
        size *= 2
    return total


def mixer_forward(
    proj_ref, pos_ref, taps_ref, gain_ref,
    heads_ref, query_ref, key_ref, inv_ref, kc_ref, score_ref, step_ref, state_ref, update_ref, raw_ref,
    free_ref, shift_ref,
):
    row, column = grid_masks()
    depth = row - column

    def prepare(index, carry):
        for sequence in range(2):
            line, place = columns_of(pos_ref, index, sequence)
            total, _ = convolve(proj_ref, taps_ref, index, sequence, place)
            beta = jax.nn.sigmoid(load(proj_ref, index, sequence, slice(384, 512)))
            _, query, _, keys, _, values = activate(total)
            query = query * 128 ** (-0.5)
            last = line[:, 127:128]
            within = (depth >= 0) & (depth.astype(jnp.float32) <= place)
            carried = place > row.astype(jnp.float32)
            closing = (127 - row).astype(jnp.float32) <= last
            gram = fine(nt, split(keys), split(keys * beta))
            solved = low(inverse(jnp.where(within & (depth > 0), gram, 0.0), row, column))
            right = jnp.concatenate([low(jnp.where(carried, keys, 0.0)), low(values)], 1)
            both = nn(solved, right)
            key_low = low(keys)
            query_low = low(query)
            score = jnp.where(within, nt(query_low, key_low), 0.0)
            weight = jnp.where(closing, beta, 0.0)
            ends = tn(key_low, low(jnp.concatenate([weight, weight], 1) * both))
            through = jnp.where((row == column) & (last > 127.0), 1.0, 0.0)
            block = index * 2 + sequence
            store(query_ref, index, sequence, query_low)
            store(key_ref, index, sequence, key_low)
            inv_ref[block] = solved
            kc_ref[block] = low(both[:, :128])
            free_ref[block] = both[:, 128:]
            score_ref[block] = low(score)
            step_ref[block] = low(through - ends[:, :128])
            shift_ref[block] = ends[:, 128:]
        return carry

    lax.fori_loop(0, 8, prepare, 0)

    def advance(index, states):
        new = []
        for sequence in range(2):
            block = index * 2 + sequence
            state_low = low(states[sequence])
            state_ref[block] = state_low
            new.append(nn(step_ref[block], state_low) + shift_ref[block])
        return tuple(new)

    zero = jnp.zeros((CHUNK, CHUNK), jnp.float32)
    states = (zero, zero)
    for index in range(8):
        states = advance(index, states)

    def finish(index, carry):
        for sequence in range(2):
            block = index * 2 + sequence
            _, place = columns_of(pos_ref, index, sequence)
            carried = place > row.astype(jnp.float32)
            beta = jax.nn.sigmoid(load(proj_ref, index, sequence, slice(384, 512)))
            state = state_ref[block]
            update = free_ref[block] - nn(kc_ref[block], state)
            output = jnp.where(carried, nn(load(query_ref, index, sequence), state), 0.0)
            output = output + nn(score_ref[block], low(beta * update))
            scale = lax.rsqrt(jnp.mean(output * output, -1, keepdims=True) + 1e-05)
            update_ref[block] = update
            raw_ref[block] = output
            store(heads_ref, index, sequence, low(output * scale * gain_ref[0:1, :]))
        return carry

    lax.fori_loop(0, 8, finish, 0)


def mixer_backward(
    grad_ref, proj_ref, pos_ref, taps_ref, gain_ref,
    query_ref, key_ref, inv_ref, kc_ref, score_ref, step_ref, state_ref, update_ref, raw_ref,
    out_ref, taps_grad_ref, gain_grad_ref,
    back_ref, pull_ref, flow_ref, enter_ref, pre_ref, place_ref,
):
    row, column = grid_masks()
    depth = row - column
    taps_grad_ref[...] = jnp.zeros_like(taps_grad_ref)
    gain_grad_ref[...] = jnp.zeros_like(gain_grad_ref)

    def prepare(index, carry):
        for sequence in range(2):
            block = index * 2 + sequence
            _, place = columns_of(pos_ref, index, sequence)
            carried = place > row.astype(jnp.float32)
            beta = jax.nn.sigmoid(load(proj_ref, index, sequence, slice(384, 512)))
            grad = load(grad_ref, index, sequence)
            output = raw_ref[block]
            scale = lax.rsqrt(jnp.mean(output * output, -1, keepdims=True) + 1e-05)
            unit = output * scale
            inner = grad * gain_ref[0:1, :]
            gain_grad_ref[0:1, :] += jnp.sum(grad * unit, 0, keepdims=True)
            back = scale * (inner - unit * jnp.mean(inner * unit, -1, keepdims=True))
            back_low = low(back)
            pull = tn(score_ref[block], back_low)
            left = jnp.concatenate([load(query_ref, index, sequence), kc_ref[block]], 0)
            right = jnp.concatenate([jnp.where(carried, back_low, 0.0), low(-beta * pull)], 0)
            enter_ref[block] = tn(left, right)
            back_ref[block] = back_low
            pull_ref[block] = pull
        return carry

    lax.fori_loop(0, 8, prepare, 0)

    def retreat(step, flows):
        index = 7 - step
        new = []
        for sequence in range(2):
            block = index * 2 + sequence
            flow_low = low(flows[sequence])
            flow_ref[block] = flow_low
            new.append(tn(step_ref[block], flow_low) + enter_ref[block])
        return tuple(new)

    zero = jnp.zeros((CHUNK, CHUNK), jnp.float32)
    flows = (zero, zero)
    for step in range(8):
        flows = retreat(step, flows)

    def collect(index, carry):
        for sequence in range(2):
            block = index * 2 + sequence
            line, place = columns_of(pos_ref, index, sequence)
            total, moved = convolve(proj_ref, taps_ref, index, sequence, place)
            sigma, query, query_scale, keys, key_scale, values = activate(total)
            beta = jax.nn.sigmoid(load(proj_ref, index, sequence, slice(384, 512)))
            last = line[:, 127:128]
            within = (depth >= 0) & (depth.astype(jnp.float32) <= place)
            later = (depth < 0) & ((-depth).astype(jnp.float32) <= line)
            carried = place > row.astype(jnp.float32)
            closing = (127 - row).astype(jnp.float32) <= last
            query_low = load(query_ref, index, sequence)
            key_low = load(key_ref, index, sequence)
            update = update_ref[block]
            weighted = beta * update
            flow = flow_ref[block]
            state = state_ref[block]
            back = back_ref[block]
            weight_grad = pull_ref[block] + jnp.where(closing, nn(key_low, flow), 0.0)
            score_grad = low(jnp.where(within, nt(back, low(weighted)), 0.0))
            right_grad = tn(inv_ref[block], low(beta * weight_grad))
            right_low = low(right_grad)
            mixing_grad = jnp.where(later, -nt(low(update), right_low), 0.0)
            gram = nt(key_low, key_low)
            beta_grad = jnp.sum(weight_grad * update + mixing_grad * gram, -1, keepdims=True)
            gram_grad = low(beta * mixing_grad)
            key_grad = nt(
                jnp.concatenate(
                    [low(jnp.where(closing, weighted, 0.0)), low(jnp.where(carried, -right_grad, 0.0))], 1
                ),
                jnp.concatenate([flow, state], 1),
            )
            key_grad = key_grad + tn(
                jnp.concatenate([score_grad, gram_grad], 0), jnp.concatenate([query_low, key_low], 0)
            )
            key_grad = key_grad + nn(gram_grad, key_low)
            query_grad = nt(jnp.where(carried, back, 0.0), state) + nn(score_grad, key_low)
            query_grad = query_grad * 128 ** (-0.5)
            query_act = query_scale * (
                query_grad - query * jnp.sum(query * query_grad, -1, keepdims=True)
            )
            key_act = key_scale * (key_grad - keys * jnp.sum(keys * key_grad, -1, keepdims=True))
            act_grad = jnp.concatenate([query_act, key_act, right_grad], 1)
            pre_grad = act_grad * (sigma * (1.0 + total * (1.0 - sigma)))
            for offset in range(4):
                taps_grad_ref[offset : offset + 1, :] += jnp.sum(
                    pre_grad * moved[offset], 0, keepdims=True
                )
            store(pre_ref, index, sequence, pre_grad)
            store(place_ref, index, sequence, place)
            logit_grad = jnp.where(column == 0, beta_grad * beta * (1.0 - beta), 0.0)
            store(out_ref, index, sequence, low(logit_grad), slice(384, 512))
        return carry

    lax.fori_loop(0, 8, collect, 0)

    def spread(index, carry):
        for sequence in range(2):
            after = pl.multiple_of(jnp.minimum(index * 256 + 256, 1792) + sequence * 64, 64)
            live = jnp.where(index == 7, 0.0, 1.0)
            current = load(pre_ref, index, sequence)
            window = jnp.concatenate([current, pre_ref[pl.ds(after, 8), :] * live], 0)
            place = load(place_ref, index, sequence)
            places = jnp.concatenate([place, place_ref[pl.ds(after, 8), :]], 0)[:, 0:1]
            total = current * taps_ref[0:1, :]
            for offset in range(1, 4):
                masked = window * (places >= offset).astype(jnp.float32)
                total = total + masked[offset : offset + CHUNK] * taps_ref[offset : offset + 1, :]
            store(out_ref, index, sequence, low(total), slice(0, 384))
        return carry

    lax.fori_loop(0, 8, spread, 0)


def saved_shapes():
    rows = jax.ShapeDtypeStruct((2048, CHUNK), jnp.bfloat16)
    small = jax.ShapeDtypeStruct((16, CHUNK, CHUNK), jnp.bfloat16)
    wide = jax.ShapeDtypeStruct((16, CHUNK, CHUNK), jnp.float32)
    return (rows, rows, small, small, small, small, small, wide, wide)


def run_forward(proj, pos, taps, gain):
    heads = jax.ShapeDtypeStruct((2048, CHUNK), jnp.bfloat16)
    return pl.pallas_call(
        mixer_forward,
        out_shape=(heads,) + saved_shapes(),
        in_specs=[pl.BlockSpec(memory_space=pltpu.VMEM)] * 4,
        out_specs=[pl.BlockSpec(memory_space=pltpu.VMEM)] * 10,
        scratch_shapes=[
            pltpu.VMEM((16, CHUNK, CHUNK), jnp.float32),
            pltpu.VMEM((16, CHUNK, CHUNK), jnp.float32),
        ],
        compiler_params=PARAMS,
        cost_estimate=pl.CostEstimate(flops=16 << 30, bytes_accessed=16 << 20, transcendentals=0),
        name="mixer_forward",
    )(proj, pos, taps, gain)


def run_backward(grad, proj, pos, taps, gain, saved):
    return pl.pallas_call(
        mixer_backward,
        out_shape=(
            jax.ShapeDtypeStruct((2048, WIDE), jnp.bfloat16),
            jax.ShapeDtypeStruct((8, 384), jnp.float32),
            jax.ShapeDtypeStruct((8, CHUNK), jnp.float32),
        ),
        in_specs=[pl.BlockSpec(memory_space=pltpu.VMEM)] * 14,
        out_specs=[pl.BlockSpec(memory_space=pltpu.VMEM)] * 3,
        scratch_shapes=[
            pltpu.VMEM((16, CHUNK, CHUNK), jnp.bfloat16),
            pltpu.VMEM((16, CHUNK, CHUNK), jnp.float32),
            pltpu.VMEM((16, CHUNK, CHUNK), jnp.bfloat16),
            pltpu.VMEM((16, CHUNK, CHUNK), jnp.float32),
            pltpu.VMEM((2048, 384), jnp.float32),
            pltpu.VMEM((2048, CHUNK), jnp.float32),
        ],
        compiler_params=PARAMS,
        cost_estimate=pl.CostEstimate(flops=32 << 30, bytes_accessed=16 << 20, transcendentals=0),
        name="mixer_backward",
    )(grad, proj, pos, taps, gain, *saved)


def spot(y, z, core):
    return (y * 2 + z) * 2 + core


class Neighbours:
    def __init__(self):
        index = lax.axis_index("tensor")
        self.core = index % 2
        self.z = (index // 2) % 2
        self.y = index // 4
        up, down, far = (self.y + 1) % 4, (self.y + 3) % 4, (self.y + 2) % 4
        other = 1 - self.z
        self.up = spot(up, self.z, self.core)
        self.down = spot(down, self.z, self.core)
        self.side = spot(self.y, other, self.core)
        self.twin = spot(self.y, self.z, 1 - self.core)
        self.chips = {
            "own": self.y * 2 + self.z,
            "side": self.y * 2 + other,
            "down": down * 2 + self.z,
            "up": up * 2 + self.z,
            "downside": down * 2 + other,
            "upside": up * 2 + other,
            "far": far * 2 + self.z,
            "farside": far * 2 + other,
        }

    def mine(self, name):
        return self.chips[name] * 2 + self.core

    def twins(self, name):
        return self.chips[name] * 2 + 1 - self.core

    def chip_at(self, step):
        quarter = step // 2
        shift = quarter + quarter // 2 - 2 * (quarter // 3)
        return ((self.y + shift) % 4) * 2 + (self.z + step % 2) % 2


def greet(devices):
    barrier = pltpu.get_barrier_semaphore()
    for device in devices:
        pl.semaphore_signal(barrier, inc=1, device_id=device, device_id_type=MESH)
    pl.semaphore_wait(barrier, len(devices))


def remote(source, target, send_sem, recv_sem, device):
    return pltpu.make_async_remote_copy(
        src_ref=source, dst_ref=target, send_sem=send_sem, recv_sem=recv_sem,
        device_id=device, device_id_type=MESH,
    )


TOP, BOTTOM, WHOLE = pl.ds(0, 64), pl.ds(64, 64), pl.ds(0, 128)
NAMES = ("own", "side", "down", "up", "downside", "upside", "far", "farside")


class Gather:
    copies = 17

    def __init__(self, near, buffer, sends, receives):
        self.near, self.buffer, self.sends, self.receives = near, buffer, sends, receives

    def send(self, key, block, rows, device):
        piece = self.buffer.at[block, rows]
        copy = remote(piece, piece, self.sends.at[key], self.receives.at[key], {"tensor": device})
        copy.start()

    def arrive(self, key, block, rows=WHOLE):
        piece = self.buffer.at[block, rows]
        remote(
            piece, piece, self.sends.at[key], self.receives.at[key], {"tensor": self.near.twin}
        ).wait_recv()

    def to_twin(self, name):
        self.send(9 + NAMES.index(name), self.near.mine(name), WHOLE, self.near.twin)

    def from_twin(self, name):
        self.arrive(9 + NAMES.index(name), self.near.twins(name))

    def start(self):
        near = self.near
        own = near.mine("own")
        self.send(1, own, WHOLE, near.up)
        self.send(2, own, WHOLE, near.down)
        self.send(0, own, WHOLE, near.side)
        self.to_twin("own")

    def second(self):
        near = self.near
        self.arrive(1, near.mine("down"))
        self.send(5, near.mine("down"), TOP, near.up)
        self.arrive(2, near.mine("up"))
        self.send(6, near.mine("up"), BOTTOM, near.down)
        self.arrive(0, near.mine("side"))
        self.send(3, near.mine("side"), WHOLE, near.up)
        self.send(4, near.mine("side"), WHOLE, near.down)
        self.to_twin("side")
        self.to_twin("up")
        self.to_twin("down")

    def third(self):
        near = self.near
        far = near.mine("far")
        self.arrive(5, far, TOP)
        self.send(7, far, TOP, near.side)
        self.arrive(6, far, BOTTOM)
        self.send(8, far, BOTTOM, near.side)
        self.to_twin("far")

    def fourth(self):
        near = self.near
        self.arrive(4, near.mine("upside"))
        self.to_twin("upside")
        self.arrive(3, near.mine("downside"))
        self.to_twin("downside")

    def fifth(self):
        far = self.near.mine("farside")
        self.arrive(7, far, TOP)
        self.arrive(8, far, BOTTOM)
        self.to_twin("farside")

    def finish(self):
        near = self.near
        names = ("own", "own", "own", "side", "side", "down", "up", "far", "far") + NAMES
        for key, name in enumerate(names):
            rows = {5: TOP, 6: BOTTOM, 7: TOP, 8: BOTTOM}.get(key, WHOLE)
            piece = self.buffer.at[near.mine(name), rows]
            remote(
                piece, piece, self.sends.at[key], self.receives.at[key], {"tensor": near.twin}
            ).wait_send()

    def before(self, step):
        @pl.when(step == 0)
        def _():
            self.from_twin("own")

        @pl.when(step == 1)
        def _():
            self.second()
            self.from_twin("side")

        @pl.when(step == 2)
        def _():
            self.from_twin("up")

        @pl.when(step == 3)
        def _():
            self.third()
            self.fourth()
            self.from_twin("upside")

        @pl.when(step == 4)
        def _():
            self.from_twin("down")

        @pl.when(step == 5)
        def _():
            self.from_twin("downside")

        @pl.when(step == 6)
        def _():
            self.from_twin("far")

        @pl.when(step == 7)
        def _():
            self.fifth()
            self.from_twin("farside")


def add_rows(target, sources, count=128):
    def piece(index, carry):
        rows = pl.ds(pl.multiple_of(index * 16, 16), 16)
        total = target[rows].astype(jnp.float32)
        for source in sources:
            total = total + source[rows].astype(jnp.float32)
        target[rows] = total.astype(target.dtype)
        return carry

    lax.fori_loop(0, count // 16, piece, 0)


class Scatter:
    slots = 8
    copies = 16

    def __init__(self, near, part, twin_part, slot, sends, receives):
        self.near, self.part, self.twin_part, self.slot = near, part, twin_part, slot
        self.sends, self.receives = sends, receives

    def describe(self, key, source, target, device):
        return remote(source, target, self.sends.at[key], self.receives.at[key], {"tensor": device})

    def twin_copy(self, chip):
        return self.describe(
            8 + chip, self.part.at[chip * 2 + 1 - self.near.core], self.twin_part.at[chip], self.near.twin
        )

    def to_twin(self, chip):
        self.twin_copy(chip).start()

    def chip_sum(self, name):
        chip = self.near.chips[name]
        self.twin_copy(chip).wait_recv()
        add_rows(self.part.at[chip * 2 + self.near.core], [self.twin_part.at[chip]])

    def outgoing(self):
        near, part, slot = self.near, self.part, self.slot
        return (
            (0, part.at[near.mine("farside")], slot.at[0], near.side),
            (1, part.at[near.mine("far"), TOP], slot.at[1, TOP], near.down),
            (2, part.at[near.mine("far"), BOTTOM], slot.at[2, BOTTOM], near.up),
            (3, part.at[near.mine("downside")], slot.at[3], near.down),
            (4, part.at[near.mine("upside")], slot.at[4], near.up),
            (5, part.at[near.mine("down")], slot.at[5], near.down),
            (6, part.at[near.mine("up")], slot.at[6], near.up),
            (7, part.at[near.mine("side")], slot.at[7], near.side),
        )

    def send(self, key):
        self.describe(*self.outgoing()[key]).start()

    def arrive(self, key):
        self.describe(*self.outgoing()[key]).wait_recv()

    def first(self):
        self.chip_sum("farside")
        self.send(0)
        self.chip_sum("downside")
        self.send(3)
        self.chip_sum("upside")
        self.send(4)
        self.chip_sum("far")
        self.chip_sum("down")
        self.chip_sum("up")
        self.chip_sum("side")

    def second(self):
        near, part, slot = self.near, self.part, self.slot
        self.arrive(0)
        add_rows(part.at[near.mine("far")], [slot.at[0]])
        self.send(1)
        self.send(2)

    def third(self):
        near, part, slot = self.near, self.part, self.slot
        self.arrive(3)
        self.arrive(4)
        add_rows(part.at[near.mine("side")], [slot.at[3], slot.at[4]])
        self.send(7)
        self.arrive(1)
        add_rows(part.at[near.mine("down"), TOP], [slot.at[1, TOP]], 64)
        self.send(5)
        self.arrive(2)
        add_rows(part.at[near.mine("up"), BOTTOM], [slot.at[2, BOTTOM]], 64)
        self.send(6)

    def fourth(self):
        near = self.near
        chip = near.chips["own"]
        self.twin_copy(chip).wait_recv()
        for key in (7, 5, 6):
            self.arrive(key)
        return self.part.at[chip * 2 + near.core], self.twin_part.at[chip]

    def total(self, rows):
        near = self.near
        chip = near.chips["own"]
        value = self.part[chip * 2 + near.core, rows].astype(jnp.float32)
        value = value + self.twin_part[chip, rows].astype(jnp.float32)
        for key in (5, 6, 7):
            value = value + self.slot[key, rows].astype(jnp.float32)
        return value

    def finish(self):
        for chip in range(8):
            self.twin_copy(chip).wait_send()
        for copy in self.outgoing():
            self.describe(*copy).wait_send()


HIDDEN = 384


def sigmoid(value):
    return 1.0 / (1.0 + jnp.exp(-value))


def ffn_kernel(
    input_ref, hidden_ref, teacher_ref, mask_ref, gate_up_ref, down_ref,
    block_ref, grad_ref, back_ref, square_ref, weight_ref,
    tokens, grads, both, act_t, both_t, part, twin_part, slot,
    gather_send, gather_recv, scatter_send, scatter_recv,
    again_send, again_recv, return_send, return_recv,
):
    near = Neighbours()
    neighbours = [{"tensor": device} for device in (near.up, near.down, near.side, near.twin)]
    own = near.mine("own")
    tokens[own] = input_ref[...]
    greet(neighbours)
    gather = Gather(near, tokens, gather_send, gather_recv)
    gather.start()
    scatter = Scatter(near, part, twin_part, slot, scatter_send, scatter_recv)

    def rows_at(buffer, chip):
        return jnp.concatenate([buffer[chip * 2], buffer[chip * 2 + 1]], 0)

    def forward(step, carry):
        gather.before(step)
        chip = near.chip_at(step)
        rows = pl.ds(pl.multiple_of(chip * 256, 256), 256)
        product = nn(rows_at(tokens, chip), gate_up_ref[...])
        both[rows, :] = product
        gate, up = product[:, :HIDDEN], product[:, HIDDEN:]
        act = low(gate * sigmoid(gate) * up)
        act_t[:, rows] = act.T
        partial = low(nt(act, down_ref[...]))
        part[chip * 2] = partial[:128]
        part[chip * 2 + 1] = partial[128:]
        scatter.to_twin(chip)
        return carry

    lax.fori_loop(0, 8, forward, 0)
    scatter.first()
    scatter.second()
    scatter.third()
    scatter.fourth()

    def middle(index, squares):
        rows = pl.ds(pl.multiple_of(index * 16, 16), 16)
        output = hidden_ref[rows] + scatter.total(rows)
        block_ref[rows] = low(output)
        diff = output - teacher_ref[rows].astype(jnp.float32)
        weight = mask_ref[0, rows, 0:1]
        grad = mask_ref[1, rows, 0:1] * diff
        grad_ref[rows] = grad
        grads[own, rows] = low(grad)
        return squares + weight * jnp.sum(diff * diff, -1, keepdims=True)

    squares = lax.fori_loop(0, 8, middle, jnp.zeros((16, 1), jnp.float32))
    square_ref[...] = jnp.broadcast_to(jnp.sum(squares, 0, keepdims=True), (8, 128))
    gather.finish()
    scatter.finish()

    again = Gather(near, grads, again_send, again_recv)
    again.start()
    back = Scatter(near, part, twin_part, slot, return_send, return_recv)

    def backward(step, carry):
        again.before(step)
        chip = near.chip_at(step)
        rows = pl.ds(pl.multiple_of(chip * 256, 256), 256)
        act_grad = nn(rows_at(grads, chip), down_ref[...])
        gate, up = both[rows, :HIDDEN], both[rows, HIDDEN:]
        sigma = sigmoid(gate)
        gate_low = low(act_grad * up * sigma * (1.0 + gate * (1.0 - sigma)))
        up_low = low(act_grad * gate * sigma)
        both_low = jnp.concatenate([gate_low, up_low], 1)
        both_t[:, rows] = both_low.T
        partial = low(nt(both_low, gate_up_ref[...]))
        part[chip * 2] = partial[:128]
        part[chip * 2 + 1] = partial[128:]
        back.to_twin(chip)
        return carry

    lax.fori_loop(0, 8, backward, 0)
    back.first()

    def weights(step, carry):
        @pl.when(step == 2)
        def _():
            back.second()

        @pl.when(step == 4)
        def _():
            back.third()

        lanes = pl.ds(pl.multiple_of(step * 256, 256), 256)
        for source, values, first, count in ((both_t, tokens, 0, 2 * HIDDEN), (act_t, grads, 2 * HIDDEN, HIDDEN)):
            column = values[:, :, lanes].reshape(2048, 256)
            weight_ref[pl.ds(first, count), lanes] = low(nn(source[...], column))
        return carry

    lax.fori_loop(0, 8, weights, 0)
    back.fourth()

    def ending(index, carry):
        rows = pl.ds(pl.multiple_of(index * 16, 16), 16)
        back_ref[rows] = back.total(rows)
        return carry

    lax.fori_loop(0, 8, ending, 0)
    again.finish()
    back.finish()


def run_ffn(ffn_in, hidden, teacher, mask, gate_up, down_t):
    rows, features = ffn_in.shape
    wide = jax.ShapeDtypeStruct((rows, features), jnp.float32)
    vmem = pl.BlockSpec(memory_space=pltpu.VMEM)
    semaphores = []
    for _ in range(2):
        for count in (Gather.copies, Gather.copies, Scatter.copies, Scatter.copies):
            semaphores.append(pltpu.SemaphoreType.DMA((count,)))
    return pl.pallas_call(
        ffn_kernel,
        out_shape=(
            jax.ShapeDtypeStruct((rows, features), jnp.bfloat16),
            wide,
            wide,
            jax.ShapeDtypeStruct((8, 128), jnp.float32),
            jax.ShapeDtypeStruct((3 * HIDDEN, features), jnp.bfloat16),
        ),
        in_specs=[vmem] * 6,
        out_specs=[vmem] * 5,
        scratch_shapes=[
            pltpu.VMEM((16, 128, 2048), jnp.bfloat16),
            pltpu.VMEM((16, 128, 2048), jnp.bfloat16),
            pltpu.VMEM((2048, 2 * HIDDEN), jnp.float32),
            pltpu.VMEM((HIDDEN, 2048), jnp.bfloat16),
            pltpu.VMEM((2 * HIDDEN, 2048), jnp.bfloat16),
            pltpu.VMEM((16, 128, 2048), jnp.bfloat16),
            pltpu.VMEM((8, 128, 2048), jnp.bfloat16),
            pltpu.VMEM((8, 128, 2048), jnp.bfloat16),
        ]
        + semaphores,
        compiler_params=pltpu.CompilerParams(
            collective_id=1, has_side_effects=True, vmem_limit_bytes=63 << 20
        ),
        cost_estimate=pl.CostEstimate(flops=160 << 30, bytes_accessed=16 << 20, transcendentals=0),
        name="feed_forward",
    )(ffn_in, hidden, teacher, mask, gate_up, down_t)


def token_places(segment):
    length = segment.shape[1]
    before = jnp.sum((segment[:, None, :] < segment[:, :, None]).astype(jnp.int32), -1)
    place = jnp.arange(length, dtype=jnp.int32)[None, :] - before
    return jnp.transpose(place.reshape(2, 8, CHUNK), (1, 0, 2)).reshape(16, CHUNK).astype(jnp.float32)


def pad_lanes(array, width):
    return jnp.pad(array, ((0, 0), (0, width - array.shape[1])))


def f32(value):
    return value.astype(jnp.float32)


def body(
    inputs, teacher, segment_ids, padding, attn_gain, qkv_weight, beta_weight, conv_taps, head_gain,
    out_weight, mlp_gain, gate_weight, up_weight, down_weight,
):
    hidden_units = gate_weight.shape[1]
    rows = 128
    features = inputs.shape[2]
    valid = f32(lax.psum(jnp.sum(padding), ("dp", "tensor")))
    scale = 16 * 1024 / valid

    small = jnp.concatenate([conv_taps.reshape(12, 16), head_gain.reshape(1, 16)], 0).reshape(1, 208)
    small = jnp.pad(small, ((0, 7), (0, WIDE - 208)))
    mix_shard = jnp.concatenate(
        [qkv_weight.reshape(256, 384), jnp.broadcast_to(beta_weight, (256, CHUNK))], 1
    )
    mix_all = lax.all_gather(jnp.concatenate([mix_shard, small], 0), "dp", axis=0)
    mix_full = mix_all[:, :256].reshape(2048, WIDE)
    small_all = f32(jnp.transpose(mix_all[:, 256, :208].reshape(8, 13, 16), (1, 0, 2)).reshape(13, CHUNK))
    taps = jnp.pad(small_all[:12].reshape(4, 384), ((0, 4), (0, 0)))
    gain = jnp.pad(small_all[12:], ((0, 7), (0, 0)))

    tokens = f32(inputs.reshape(rows, features))
    attn_scale = lax.rsqrt(jnp.mean(tokens * tokens, -1, keepdims=True) + 1e-06)
    attn_unit = tokens * attn_scale
    normed = (attn_unit * attn_gain).astype(jnp.bfloat16)
    gathered = lax.all_gather(normed, "tensor", axis=0, tiled=True)

    ffn_shard = jnp.concatenate(
        [pad_lanes(gate_weight, 384), pad_lanes(up_weight, 384), pad_lanes(jnp.transpose(down_weight), 384)], 1
    )
    ffn_full = lax.all_gather(ffn_shard, "dp", axis=0, tiled=True)
    gate_up, down_t = ffn_full[:, :768], ffn_full[:, 768:]
    out_all = lax.all_gather(lax.all_gather(jnp.transpose(out_weight), "dp", axis=0, tiled=True), "tensor", axis=1, tiled=True)

    proj = nn(gathered, mix_full)
    pos = token_places(segment_ids)
    heads, *saved = run_forward(proj, pos, taps, gain)
    spread = lax.all_to_all(heads.reshape(16, rows, CHUNK), "tensor", 0, 0, tiled=True)
    heads_rows = jnp.transpose(spread, (1, 0, 2)).reshape(rows, features)
    hidden = tokens + nt(heads_rows, out_all)

    mlp_scale = lax.rsqrt(jnp.mean(hidden * hidden, -1, keepdims=True) + 1e-06)
    mlp_unit = hidden * mlp_scale
    ffn_in = (mlp_unit * mlp_gain).astype(jnp.bfloat16)
    mask = f32(padding.reshape(rows, 1))
    masks = jnp.broadcast_to(jnp.stack([mask, scale * mask]), (2, rows, CHUNK))
    output, block_grad, mlp_grad, square_tile, ffn_part = run_ffn(
        ffn_in, hidden, teacher.reshape(rows, features), masks, gate_up, down_t
    )
    squares = square_tile[0, 0]
    ffn_grads = f32(lax.psum_scatter(ffn_part, "dp", scatter_dimension=1, tiled=True))

    mlp_sum = jnp.sum(mlp_grad * mlp_unit, 0)
    mlp_inner = mlp_grad * mlp_gain
    hidden_grad = block_grad + mlp_scale * (
        mlp_inner - mlp_unit * jnp.mean(mlp_inner * mlp_unit, -1, keepdims=True)
    )
    attention_low = hidden_grad.astype(jnp.bfloat16)
    heads_grad_rows = nn(attention_low, out_all).astype(jnp.bfloat16)
    heads_grad = lax.all_to_all(
        jnp.transpose(heads_grad_rows.reshape(rows, 16, CHUNK), (1, 0, 2)), "tensor", 0, 0, tiled=True
    ).reshape(2048, CHUNK)
    attention_all = lax.all_gather(attention_low, "tensor", axis=0, tiled=True)
    out_part = tn(attention_all, heads).astype(jnp.bfloat16)

    proj_low, taps_part, gain_part = run_backward(f32(heads_grad), proj, pos, taps, gain, saved)
    attn_grad = f32(
        lax.psum_scatter(
            nt(proj_low, jnp.where(jnp.arange(WIDE) <= 384, mix_full, 0)).astype(jnp.bfloat16),
            "tensor", scatter_dimension=0, tiled=True,
        )
    )
    mix_part = tn(gathered, proj_low)[:, :385]
    small_part = jnp.concatenate([taps_part[:4].reshape(12, CHUNK), gain_part[:1]], 0)
    small_part = jnp.transpose(small_part.reshape(13, 8, 16), (1, 0, 2)).reshape(8, 208)
    small_part = jnp.pad(small_part, ((0, 0), (0, 48))).reshape(2048, 1)
    mix_part = jnp.concatenate([mix_part, small_part, jnp.zeros((2048, 126), jnp.float32)], 1)
    mix_part = jnp.concatenate([mix_part.astype(jnp.bfloat16), out_part], 1)
    mix_grads = f32(lax.psum_scatter(mix_part, "dp", scatter_dimension=0, tiled=True))

    attn_sum = jnp.sum(attn_grad * attn_unit, 0)
    attn_inner = attn_grad * attn_gain
    input_grad = hidden_grad + attn_scale * (
        attn_inner - attn_unit * jnp.mean(attn_inner * attn_unit, -1, keepdims=True)
    )
    attn_total, mlp_total, square_total = lax.psum((attn_sum, mlp_sum, squares), ("dp", "tensor"))
    loss = square_total / (valid * features)
    small_grad = mix_grads[:208, 385].reshape(13, 16)
    shape = (2, 64, features)
    return (
        output.reshape(shape),
        loss,
        input_grad.reshape(shape),
        attn_total,
        mix_grads[:, :384].reshape(256, 3, CHUNK),
        mix_grads[:, 384:385],
        small_grad[:12].reshape(4, 3, 1, 16),
        small_grad[12:].reshape(1, 16),
        jnp.transpose(mix_grads[:, 512:]),
        mlp_total,
        jnp.transpose(ffn_grads[:hidden_units]),
        jnp.transpose(ffn_grads[384 : 384 + hidden_units]),
        ffn_grads[768 : 768 + hidden_units],
    )


def solution(mesh):
    in_specs = (
        P("dp", "tensor", None),
        P("dp", "tensor", None),
        P("dp", None),
        P("dp", "tensor"),
        P(),
        P("dp", None, "tensor"),
        P("dp", "tensor"),
        P(None, None, "tensor", "dp"),
        P("tensor", "dp"),
        P("tensor", "dp"),
        P(),
        P("dp", "tensor"),
        P("dp", "tensor"),
        P("tensor", "dp"),
    )
    out_specs = (
        P("dp", "tensor", None),
        P(),
        P("dp", "tensor", None),
        P(),
        P("dp", None, "tensor"),
        P("dp", "tensor"),
        P(None, None, "tensor", "dp"),
        P("tensor", "dp"),
        P("tensor", "dp"),
        P(),
        P("dp", "tensor"),
        P("dp", "tensor"),
        P("tensor", "dp"),
    )
    return jax.shard_map(body, mesh=mesh, in_specs=in_specs, out_specs=out_specs, check_vma=False)
```

```python
import jax
import jax.numpy as jnp
from jax import lax
from jax.experimental import pallas as pl
from jax.experimental.pallas import tpu as pltpu
from jax.sharding import PartitionSpec as P

MESH = pl.DeviceIdType.MESH
CHUNK = 128
WIDE = 512
GROUPED = 4
PAIRED = 2
PARAMS = pltpu.CompilerParams(vmem_limit_bytes=56 << 20)


def nn(a, b):
    return jnp.dot(a, b, preferred_element_type=jnp.float32)


def nt(a, b):
    return lax.dot_general(a, b, (((1,), (1,)), ((), ())), preferred_element_type=jnp.float32)


def tn(a, b):
    return lax.dot_general(a, b, (((0,), (0,)), ((), ())), preferred_element_type=jnp.float32)


def low(value):
    return value.astype(jnp.bfloat16)


def split(value):
    high = low(value)
    return high, low(value - high.astype(jnp.float32))


def fine(product, a, b):
    a_high, a_rest = a
    b_high, b_rest = b
    return product(a_high, b_high) + (product(a_high, b_rest) + product(a_rest, b_high))


def grid_masks():
    row = lax.broadcasted_iota(jnp.int32, (CHUNK, CHUNK), 0)
    column = lax.broadcasted_iota(jnp.int32, (CHUNK, CHUNK), 1)
    return row, column


def rows_of(index, sequence):
    first = pl.multiple_of(index * 256 + sequence * 64, 64)
    second = pl.multiple_of(index * 256 + 128 + sequence * 64, 64)
    return first, second


def load(ref, index, sequence, lanes=slice(None)):
    first, second = rows_of(index, sequence)
    return jnp.concatenate([ref[pl.ds(first, 64), lanes], ref[pl.ds(second, 64), lanes]], 0)


def store(ref, index, sequence, value, lanes=slice(None)):
    first, second = rows_of(index, sequence)
    ref[pl.ds(first, 64), lanes] = value[:64]
    ref[pl.ds(second, 64), lanes] = value[64:]


def columns_of(pos_ref, index, sequence):
    line = pos_ref[pl.ds(index * 2 + sequence, 1), :]
    return line, jnp.broadcast_to(line, (CHUNK, CHUNK)).T


def convolve(proj_ref, taps_ref, index, sequence, place):
    fields = slice(0, 384)
    current = load(proj_ref, index, sequence, fields)
    before = pl.multiple_of(jnp.maximum(index * 256 - 128 + sequence * 64 + 56, 0), 8)
    window = jnp.concatenate([proj_ref[pl.ds(before, 8), fields], current], 0)
    total = current * taps_ref[0:1, :]
    moved = [current]
    for offset in range(1, 4):
        keep = (place[:, 0:1] >= offset).astype(jnp.float32)
        shifted = window[8 - offset : 8 - offset + CHUNK] * keep
        moved.append(shifted)
        total = total + shifted * taps_ref[offset : offset + 1, :]
    return total, moved


def activate(total):
    sigma = jax.nn.sigmoid(total)
    act = total * sigma
    query, keys, values = act[:, :128], act[:, 128:256], act[:, 256:]
    query_scale = lax.rsqrt(jnp.sum(query * query, -1, keepdims=True) + 1e-06)
    key_scale = lax.rsqrt(jnp.sum(keys * keys, -1, keepdims=True) + 1e-06)
    return sigma, query * query_scale, query_scale, keys * key_scale, key_scale, values


def inverses(mixings, row, column):
    eye = (row == column).astype(jnp.float32)
    pair = (row // 2) == (column // 2)
    totals = [eye - jnp.where(pair, mixing, 0.0) for mixing in mixings]
    size = 2
    while size < CHUNK:
        corner = (
            ((row // (2 * size)) == (column // (2 * size)))
            & (((row // size) % 2) == 1)
            & (((column // size) % 2) == 0)
        )
        corners = [low(jnp.where(corner, mixing, 0.0)) for mixing in mixings]
        helds = [low(total) for total in totals]
        inners = [low(nn(held, part)) for held, part in zip(helds, corners)]
        totals = [total - nn(inner, held) for total, inner, held in zip(totals, inners, helds)]
        size *= 2
    helds = [split(total) for total in totals]
    rests = [
        low(eye - total - fine(nn, split(mixing), held))
        for total, mixing, held in zip(totals, mixings, helds)
    ]
    return [total + nn(held[0], rest) for total, held, rest in zip(totals, helds, rests)]


def mixer_forward(
    proj_ref, pos_ref, taps_ref, gain_ref,
    heads_ref, query_ref, key_ref, inv_ref, kc_ref, score_ref, step_ref, state_ref, update_ref, raw_ref,
    free_ref, shift_ref, after_prepare, after_advance,
):
    row, column = grid_masks()
    depth = row - column

    def prepare(double, carry):
        streams = [(double * GROUPED + item // 2, item % 2) for item in range(2 * GROUPED)]
        lines, queries, keys_all, values_all, betas, withins, carrieds, mixings = ([] for _ in range(8))
        for index, sequence in streams:
            line, place = columns_of(pos_ref, index, sequence)
            total, _ = convolve(proj_ref, taps_ref, index, sequence, place)
            _, query, _, keys, _, values = activate(total)
            lines.append(line[:, 127:128])
            queries.append(low(query * 128 ** (-0.5)))
            keys_all.append(keys)
            values_all.append(low(values))
            betas.append(jax.nn.sigmoid(load(proj_ref, index, sequence, slice(384, 512))))
            withins.append((depth >= 0) & (depth.astype(jnp.float32) <= place))
            carrieds.append(place > row.astype(jnp.float32))
        grams = [fine(nt, split(keys), split(keys * beta)) for keys, beta in zip(keys_all, betas)]
        mixings = [jnp.where(within & (depth > 0), gram, 0.0) for within, gram in zip(withins, grams)]
        solved_all = [low(solved) for solved in inverses(mixings, row, column)]
        boths = [
            nn(solved, jnp.concatenate([low(jnp.where(carried, keys, 0.0)), values], 1))
            for solved, carried, keys, values in zip(solved_all, carrieds, keys_all, values_all)
        ]
        key_lows = [low(keys) for keys in keys_all]
        scores = [nt(query, key_low) for query, key_low in zip(queries, key_lows)]
        weights = [
            jnp.where((127 - row).astype(jnp.float32) <= last, beta, 0.0)
            for last, beta in zip(lines, betas)
        ]
        ends_all = [
            tn(key_low, low(jnp.concatenate([weight, weight], 1) * both))
            for key_low, weight, both in zip(key_lows, weights, boths)
        ]
        for item, (index, sequence) in enumerate(streams):
            block = index * 2 + sequence
            through = jnp.where((row == column) & (lines[item] > 127.0), 1.0, 0.0)
            store(query_ref, index, sequence, queries[item])
            store(key_ref, index, sequence, key_lows[item])
            inv_ref[block] = solved_all[item]
            kc_ref[block] = low(boths[item][:, :128])
            free_ref[block] = boths[item][:, 128:]
            score_ref[block] = low(jnp.where(withins[item], scores[item], 0.0))
            step_ref[block] = low(through - ends_all[item][:, :128])
            shift_ref[block] = ends_all[item][:, 128:]
        return carry

    lax.fori_loop(0, 8 // GROUPED, prepare, 0)

    def advance(index, states):
        new = []
        for sequence in range(2):
            block = index * 2 + sequence
            state_low = low(states[sequence])
            state_ref[block] = state_low
            new.append(nn(step_ref[block], state_low) + shift_ref[block])
        return tuple(new)

    zero = jnp.zeros((CHUNK, CHUNK), jnp.float32)
    after_prepare()
    states = (zero, zero)
    for index in range(8):
        states = advance(index, states)
    after_advance()

    def finish(double, carry):
        streams = [(double * GROUPED + item // 2, item % 2) for item in range(2 * GROUPED)]
        blocks = [index * 2 + sequence for index, sequence in streams]
        states = [state_ref[block] for block in blocks]
        recalls = [nn(kc_ref[block], state) for block, state in zip(blocks, states)]
        reads = [nn(load(query_ref, *stream), state) for stream, state in zip(streams, states)]
        updates = [free_ref[block] - recall for block, recall in zip(blocks, recalls)]
        weighted = [
            low(jax.nn.sigmoid(load(proj_ref, *stream, slice(384, 512))) * update)
            for stream, update in zip(streams, updates)
        ]
        mixed = [nn(score_ref[block], weight) for block, weight in zip(blocks, weighted)]
        for item, (index, sequence) in enumerate(streams):
            _, place = columns_of(pos_ref, index, sequence)
            output = jnp.where(place > row.astype(jnp.float32), reads[item], 0.0) + mixed[item]
            scale = lax.rsqrt(jnp.mean(output * output, -1, keepdims=True) + 1e-05)
            update_ref[blocks[item]] = low(updates[item])
            raw_ref[blocks[item]] = output
            store(heads_ref, index, sequence, low(output * scale * gain_ref[0:1, :]))
        return carry

    lax.fori_loop(0, 8 // GROUPED, finish, 0)


def mixer_backward(
    grad_ref, proj_ref, pos_ref, taps_ref, gain_ref,
    query_ref, key_ref, inv_ref, kc_ref, score_ref, step_ref, state_ref, update_ref, raw_ref,
    out_ref, taps_grad_ref, gain_grad_ref,
    back_ref, pull_ref, flow_ref, enter_ref, pre_ref, after_prepare, after_collect,
):
    row, column = grid_masks()
    depth = row - column
    taps_grad_ref[...] = jnp.zeros_like(taps_grad_ref)
    gain_grad_ref[...] = jnp.zeros_like(gain_grad_ref)

    def prepare(double, carry):
        streams = [(double * GROUPED + item // 2, item % 2) for item in range(2 * GROUPED)]
        blocks = [index * 2 + sequence for index, sequence in streams]
        back_lows = []
        for (index, sequence), block in zip(streams, blocks):
            grad = load(grad_ref, index, sequence).astype(jnp.float32)
            output = raw_ref[block]
            scale = lax.rsqrt(jnp.mean(output * output, -1, keepdims=True) + 1e-05)
            unit = output * scale
            inner = grad * gain_ref[0:1, :]
            gain_grad_ref[0:1, :] += jnp.sum(grad * unit, 0, keepdims=True)
            back = scale * (inner - unit * jnp.mean(inner * unit, -1, keepdims=True))
            back_lows.append(low(back))
        pulls = [tn(score_ref[block], back_low) for block, back_low in zip(blocks, back_lows)]
        rights = []
        for (index, sequence), back_low, pull in zip(streams, back_lows, pulls):
            _, place = columns_of(pos_ref, index, sequence)
            carried = place > row.astype(jnp.float32)
            beta = jax.nn.sigmoid(load(proj_ref, index, sequence, slice(384, 512)))
            rights.append(
                jnp.concatenate([jnp.where(carried, back_low, 0.0), low(-beta * pull)], 0)
            )
        enters = [
            tn(jnp.concatenate([load(query_ref, *stream), kc_ref[block]], 0), right)
            for stream, block, right in zip(streams, blocks, rights)
        ]
        for block, back_low, pull, enter in zip(blocks, back_lows, pulls, enters):
            enter_ref[block] = enter
            back_ref[block] = back_low
            pull_ref[block] = pull
        return carry

    lax.fori_loop(0, 8 // GROUPED, prepare, 0)

    def retreat(step, flows):
        index = 7 - step
        new = []
        for sequence in range(2):
            block = index * 2 + sequence
            flow_low = low(flows[sequence])
            flow_ref[block] = flow_low
            new.append(tn(step_ref[block], flow_low) + enter_ref[block])
        return tuple(new)

    zero = jnp.zeros((CHUNK, CHUNK), jnp.float32)
    after_prepare()
    flows = (zero, zero)
    for step in range(8):
        flows = retreat(step, flows)

    def collect(double, carry):
        streams = [(double * PAIRED + item // 2, item % 2) for item in range(2 * PAIRED)]
        blocks = [index * 2 + sequence for index, sequence in streams]
        lines, places, betas, carrieds, closings = ([] for _ in range(5))
        for index, sequence in streams:
            line, place = columns_of(pos_ref, index, sequence)
            lines.append(line)
            places.append(place)
            betas.append(jax.nn.sigmoid(load(proj_ref, index, sequence, slice(384, 512))))
            carrieds.append(place > row.astype(jnp.float32))
            closings.append((127 - row).astype(jnp.float32) <= line[:, 127:128])
        queries = [load(query_ref, *stream) for stream in streams]
        keys_all = [load(key_ref, *stream) for stream in streams]
        updates = [update_ref[block].astype(jnp.float32) for block in blocks]
        weighted = [beta * update for beta, update in zip(betas, updates)]
        flows = [flow_ref[block] for block in blocks]
        states = [state_ref[block] for block in blocks]
        backs = [back_ref[block] for block in blocks]
        key_flows = [nn(keys, flow) for keys, flow in zip(keys_all, flows)]
        score_grads = [nt(back, low(weight)) for back, weight in zip(backs, weighted)]
        grams = [nt(keys, keys) for keys in keys_all]
        weight_grads = [
            pull_ref[block] + jnp.where(closing, key_flow, 0.0)
            for block, closing, key_flow in zip(blocks, closings, key_flows)
        ]
        right_grads = [
            tn(inv_ref[block], low(beta * weight_grad))
            for block, beta, weight_grad in zip(blocks, betas, weight_grads)
        ]
        score_lows = [
            low(jnp.where((depth >= 0) & (depth.astype(jnp.float32) <= place), score_grad, 0.0))
            for place, score_grad in zip(places, score_grads)
        ]
        query_grads = [
            nt(jnp.where(carried, back, 0.0), state) + nn(score_low, keys)
            for carried, back, state, score_low, keys in zip(
                carrieds, backs, states, score_lows, keys_all
            )
        ]
        mixing_grads = [
            jnp.where((depth < 0) & ((-depth).astype(jnp.float32) <= line), -nt(low(update), low(right_grad)), 0.0)
            for line, update, right_grad in zip(lines, updates, right_grads)
        ]
        gram_lows = [low(beta * mixing_grad) for beta, mixing_grad in zip(betas, mixing_grads)]
        key_grads = [
            nt(
                jnp.concatenate(
                    [low(jnp.where(closing, weight, 0.0)), low(jnp.where(carried, -right_grad, 0.0))], 1
                ),
                jnp.concatenate([flow, state], 1),
            )
            for closing, weight, carried, right_grad, flow, state in zip(
                closings, weighted, carrieds, right_grads, flows, states
            )
        ]
        key_grads = [
            key_grad
            + tn(jnp.concatenate([score_low, gram_low], 0), jnp.concatenate([query, keys], 0))
            + nn(gram_low, keys)
            for key_grad, score_low, gram_low, query, keys in zip(
                key_grads, score_lows, gram_lows, queries, keys_all
            )
        ]
        for item, (index, sequence) in enumerate(streams):
            total, moved = convolve(proj_ref, taps_ref, index, sequence, places[item])
            sigma, query, query_scale, keys, key_scale, _ = activate(total)
            beta = betas[item]
            beta_grad = jnp.sum(
                weight_grads[item] * updates[item] + mixing_grads[item] * grams[item], -1, keepdims=True
            )
            query_grad = query_grads[item] * 128 ** (-0.5)
            query_act = query_scale * (
                query_grad - query * jnp.sum(query * query_grad, -1, keepdims=True)
            )
            key_act = key_scale * (
                key_grads[item] - keys * jnp.sum(keys * key_grads[item], -1, keepdims=True)
            )
            act_grad = jnp.concatenate([query_act, key_act, right_grads[item]], 1)
            pre_grad = act_grad * (sigma * (1.0 + total * (1.0 - sigma)))
            for offset in range(4):
                taps_grad_ref[offset : offset + 1, :] += jnp.sum(
                    pre_grad * moved[offset], 0, keepdims=True
                )
            store(pre_ref, index, sequence, pre_grad)
            logit_grad = jnp.where(column == 0, beta_grad * beta * (1.0 - beta), 0.0)
            store(out_ref, index, sequence, low(logit_grad), slice(384, 512))
        return carry

    lax.fori_loop(0, 8 // PAIRED, collect, 0)
    after_collect()

    def spread(index, carry):
        for sequence in range(2):
            after = pl.multiple_of(jnp.minimum(index * 256 + 256, 1792) + sequence * 64, 64)
            live = jnp.where(index == 7, 0.0, 1.0)
            current = load(pre_ref, index, sequence)
            window = jnp.concatenate([current, pre_ref[pl.ds(after, 8), :] * live], 0)
            _, place = columns_of(pos_ref, index, sequence)
            _, follow = columns_of(pos_ref, jnp.minimum(index + 1, 7), sequence)
            places = jnp.concatenate([place, follow[0:8]], 0)[:, 0:1]
            total = current * taps_ref[0:1, :]
            for offset in range(1, 4):
                masked = window * (places >= offset).astype(jnp.float32)
                total = total + masked[offset : offset + CHUNK] * taps_ref[offset : offset + 1, :]
            store(out_ref, index, sequence, low(total), slice(0, 384))
        return carry

    lax.fori_loop(0, 8, spread, 0)


def saved_shapes():
    rows = jax.ShapeDtypeStruct((2048, CHUNK), jnp.bfloat16)
    small = jax.ShapeDtypeStruct((16, CHUNK, CHUNK), jnp.bfloat16)
    wide = jax.ShapeDtypeStruct((16, CHUNK, CHUNK), jnp.float32)
    return (rows, rows, small, small, small, small, small, small, wide)


def spot(y, z, core):
    return (y * 2 + z) * 2 + core


class Neighbours:
    def __init__(self):
        index = lax.axis_index("tensor")
        self.core = index % 2
        self.z = (index // 2) % 2
        self.y = index // 4
        up, down, far = (self.y + 1) % 4, (self.y + 3) % 4, (self.y + 2) % 4
        other = 1 - self.z
        self.up = spot(up, self.z, self.core)
        self.down = spot(down, self.z, self.core)
        self.side = spot(self.y, other, self.core)
        self.twin = spot(self.y, self.z, 1 - self.core)
        self.chips = {
            "own": self.y * 2 + self.z,
            "side": self.y * 2 + other,
            "down": down * 2 + self.z,
            "up": up * 2 + self.z,
            "downside": down * 2 + other,
            "upside": up * 2 + other,
            "far": far * 2 + self.z,
            "farside": far * 2 + other,
        }

    def mine(self, name):
        return self.chips[name] * 2 + self.core

    def twins(self, name):
        return self.chips[name] * 2 + 1 - self.core

    def chip_at(self, step):
        quarter = step // 2
        shift = quarter + quarter // 2 - 2 * (quarter // 3)
        return ((self.y + shift) % 4) * 2 + (self.z + step % 2) % 2


def greet(devices):
    barrier = pltpu.get_barrier_semaphore()
    for device in devices:
        pl.semaphore_signal(barrier, inc=1, device_id=device, device_id_type=MESH)
    pl.semaphore_wait(barrier, len(devices))


def remote(source, target, send_sem, recv_sem, device):
    return pltpu.make_async_remote_copy(
        src_ref=source, dst_ref=target, send_sem=send_sem, recv_sem=recv_sem,
        device_id=device, device_id_type=MESH,
    )


TOP, BOTTOM, WHOLE = pl.ds(0, 64), pl.ds(64, 64), pl.ds(0, 128)
NAMES = ("own", "side", "down", "up", "downside", "upside", "far", "farside")


class Gather:
    copies = 17

    def __init__(self, near, buffer, sends, receives):
        self.near, self.buffer, self.sends, self.receives = near, buffer, sends, receives

    def send(self, key, block, rows, device):
        piece = self.buffer.at[block, rows]
        copy = remote(piece, piece, self.sends.at[key], self.receives.at[key], {"tensor": device})
        copy.start()

    def arrive(self, key, block, rows=WHOLE):
        piece = self.buffer.at[block, rows]
        remote(
            piece, piece, self.sends.at[key], self.receives.at[key], {"tensor": self.near.twin}
        ).wait_recv()

    def to_twin(self, name):
        self.send(9 + NAMES.index(name), self.near.mine(name), WHOLE, self.near.twin)

    def from_twin(self, name):
        self.arrive(9 + NAMES.index(name), self.near.twins(name))

    def start(self):
        near = self.near
        own = near.mine("own")
        self.send(1, own, WHOLE, near.up)
        self.send(2, own, WHOLE, near.down)
        self.send(0, own, WHOLE, near.side)
        self.to_twin("own")

    def second(self):
        near = self.near
        self.arrive(1, near.mine("down"))
        self.send(5, near.mine("down"), TOP, near.up)
        self.arrive(2, near.mine("up"))
        self.send(6, near.mine("up"), BOTTOM, near.down)
        self.arrive(0, near.mine("side"))
        self.send(3, near.mine("side"), WHOLE, near.up)
        self.send(4, near.mine("side"), WHOLE, near.down)
        self.to_twin("side")
        self.to_twin("up")
        self.to_twin("down")

    def third(self):
        near = self.near
        far = near.mine("far")
        self.arrive(5, far, TOP)
        self.send(7, far, TOP, near.side)
        self.arrive(6, far, BOTTOM)
        self.send(8, far, BOTTOM, near.side)
        self.to_twin("far")

    def fourth(self):
        near = self.near
        self.arrive(4, near.mine("upside"))
        self.to_twin("upside")
        self.arrive(3, near.mine("downside"))
        self.to_twin("downside")

    def fifth(self):
        far = self.near.mine("farside")
        self.arrive(7, far, TOP)
        self.arrive(8, far, BOTTOM)
        self.to_twin("farside")

    def finish(self):
        near = self.near
        names = ("own", "own", "own", "side", "side", "down", "up", "far", "far") + NAMES
        for key, name in enumerate(names):
            rows = {5: TOP, 6: BOTTOM, 7: TOP, 8: BOTTOM}.get(key, WHOLE)
            piece = self.buffer.at[near.mine(name), rows]
            remote(
                piece, piece, self.sends.at[key], self.receives.at[key], {"tensor": near.twin}
            ).wait_send()

    def before(self, step):
        @pl.when(step == 0)
        def _():
            self.from_twin("own")

        @pl.when(step == 1)
        def _():
            self.second()
            self.from_twin("side")

        @pl.when(step == 2)
        def _():
            self.from_twin("up")

        @pl.when(step == 3)
        def _():
            self.third()
            self.fourth()
            self.from_twin("upside")

        @pl.when(step == 4)
        def _():
            self.from_twin("down")

        @pl.when(step == 5)
        def _():
            self.from_twin("downside")

        @pl.when(step == 6)
        def _():
            self.from_twin("far")

        @pl.when(step == 7)
        def _():
            self.fifth()
            self.from_twin("farside")


def add_rows(target, sources, count=128):
    def piece(index, carry):
        rows = pl.ds(pl.multiple_of(index * 16, 16), 16)
        total = target[rows].astype(jnp.float32)
        for source in sources:
            total = total + source[rows].astype(jnp.float32)
        target[rows] = total.astype(target.dtype)
        return carry

    lax.fori_loop(0, count // 16, piece, 0)


class Scatter:
    slots = 8
    copies = 16

    def __init__(self, near, part, twin_part, slot, sends, receives):
        self.near, self.part, self.twin_part, self.slot = near, part, twin_part, slot
        self.sends, self.receives = sends, receives

    def describe(self, key, source, target, device):
        return remote(source, target, self.sends.at[key], self.receives.at[key], {"tensor": device})

    def twin_copy(self, chip):
        return self.describe(
            8 + chip, self.part.at[chip * 2 + 1 - self.near.core], self.twin_part.at[chip], self.near.twin
        )

    def to_twin(self, chip):
        self.twin_copy(chip).start()

    def chip_sum(self, name):
        chip = self.near.chips[name]
        self.twin_copy(chip).wait_recv()
        add_rows(self.part.at[chip * 2 + self.near.core], [self.twin_part.at[chip]])

    def outgoing(self):
        near, part, slot = self.near, self.part, self.slot
        return (
            (0, part.at[near.mine("farside")], slot.at[0], near.side),
            (1, part.at[near.mine("far"), TOP], slot.at[1, TOP], near.down),
            (2, part.at[near.mine("far"), BOTTOM], slot.at[1, BOTTOM], near.up),
            (3, part.at[near.mine("downside")], slot.at[2], near.down),
            (4, part.at[near.mine("upside")], slot.at[3], near.up),
            (5, part.at[near.mine("down")], slot.at[4], near.down),
            (6, part.at[near.mine("up")], slot.at[5], near.up),
            (7, part.at[near.mine("side")], slot.at[6], near.side),
        )

    def send(self, key):
        self.describe(*self.outgoing()[key]).start()

    def arrive(self, key):
        self.describe(*self.outgoing()[key]).wait_recv()

    def first(self):
        self.chip_sum("farside")
        self.send(0)
        self.chip_sum("downside")
        self.send(3)
        self.chip_sum("upside")
        self.send(4)
        self.chip_sum("far")
        self.chip_sum("down")
        self.chip_sum("up")
        self.chip_sum("side")

    def second(self):
        near, part, slot = self.near, self.part, self.slot
        self.arrive(0)
        add_rows(part.at[near.mine("far")], [slot.at[0]])
        self.send(1)
        self.send(2)

    def third(self):
        near, part, slot = self.near, self.part, self.slot
        self.arrive(3)
        self.arrive(4)
        add_rows(part.at[near.mine("side")], [slot.at[2], slot.at[3]])
        self.send(7)
        self.arrive(1)
        add_rows(part.at[near.mine("down"), TOP], [slot.at[1, TOP]], 64)
        self.send(5)
        self.arrive(2)
        add_rows(part.at[near.mine("up"), BOTTOM], [slot.at[1, BOTTOM]], 64)
        self.send(6)

    def fourth(self):
        near = self.near
        chip = near.chips["own"]
        self.twin_copy(chip).wait_recv()
        for key in (7, 5, 6):
            self.arrive(key)
        return self.part.at[chip * 2 + near.core], self.twin_part.at[chip]

    def total(self, rows):
        near = self.near
        chip = near.chips["own"]
        value = self.part[chip * 2 + near.core, rows].astype(jnp.float32)
        value = value + self.twin_part[chip, rows].astype(jnp.float32)
        for key in (4, 5, 6):
            value = value + self.slot[key, rows].astype(jnp.float32)
        return value

    def finish(self):
        for chip in range(8):
            self.twin_copy(chip).wait_send()
        for copy in self.outgoing():
            self.describe(*copy).wait_send()


HIDDEN = 384


def sigmoid(value):
    return 1.0 / (1.0 + jnp.exp(-value))


def ffn_kernel(
    input_ref, hidden_ref, teacher_ref, mask_ref, gate_up_ref, down_shard_ref,
    block_ref, grad_ref, back_ref, square_ref, weight_ref, down_grad_ref,
    tokens, grads, both, act_t, both_t, part, twin_part, slot, down_ref, down_part, down_slot, down_staged,
    down_send, down_recv, leave_send, leave_recv, gather_send, gather_recv, scatter_send, scatter_recv,
    again_send, again_recv, return_send, return_recv,
):
    near = Neighbours()
    data = lax.axis_index("dp")
    neighbours = [{"tensor": device} for device in (near.up, near.down, near.side, near.twin)]
    neighbours = neighbours + [{"dp": device} for device in data_neighbours()]
    own = near.mine("own")
    tokens[own] = input_ref[...]
    down_ref[pl.ds(pl.multiple_of(data * 256, 256), 256)] = down_shard_ref[...]
    greet(neighbours)
    gather = Gather(near, tokens, gather_send, gather_recv)
    gather.start()
    down = DataGather(
        down_shard_ref, lambda block: down_ref.at[pl.ds(pl.multiple_of(block * 256, 256), 256)],
        down_send, down_recv,
    )
    down.start()
    down.relay()
    down.arrive()
    scatter = Scatter(near, part, twin_part, slot, scatter_send, scatter_recv)

    def rows_at(buffer, chip):
        return jnp.concatenate([buffer[chip * 2], buffer[chip * 2 + 1]], 0)

    def forward(step, carry):
        gather.before(step)
        chip = near.chip_at(step)
        rows = pl.ds(pl.multiple_of(chip * 256, 256), 256)
        product = nn(rows_at(tokens, chip), gate_up_ref[...])
        both[rows, :] = product
        gate, up = product[:, :HIDDEN], product[:, HIDDEN:]
        act = low(gate * sigmoid(gate) * up)
        act_t[:, rows] = act.T
        partial = low(nt(act, down_ref[...]))
        part[chip * 2] = partial[:128]
        part[chip * 2 + 1] = partial[128:]
        scatter.to_twin(chip)
        return carry

    lax.fori_loop(0, 8, forward, 0)
    scatter.first()
    scatter.second()
    scatter.third()
    scatter.fourth()

    def middle(index, squares):
        rows = pl.ds(pl.multiple_of(index * 16, 16), 16)
        output = hidden_ref[rows] + scatter.total(rows)
        block_ref[rows] = low(output)
        diff = output - teacher_ref[rows].astype(jnp.float32)
        weight = mask_ref[0, rows, 0:1]
        grad = mask_ref[1, rows, 0:1] * diff
        grad_ref[rows] = grad
        grads[own, rows] = low(grad)
        return squares + weight * jnp.sum(diff * diff, -1, keepdims=True)

    squares = lax.fori_loop(0, 8, middle, jnp.zeros((16, 1), jnp.float32))
    square_ref[...] = jnp.broadcast_to(jnp.sum(squares, 0, keepdims=True), (8, 128))
    gather.finish()
    down.finish()
    scatter.finish()

    again = Gather(near, grads, again_send, again_recv)
    again.start()
    back = Scatter(near, part, twin_part, slot, return_send, return_recv)

    def backward(step, carry):
        again.before(step)
        chip = near.chip_at(step)
        rows = pl.ds(pl.multiple_of(chip * 256, 256), 256)
        act_grad = nn(rows_at(grads, chip), down_ref[...])
        gate, up = both[rows, :HIDDEN], both[rows, HIDDEN:]
        sigma = sigmoid(gate)
        gate_low = low(act_grad * up * sigma * (1.0 + gate * (1.0 - sigma)))
        up_low = low(act_grad * gate * sigma)
        both_low = jnp.concatenate([gate_low, up_low], 1)
        both_t[:, rows] = both_low.T
        partial = low(nt(both_low, gate_up_ref[...]))
        part[chip * 2] = partial[:128]
        part[chip * 2 + 1] = partial[128:]
        back.to_twin(chip)
        return carry

    lax.fori_loop(0, 8, backward, 0)
    back.first()

    def lanes(block):
        return pl.ds(pl.multiple_of(block * 256, 256), 256)

    def down_weights(step, carry):
        column = grads[:, :, lanes(step)].reshape(2048, 256)
        down_part[:, lanes(step)] = low(nn(act_t[...], column))
        return carry

    lax.fori_loop(0, 8, down_weights, 0)
    place = DataPlace()
    leave = DataScatter(
        lambda block: down_part.at[:, lanes(block)],
        lambda other, rows: down_part[rows, lanes(place.block(0, other))],
        down_slot, down_staged, leave_send, leave_recv,
    )
    leave.start()
    back.second()

    def weights(step, carry):
        @pl.when(step == 4)
        def _():
            back.third()

        column = tokens[:, :, lanes(step)].reshape(2048, 256)
        weight_ref[:, lanes(step)] = low(nn(both_t[...], column))
        return carry

    lax.fori_loop(0, 8, weights, 0)
    leave.relay()
    back.fourth()

    def ending(index, carry):
        rows = pl.ds(pl.multiple_of(index * 16, 16), 16)
        back_ref[rows] = back.total(rows)
        return carry

    lax.fori_loop(0, 8, ending, 0)
    leave.result(down_grad_ref)
    leave.finish()
    again.finish()
    back.finish()


def data_neighbours():
    place = DataPlace()
    return [place.block(shift, 0) for shift in range(1, 4)] + [place.block(0, 1)]


def run_ffn(ffn_in, hidden, teacher, mask, gate_up, down_shard):
    rows, features = ffn_in.shape
    wide = jax.ShapeDtypeStruct((rows, features), jnp.float32)
    vmem = pl.BlockSpec(memory_space=pltpu.VMEM)
    semaphores = [pltpu.SemaphoreType.DMA((7,)) for _ in range(4)]
    for _ in range(2):
        for count in (Gather.copies, Gather.copies, Scatter.copies, Scatter.copies):
            semaphores.append(pltpu.SemaphoreType.DMA((count,)))
    return pl.pallas_call(
        ffn_kernel,
        out_shape=(
            jax.ShapeDtypeStruct((rows, features), jnp.bfloat16),
            wide,
            wide,
            jax.ShapeDtypeStruct((8, 128), jnp.float32),
            jax.ShapeDtypeStruct((2 * HIDDEN, features), jnp.bfloat16),
            jax.ShapeDtypeStruct((HIDDEN, 256), jnp.float32),
        ),
        in_specs=[vmem] * 6,
        out_specs=[vmem] * 6,
        scratch_shapes=[
            pltpu.VMEM((16, 128, 2048), jnp.bfloat16),
            pltpu.VMEM((16, 128, 2048), jnp.bfloat16),
            pltpu.VMEM((2048, 2 * HIDDEN), jnp.float32),
            pltpu.VMEM((HIDDEN, 2048), jnp.bfloat16),
            pltpu.VMEM((2 * HIDDEN, 2048), jnp.bfloat16),
            pltpu.VMEM((16, 128, 2048), jnp.bfloat16),
            pltpu.VMEM((8, 128, 2048), jnp.bfloat16),
            pltpu.VMEM((7, 128, 2048), jnp.bfloat16),
            pltpu.VMEM((2048, HIDDEN), jnp.bfloat16),
            pltpu.VMEM((HIDDEN, 2048), jnp.bfloat16),
            pltpu.VMEM((7, HIDDEN, 256), jnp.bfloat16),
            pltpu.VMEM((HIDDEN, 256), jnp.bfloat16),
        ]
        + semaphores,
        compiler_params=pltpu.CompilerParams(
            collective_id=1, has_side_effects=True, vmem_limit_bytes=63 << 20
        ),
        cost_estimate=pl.CostEstimate(flops=160 << 30, bytes_accessed=16 << 20, transcendentals=0),
        name="feed_forward",
    )(ffn_in, hidden, teacher, mask, gate_up, down_shard)


def everyone():
    tensor, data = lax.axis_index("tensor"), lax.axis_index("dp")
    devices = [{"tensor": (tensor + shift) % 16} for shift in range(1, 16)]
    return devices + [{"dp": (data + shift) % 8} for shift in range(1, 8)]


class Fan:
    def __init__(self, axis, count, source, target, sends, receives):
        self.axis, self.count, self.source, self.target = axis, count, source, target
        self.sends, self.receives = sends, receives
        self.index = lax.axis_index(axis)

    def copy(self, shift):
        peer = (self.index + shift) % self.count
        return remote(
            self.source(peer), self.target(self.index), self.sends.at[shift],
            self.receives.at[shift], {self.axis: peer},
        )

    def start(self):
        for shift in range(1, self.count):
            self.copy(shift).start()

    def arrive(self):
        for shift in range(1, self.count):
            piece = self.target((self.index + self.count - shift) % self.count)
            peer = (self.index + shift) % self.count
            remote(
                piece, piece, self.sends.at[shift], self.receives.at[shift], {self.axis: peer}
            ).wait_recv()

    def finish(self):
        for shift in range(1, self.count):
            self.copy(shift).wait_send()


class DataPlace:
    def __init__(self):
        index = lax.axis_index("dp")
        self.x, self.z = index % 4, index // 4

    def block(self, shift, other):
        return ((self.z + other) % 2) * 4 + (self.x + shift) % 4


class DataGather:
    copies = 7

    def __init__(self, source, target, sends, receives):
        self.place = DataPlace()
        self.source, self.target, self.sends, self.receives = source, target, sends, receives

    def describe(self, key):
        place = self.place
        if key == 0:
            return self.copy(key, self.source, place.block(0, 0), place.block(0, 1))
        if key < 4:
            return self.copy(key, self.source, place.block(0, 0), place.block(key, 0))
        partner = place.block(0, 1)
        return self.copy(key, self.target(partner), partner, place.block(key - 3, 0))

    def copy(self, key, source, block, peer):
        return remote(
            source, self.target(block), self.sends.at[key], self.receives.at[key], {"dp": peer}
        )

    def start(self):
        for key in range(4):
            self.describe(key).start()

    def wait(self, key, block):
        piece = self.target(block)
        self.copy(key, piece, block, self.place.block(0, 1)).wait_recv()

    def relay(self):
        self.wait(0, self.place.block(0, 1))
        for key in range(4, 7):
            self.describe(key).start()

    def arrive(self):
        for shift in range(1, 4):
            self.wait(shift, self.place.block(4 - shift, 0))
            self.wait(3 + shift, self.place.block(4 - shift, 1))

    def finish(self):
        for key in range(7):
            self.describe(key).wait_send()


class DataScatter:
    copies = 7

    def __init__(self, part, own, slot, staged, sends, receives):
        self.place = DataPlace()
        self.part, self.own, self.slot, self.staged = part, own, slot, staged
        self.sends, self.receives = sends, receives

    def describe(self, key):
        place = self.place
        if key == 6:
            source, peer = self.staged, place.block(0, 1)
        else:
            shift, other = key // 2 + 1, key % 2
            source, peer = self.part(place.block(shift, other)), place.block(shift, 0)
        return remote(
            source, self.slot.at[key], self.sends.at[key], self.receives.at[key], {"dp": peer}
        )

    def start(self):
        for key in range(6):
            self.describe(key).start()

    def summed(self, other, rows, extra):
        total = self.own(other, rows).astype(jnp.float32)
        for key in range(other, 6, 2):
            total = total + self.slot[key, rows].astype(jnp.float32)
        if extra:
            total = total + self.slot[6, rows].astype(jnp.float32)
        return total

    def relay(self):
        for key in (1, 3, 5):
            self.describe(key).wait_recv()

        def piece(index, carry):
            rows = pl.ds(pl.multiple_of(index * 16, 16), 16)
            self.staged[rows] = low(self.summed(1, rows, False))
            return carry

        lax.fori_loop(0, self.staged.shape[0] // 16, piece, 0)
        self.describe(6).start()

    def result(self, output):
        for key in (0, 2, 4, 6):
            self.describe(key).wait_recv()

        def piece(index, carry):
            rows = pl.ds(pl.multiple_of(index * 16, 16), 16)
            output[rows] = self.summed(0, rows, True)
            return carry

        lax.fori_loop(0, self.staged.shape[0] // 16, piece, 0)

    def finish(self):
        for key in range(7):
            self.describe(key).wait_send()


def tile_sum(first, second, axes, sems):
    tensor, data = lax.axis_index("tensor"), lax.axis_index("dp")
    one = Fan("tensor", 16, lambda peer: first.at[tensor], lambda index: first.at[index], sems[0], sems[1])
    two = Fan("dp", 8, lambda peer: second.at[data], lambda index: second.at[index], sems[2], sems[3])
    return one, two


def entry_kernel(
    normed_ref, mix_ref, small_ref, count_ref, pos_ref, gate_up_ref, out_ref,
    gathered_ref, mix_full_ref, taps_ref, gain_ref, total_ref, gate_up_full_ref, out_full_ref,
    proj_ref, spread_ref, heads_ref,
    query_ref, key_ref, inv_ref, kc_ref, score_ref, step_ref, state_ref, update_ref, raw_ref,
    tokens, small, counts, count_rows, free_ref, shift_ref,
    gather_send, gather_recv, mix_send, mix_recv, wide_send, wide_recv, small_send, small_recv,
    out_send, out_recv, all_send, all_recv, count_send, count_recv, row_send, row_recv,
    head_send, head_recv, local,
):
    near = Neighbours()
    tensor, data = lax.axis_index("tensor"), lax.axis_index("dp")
    own = near.mine("own")
    block_rows = pl.ds(pl.multiple_of(data * 256, 256), 256)

    def rows_of_data(ref):
        return lambda block: ref.at[pl.ds(pl.multiple_of(block * 256, 256), 256)]

    def lanes_of_data(block):
        return out_full_ref.at[tensor, :, pl.ds(pl.multiple_of(block * 256, 256), 256)]

    wide_own = pltpu.make_async_copy(gate_up_ref, gate_up_full_ref.at[block_rows], local.at[0])
    out_own = pltpu.make_async_copy(out_ref, lanes_of_data(data), local.at[1])
    wide_own.start()
    out_own.start()
    tokens[own] = normed_ref[...]
    mix_full_ref[block_rows] = mix_ref[...]
    small[data] = small_ref[...]
    counts[tensor] = count_ref[...]
    greet(everyone())
    gather = Gather(near, tokens, gather_send, gather_recv)
    mix = DataGather(mix_ref, rows_of_data(mix_full_ref), mix_send, mix_recv)
    wide = DataGather(gate_up_ref, rows_of_data(gate_up_full_ref), wide_send, wide_recv)
    tiny = Fan("dp", 8, lambda peer: small.at[data], lambda index: small.at[index], small_send, small_recv)
    outs = Fan("dp", 8, lambda peer: out_ref, lanes_of_data, out_send, out_recv)
    one, two = tile_sum(counts, count_rows, None, (count_send, count_recv, row_send, row_recv))
    tiny.start()
    gather.start()
    mix.start()
    one.start()
    outs.start()
    wide.start()
    one.arrive()
    count_rows[data] = jnp.sum(counts[...], 0)
    two.start()
    mix.relay()
    mix.arrive()

    def project(step, carry):
        gather.before(step)
        chip = near.chip_at(step)
        rows = pl.ds(pl.multiple_of(chip * 256, 256), 256)
        values = jnp.concatenate([tokens[chip * 2], tokens[chip * 2 + 1]], 0)
        proj_ref[rows, :] = nn(values, mix_full_ref[...])
        return carry

    lax.fori_loop(0, 8, project, 0)
    keep = pltpu.make_async_copy(tokens, gathered_ref, local.at[2])
    keep.start()
    wide.relay()
    out_own.wait()
    outs.arrive()
    out_gather = Gather(near, out_full_ref, all_send, all_recv)
    out_gather.start()
    tiny.arrive()
    two.arrive()
    total_ref[...] = jnp.sum(count_rows[...], 0)
    table = jnp.sum(small[...].astype(jnp.float32), 0)
    for tap in range(4):
        for field in range(3):
            taps_ref[tap : tap + 1, field * 128 : field * 128 + 128] = table[tap * 3 + field : tap * 3 + field + 1]
    gain_ref[0:1, :] = table[12:13]
    mixer_forward(
        proj_ref, pos_ref, taps_ref, gain_ref,
        heads_ref, query_ref, key_ref, inv_ref, kc_ref, score_ref, step_ref, state_ref, update_ref, raw_ref,
        free_ref, shift_ref, out_gather.second, out_gather.third,
    )

    def head_rows(block):
        return heads_ref.at[pl.ds(pl.multiple_of(block * 128, 128), 128)]

    exchange = Fan("tensor", 16, head_rows, lambda index: spread_ref.at[index], head_send, head_recv)
    exchange.start()
    spread_ref[tensor] = heads_ref[pl.ds(pl.multiple_of(tensor * 128, 128), 128)]
    out_gather.fourth()
    out_gather.fifth()
    exchange.arrive()
    for name in NAMES:
        out_gather.from_twin(name)
    wide.arrive()
    wide_own.wait()
    keep.wait()
    for part in (gather, mix, wide, tiny, outs, one, two, out_gather, exchange):
        part.finish()


def dma(*counts):
    return [pltpu.SemaphoreType.DMA((count,)) for count in counts]


def run_entry(normed, mix_shard, small, count, pos, gate_up, out_weight):
    vmem, hbm = pl.BlockSpec(memory_space=pltpu.VMEM), pl.BlockSpec(memory_space=pl.ANY)
    half, full = jnp.bfloat16, jnp.float32
    shape = jax.ShapeDtypeStruct
    return pl.pallas_call(
        entry_kernel,
        out_shape=(
            shape((16, 128, 2048), half),
            shape((2048, WIDE), half),
            shape((8, 384), full),
            shape((8, CHUNK), full),
            shape((8, 128), full),
            shape((2048, 2 * HIDDEN), half),
            shape((16, 128, 2048), half),
            shape((2048, WIDE), full),
            shape((16, 128, CHUNK), half),
            shape((2048, CHUNK), half),
        )
        + saved_shapes(),
        in_specs=[vmem] * 5 + [hbm] * 2,
        out_specs=[hbm, vmem, vmem, vmem, vmem, hbm, hbm] + [vmem] * 12,
        scratch_shapes=[
            pltpu.VMEM((16, 128, 2048), half),
            pltpu.VMEM((8, 16, 128), half),
            pltpu.VMEM((16, 8, 128), full),
            pltpu.VMEM((8, 8, 128), full),
            pltpu.VMEM((16, CHUNK, CHUNK), full),
            pltpu.VMEM((16, CHUNK, CHUNK), full),
        ]
        + dma(17, 17, 7, 7, 7, 7, 8, 8, 8, 8, 17, 17, 16, 16, 8, 8, 16, 16, 3),
        compiler_params=pltpu.CompilerParams(
            collective_id=2, has_side_effects=True, vmem_limit_bytes=62 << 20
        ),
        cost_estimate=pl.CostEstimate(flops=60 << 30, bytes_accessed=16 << 20, transcendentals=0),
        name="entry",
    )(normed, mix_shard, small, count, pos, gate_up, out_weight)


SMALL = 16


def exit_kernel(
    heads_grad_ref, attention_ref, ffn_part_ref, gathered_ref, proj_ref, pos_ref, taps_ref, gain_ref,
    mix_ref, heads_ref, unit_ref, sums_ref,
    query_ref, key_ref, inv_ref, kc_ref, score_ref, step_ref, state_ref, update_ref, raw_ref,
    attn_ref, ffn_ref, weight_ref, total_ref,
    grad, attention, proj_low, taps_grad, gain_grad,
    back_ref, pull_ref, flow_ref, enter_ref, pre_ref,
    part, twin_part, slot, ffn_own, ffn_slot, ffn_staged, parts, part_slot, part_staged, proj_t, tile,
    sums, sum_rows,
    head_send, head_recv, gather_send, gather_recv, ffn_send, ffn_recv, mix_send, mix_recv,
    scatter_send, scatter_recv, sum_send, sum_recv, row_send, row_recv, local,
):
    near = Neighbours()
    tensor, data = lax.axis_index("tensor"), lax.axis_index("dp")
    own = near.mine("own")
    place = DataPlace()

    def lanes(block):
        return pl.ds(pl.multiple_of(block * 256, 256), 256)

    loads = [
        pltpu.make_async_copy(ffn_part_ref.at[:, lanes(place.block(0, other))], ffn_own.at[other], local.at[other])
        for other in range(2)
    ]
    for copy in loads:
        copy.start()
    attention[own] = attention_ref[...]
    greet(everyone())

    def head_rows(block):
        return grad.at[pl.ds(pl.multiple_of(block * 128, 128), 128)]

    exchange = Fan("tensor", 16, lambda peer: heads_grad_ref.at[peer], head_rows, head_send, head_recv)
    exchange.start()
    gather = Gather(near, attention, gather_send, gather_recv)
    gather.start()
    ffn = DataScatter(
        lambda block: ffn_part_ref.at[:, lanes(block)], lambda other, rows: ffn_own[other, rows],
        ffn_slot, ffn_staged, ffn_send, ffn_recv,
    )
    ffn.start()
    grad[pl.ds(pl.multiple_of(tensor * 128, 128), 128)] = heads_grad_ref[tensor]
    exchange.arrive()
    mixer_backward(
        grad, proj_ref, pos_ref, taps_ref, gain_ref,
        query_ref, key_ref, inv_ref, kc_ref, score_ref, step_ref, state_ref, update_ref, raw_ref,
        proj_low, taps_grad, gain_grad,
        back_ref, pull_ref, flow_ref, enter_ref, pre_ref, gather.second, gather.third,
    )
    gather.fourth()
    units = pltpu.make_async_copy(unit_ref, enter_ref, local.at[4])
    units.start()
    scatter = Scatter(near, part, twin_part, slot, scatter_send, scatter_recv)

    def backward(step, carry):
        chip = near.chip_at(step)
        rows = pl.ds(pl.multiple_of(chip * 256, 256), 256)
        values = proj_low[rows, :]
        keep = lax.broadcasted_iota(jnp.int32, (256, WIDE), 1) <= 384
        partial = low(nt(jnp.where(keep, values, jnp.zeros_like(values)), mix_ref[...]))
        proj_t[:, rows] = values.T[:400]
        part[chip * 2] = partial[:128]
        part[chip * 2 + 1] = partial[128:]
        scatter.to_twin(chip)
        return carry

    lax.fori_loop(0, 8, backward, 0)
    gather.fifth()
    for name in NAMES:
        gather.from_twin(name)
    scatter.first()

    def fetch(step):
        return pltpu.make_async_copy(gathered_ref.at[:, :, lanes(step)], tile.at[step % 2], local.at[2 + step % 2])

    fetch(0).start()
    table = jnp.concatenate([taps_grad[...], gain_grad[...]], 1)

    def weights(step, carry):
        @pl.when(step < 7)
        def _():
            fetch(step + 1).start()

        @pl.when(step == 3)
        def _():
            scatter.second()

        fetch(step).wait()
        column = tile[step % 2].reshape(2048, 256)
        product = nn(proj_t[...], column)
        parts[0:400, lanes(step)] = low(product)
        parts[400:528, lanes(step)] = low(tn(heads_ref[...], attention[:, :, lanes(step)].reshape(2048, 256)))
        return carry

    lax.fori_loop(0, 8, weights, 0)
    pick_row = lax.broadcasted_iota(jnp.int32, (CHUNK, 2048), 0)
    pick_lane = lax.broadcasted_iota(jnp.int32, (CHUNK, 2048), 1)
    wanted = (pick_lane // 256) * 16 + pick_lane % 256
    select = ((pick_row == wanted) & (pick_lane % 256 < 16)).astype(jnp.bfloat16)
    for tap in range(4):
        for field in range(3):
            row = tap * 3 + field
            pull_ref[0, row : row + 1, :] = taps_grad[tap : tap + 1, field * 128 : field * 128 + 128]
    pull_ref[0, 12:13, :] = gain_grad[0:1, :]
    small = nn(low(pull_ref[0, 0:16, :]), select)
    small_row = lax.broadcasted_iota(jnp.int32, (16, 2048), 0)
    moved = jnp.concatenate([small[15:16], small[0:15]], 0)
    beta_row = parts[384:400, :].astype(jnp.float32)
    parts[384:400, :] = low(jnp.where(small_row == 0, beta_row, moved))
    mix = DataScatter(
        lambda block: parts.at[:, lanes(block)],
        lambda other, rows: parts[rows, lanes(place.block(0, other))],
        part_slot, part_staged, mix_send, mix_recv,
    )
    mix.start()
    scatter.third()
    for copy in loads:
        copy.wait()
    ffn.relay()
    scatter.fourth()
    units.wait()

    def ending(index, total):
        rows = pl.ds(pl.multiple_of(index * 16, 16), 16)
        value = scatter.total(rows)
        attn_ref[rows] = value
        unit = jnp.concatenate([enter_ref[piece, rows] for piece in range(16)], 1)
        return total + value * unit

    total = lax.fori_loop(0, 8, ending, jnp.zeros((16, 2048), jnp.float32))
    total = jnp.sum(total, 0, keepdims=True)
    sums[tensor, 8:24] = sums_ref[8:24]
    for piece in range(8):
        sums[tensor, piece : piece + 1] = total[:, piece * 256 : piece * 256 + 256]
    one, two = tile_sum(sums, sum_rows, None, (sum_send, sum_recv, row_send, row_recv))
    one.start()
    mix.relay()
    one.arrive()
    sum_rows[data] = jnp.sum(sums[...], 0)
    two.start()
    ffn.result(ffn_ref)
    two.arrive()
    total_ref[...] = jnp.sum(sum_rows[...], 0)
    mix.result(weight_ref)
    for item in (exchange, gather, ffn, scatter, mix, one, two):
        item.finish()


def run_exit(heads_grad, attention, ffn_part, gathered, proj, pos, taps, gain, mix, heads, unit, sums, saved):
    vmem, hbm = pl.BlockSpec(memory_space=pltpu.VMEM), pl.BlockSpec(memory_space=pl.ANY)
    half, full = jnp.bfloat16, jnp.float32
    shape = jax.ShapeDtypeStruct
    return pl.pallas_call(
        exit_kernel,
        out_shape=(
            shape((128, 2048), full),
            shape((2 * HIDDEN, 256), full),
            shape((528, 256), full),
            shape((24, 256), full),
        ),
        in_specs=[vmem] * 2 + [hbm] * 2 + [vmem] * 6 + [hbm] + [vmem] * 10,
        out_specs=[vmem] * 4,
        scratch_shapes=[
            pltpu.VMEM((2048, CHUNK), half),
            pltpu.VMEM((16, 128, 2048), half),
            pltpu.VMEM((2048, WIDE), half),
            pltpu.VMEM((8, 384), full),
            pltpu.VMEM((8, CHUNK), full),
            pltpu.VMEM((16, CHUNK, CHUNK), half),
            pltpu.VMEM((16, CHUNK, CHUNK), full),
            pltpu.VMEM((16, CHUNK, CHUNK), half),
            pltpu.VMEM((16, CHUNK, CHUNK), full),
            pltpu.VMEM((2048, 384), full),
            pltpu.VMEM((16, 128, 2048), half),
            pltpu.VMEM((8, 128, 2048), half),
            pltpu.VMEM((7, 128, 2048), half),
            pltpu.VMEM((2, 2 * HIDDEN, 256), half),
            pltpu.VMEM((7, 2 * HIDDEN, 256), half),
            pltpu.VMEM((2 * HIDDEN, 256), half),
            pltpu.VMEM((528, 2048), half),
            pltpu.VMEM((7, 528, 256), half),
            pltpu.VMEM((528, 256), half),
            pltpu.VMEM((400, 2048), half),
            pltpu.VMEM((2, 16, 128, 256), half),
            pltpu.VMEM((16, 24, 256), full),
            pltpu.VMEM((8, 24, 256), full),
        ]
        + dma(16, 16, 17, 17, 7, 7, 7, 7, 16, 16, 16, 16, 8, 8, 5),
        compiler_params=pltpu.CompilerParams(
            collective_id=3, has_side_effects=True, vmem_limit_bytes=63 << 20
        ),
        cost_estimate=pl.CostEstimate(flops=60 << 30, bytes_accessed=16 << 20, transcendentals=0),
        name="exit",
    )(heads_grad, attention, ffn_part, gathered, proj, pos, taps, gain, mix, heads, unit, sums, *saved)


def token_places(segment):
    length = segment.shape[1]
    before = jnp.sum((segment[:, None, :] < segment[:, :, None]).astype(jnp.int32), -1)
    place = jnp.arange(length, dtype=jnp.int32)[None, :] - before
    return jnp.transpose(place.reshape(2, 8, CHUNK), (1, 0, 2)).reshape(16, CHUNK).astype(jnp.float32)


def pad_lanes(array, width):
    return jnp.pad(array, ((0, 0), (0, width - array.shape[1])))


def f32(value):
    return value.astype(jnp.float32)


def body(
    inputs, teacher, segment_ids, padding, attn_gain, qkv_weight, beta_weight, conv_taps, head_gain,
    out_weight, mlp_gain, gate_weight, up_weight, down_weight,
):
    hidden_units = gate_weight.shape[1]
    rows = 128
    features = inputs.shape[2]

    small = jnp.concatenate([conv_taps.reshape(12, 16), head_gain.reshape(1, 16)], 0)
    lane = jnp.arange(CHUNK)[None, :] // 16 == lax.axis_index("dp")
    small = jnp.where(lane, jnp.tile(jnp.pad(small, ((0, 3), (0, 0))), (1, 8)), 0)
    mix_shard = jnp.concatenate(
        [qkv_weight.reshape(256, 384), jnp.broadcast_to(beta_weight, (256, CHUNK))], 1
    )
    gate_up_shard = jnp.concatenate([pad_lanes(gate_weight, HIDDEN), pad_lanes(up_weight, HIDDEN)], 1)
    down_shard = pad_lanes(jnp.transpose(down_weight), HIDDEN)
    count = jnp.broadcast_to(f32(jnp.sum(padding)), (8, 128))

    tokens = f32(inputs.reshape(rows, features))
    attn_scale = lax.rsqrt(jnp.mean(tokens * tokens, -1, keepdims=True) + 1e-06)
    attn_unit = tokens * attn_scale
    normed = (attn_unit * attn_gain).astype(jnp.bfloat16)
    pos = token_places(segment_ids)
    (
        gathered, mix_full, taps, gain, total, gate_up, out_full, proj, spread, heads, *saved
    ) = run_entry(normed, mix_shard, small, count, pos, gate_up_shard, out_weight)
    out_full = out_full.reshape(features, features)
    valid = total[0, 0]
    scale = 16 * 1024 / valid
    heads_rows = jnp.transpose(spread, (1, 0, 2)).reshape(rows, features)
    hidden = tokens + nn(heads_rows, out_full)

    mlp_scale = lax.rsqrt(jnp.mean(hidden * hidden, -1, keepdims=True) + 1e-06)
    mlp_unit = hidden * mlp_scale
    ffn_in = (mlp_unit * mlp_gain).astype(jnp.bfloat16)
    mask = f32(padding.reshape(rows, 1))
    masks = jnp.broadcast_to(jnp.stack([mask, scale * mask]), (2, rows, CHUNK))
    output, block_grad, mlp_grad, square_tile, ffn_part, down_grad = run_ffn(
        ffn_in, hidden, teacher.reshape(rows, features), masks, gate_up, down_shard
    )

    mlp_sum = jnp.sum(mlp_grad * mlp_unit, 0)
    mlp_inner = mlp_grad * mlp_gain
    hidden_grad = block_grad + mlp_scale * (
        mlp_inner - mlp_unit * jnp.mean(mlp_inner * mlp_unit, -1, keepdims=True)
    )
    attention_low = hidden_grad.astype(jnp.bfloat16)
    heads_grad_rows = nt(attention_low, out_full).astype(jnp.bfloat16)
    heads_grad = jnp.transpose(heads_grad_rows.reshape(rows, 16, CHUNK), (1, 0, 2))
    sums = jnp.concatenate(
        [jnp.zeros((8, 256)), mlp_sum.reshape(8, 256), jnp.broadcast_to(square_tile[0:1, 0:1], (8, 256))], 0
    )
    units = jnp.transpose(attn_unit.reshape(rows, 16, CHUNK), (1, 0, 2))
    attn_grad, ffn_grads, mix_grads, totals = run_exit(
        heads_grad, attention_low, ffn_part, gathered, proj, pos, taps, gain, mix_full, heads, units, sums, saved
    )
    attn_inner = attn_grad * attn_gain
    input_grad = hidden_grad + attn_scale * (
        attn_inner - attn_unit * jnp.mean(attn_inner * attn_unit, -1, keepdims=True)
    )
    loss = totals[16, 0] / (valid * features)
    small_grad = mix_grads[385:398, :16]
    shape = (2, 64, features)
    return (
        output.reshape(shape),
        loss,
        input_grad.reshape(shape),
        totals[:8].reshape(features),
        jnp.transpose(mix_grads[:384]).reshape(256, 3, CHUNK),
        jnp.transpose(mix_grads[384:385]),
        small_grad[:12].reshape(4, 3, 1, 16),
        small_grad[12:].reshape(1, 16),
        mix_grads[400:],
        totals[8:16].reshape(features),
        jnp.transpose(ffn_grads[:hidden_units]),
        jnp.transpose(ffn_grads[HIDDEN : HIDDEN + hidden_units]),
        down_grad[:hidden_units],
    )


def solution(mesh):
    in_specs = (
        P("dp", "tensor", None),
        P("dp", "tensor", None),
        P("dp", None),
        P("dp", "tensor"),
        P(),
        P("dp", None, "tensor"),
        P("dp", "tensor"),
        P(None, None, "tensor", "dp"),
        P("tensor", "dp"),
        P("tensor", "dp"),
        P(),
        P("dp", "tensor"),
        P("dp", "tensor"),
        P("tensor", "dp"),
    )
    out_specs = (
        P("dp", "tensor", None),
        P(),
        P("dp", "tensor", None),
        P(),
        P("dp", None, "tensor"),
        P("dp", "tensor"),
        P(None, None, "tensor", "dp"),
        P("tensor", "dp"),
        P("tensor", "dp"),
        P(),
        P("dp", "tensor"),
        P("dp", "tensor"),
        P("tensor", "dp"),
    )
    return jax.shard_map(body, mesh=mesh, in_specs=in_specs, out_specs=out_specs, check_vma=False)
```

```python
import jax
import jax.numpy as jnp
from jax import lax
from jax.experimental import pallas as pl
from jax.experimental.pallas import tpu as pltpu
from jax.sharding import PartitionSpec as P

MESH = pl.DeviceIdType.MESH
CHUNK = 128
WIDE = 512
PARAMS = pltpu.CompilerParams(vmem_limit_bytes=56 << 20)


def nn(a, b):
    return jnp.dot(a, b, preferred_element_type=jnp.float32)


def nt(a, b):
    return lax.dot_general(a, b, (((1,), (1,)), ((), ())), preferred_element_type=jnp.float32)


def tn(a, b):
    return lax.dot_general(a, b, (((0,), (0,)), ((), ())), preferred_element_type=jnp.float32)


def low(value):
    return value.astype(jnp.bfloat16)


def split(value):
    high = low(value)
    return high, low(value - high.astype(jnp.float32))


def fine(product, a, b):
    a_high, a_rest = a
    b_high, b_rest = b
    return product(a_high, b_high) + (product(a_high, b_rest) + product(a_rest, b_high))


def grid_masks():
    row = lax.broadcasted_iota(jnp.int32, (CHUNK, CHUNK), 0)
    column = lax.broadcasted_iota(jnp.int32, (CHUNK, CHUNK), 1)
    return row, column


def chunk_rows(index, sequence):
    first = pl.multiple_of(index * 256 + sequence * 64, 64)
    second = pl.multiple_of(index * 256 + 128 + sequence * 64, 64)
    return first, second


def load(ref, index, sequence, lanes=slice(None)):
    first, second = chunk_rows(index, sequence)
    return jnp.concatenate([ref[pl.ds(first, 64), lanes], ref[pl.ds(second, 64), lanes]], 0)


def store(ref, index, sequence, value, lanes=slice(None)):
    first, second = chunk_rows(index, sequence)
    ref[pl.ds(first, 64), lanes] = value[:64]
    ref[pl.ds(second, 64), lanes] = value[64:]


def columns_of(pos_ref, index, sequence):
    line = pos_ref[pl.ds(index * 2 + sequence, 1), :]
    return line, jnp.broadcast_to(line, (CHUNK, CHUNK)).T


def convolve(proj_ref, taps_ref, index, sequence, place):
    fields = slice(0, 384)
    current = load(proj_ref, index, sequence, fields)
    before = pl.multiple_of(jnp.maximum(index * 256 - 128 + sequence * 64 + 56, 0), 8)
    window = jnp.concatenate([proj_ref[pl.ds(before, 8), fields], current], 0)
    total = current * taps_ref[0:1, :]
    moved = [current]
    for offset in range(1, 4):
        keep = (place[:, 0:1] >= offset).astype(jnp.float32)
        shifted = window[8 - offset : 8 - offset + CHUNK] * keep
        moved.append(shifted)
        total = total + shifted * taps_ref[offset : offset + 1, :]
    return total, moved


def activate(total):
    sigma = jax.nn.sigmoid(total)
    act = total * sigma
    query, keys, values = act[:, :128], act[:, 128:256], act[:, 256:]
    query_scale = lax.rsqrt(jnp.sum(query * query, -1, keepdims=True) + 1e-06)
    key_scale = lax.rsqrt(jnp.sum(keys * keys, -1, keepdims=True) + 1e-06)
    return sigma, query * query_scale, query_scale, keys * key_scale, key_scale, values


def inverses(mixings, row, column):
    eye = (row == column).astype(jnp.float32)
    pair = (row // 2) == (column // 2)
    totals = [eye - jnp.where(pair, mixing, 0.0) for mixing in mixings]
    size = 2
    while size < CHUNK:
        corner = (
            ((row // (2 * size)) == (column // (2 * size)))
            & (((row // size) % 2) == 1)
            & (((column // size) % 2) == 0)
        )
        corners = [low(jnp.where(corner, mixing, 0.0)) for mixing in mixings]
        helds = [low(total) for total in totals]
        inners = [low(nn(held, part)) for held, part in zip(helds, corners)]
        totals = [total - nn(inner, held) for total, inner, held in zip(totals, inners, helds)]
        size *= 2
    helds = [split(total) for total in totals]
    rests = [
        low(eye - total - fine(nn, split(mixing), held))
        for total, mixing, held in zip(totals, mixings, helds)
    ]
    return [total + nn(held[0], rest) for total, held, rest in zip(totals, helds, rests)]


def mixer_forward(
    proj_ref, pos_ref, taps_ref, gain_ref,
    heads_ref, query_ref, key_ref, inv_ref, kc_ref, score_ref, step_ref, state_ref, update_ref, raw_ref,
    free_ref, shift_ref, which, between,
):
    row, column = grid_masks()
    depth = row - column

    streams = [(index, which) for index in range(8)]

    def prepare():
        lines, queries, keys_all, values_all, betas, withins, carrieds, mixings = ([] for _ in range(8))
        for index, sequence in streams:
            line, place = columns_of(pos_ref, index, sequence)
            total, _ = convolve(proj_ref, taps_ref, index, sequence, place)
            _, query, _, keys, _, values = activate(total)
            lines.append(line[:, 127:128])
            queries.append(low(query * 128 ** (-0.5)))
            keys_all.append(keys)
            values_all.append(low(values))
            betas.append(jax.nn.sigmoid(load(proj_ref, index, sequence, slice(384, 512))))
            withins.append((depth >= 0) & (depth.astype(jnp.float32) <= place))
            carrieds.append(place > row.astype(jnp.float32))
        grams = [fine(nt, split(keys), split(keys * beta)) for keys, beta in zip(keys_all, betas)]
        mixings = [jnp.where(within & (depth > 0), gram, 0.0) for within, gram in zip(withins, grams)]
        solved_all = [low(solved) for solved in inverses(mixings, row, column)]
        boths = [
            nn(solved, jnp.concatenate([low(jnp.where(carried, keys, 0.0)), values], 1))
            for solved, carried, keys, values in zip(solved_all, carrieds, keys_all, values_all)
        ]
        key_lows = [low(keys) for keys in keys_all]
        scores = [nt(query, key_low) for query, key_low in zip(queries, key_lows)]
        weights = [
            jnp.where((127 - row).astype(jnp.float32) <= last, beta, 0.0)
            for last, beta in zip(lines, betas)
        ]
        ends_all = [
            tn(key_low, low(jnp.concatenate([weight, weight], 1) * both))
            for key_low, weight, both in zip(key_lows, weights, boths)
        ]
        for item, (index, sequence) in enumerate(streams):
            block = index * 2 + sequence
            through = jnp.where((row == column) & (lines[item] > 127.0), 1.0, 0.0)
            store(query_ref, index, sequence, queries[item])
            store(key_ref, index, sequence, key_lows[item])
            inv_ref[block] = solved_all[item]
            kc_ref[block] = low(boths[item][:, :128])
            free_ref[block] = boths[item][:, 128:]
            score_ref[block] = low(jnp.where(withins[item], scores[item], 0.0))
            step_ref[block] = low(through - ends_all[item][:, :128])
            shift_ref[block] = ends_all[item][:, 128:]

    prepare()
    between()
    state = jnp.zeros((CHUNK, CHUNK), jnp.float32)
    for index in range(8):
        block = index * 2 + which
        state_low = low(state)
        state_ref[block] = state_low
        state = nn(step_ref[block], state_low) + shift_ref[block]

    def finish():
        blocks = [index * 2 + sequence for index, sequence in streams]
        states = [state_ref[block] for block in blocks]
        recalls = [nn(kc_ref[block], state) for block, state in zip(blocks, states)]
        reads = [nn(load(query_ref, *stream), state) for stream, state in zip(streams, states)]
        updates = [free_ref[block] - recall for block, recall in zip(blocks, recalls)]
        weighted = [
            low(jax.nn.sigmoid(load(proj_ref, *stream, slice(384, 512))) * update)
            for stream, update in zip(streams, updates)
        ]
        mixed = [nn(score_ref[block], weight) for block, weight in zip(blocks, weighted)]
        for item, (index, sequence) in enumerate(streams):
            _, place = columns_of(pos_ref, index, sequence)
            output = jnp.where(place > row.astype(jnp.float32), reads[item], 0.0) + mixed[item]
            scale = lax.rsqrt(jnp.mean(output * output, -1, keepdims=True) + 1e-05)
            update_ref[blocks[item]] = low(updates[item])
            raw_ref[blocks[item]] = output
            store(heads_ref, index, sequence, low(output * scale * gain_ref[0:1, :]))

    finish()


def mixer_backward(
    grad_ref, proj_ref, pos_ref, taps_ref, gain_ref,
    query_ref, key_ref, inv_ref, kc_ref, score_ref, step_ref, state_ref, update_ref, raw_ref,
    out_ref, taps_grad_ref, gain_grad_ref,
    back_ref, pull_ref, flow_ref, enter_ref, pre_ref, which, between, after,
):
    row, column = grid_masks()
    depth = row - column

    def prepare():
        streams = [(index, which) for index in range(8)]
        blocks = [index * 2 + sequence for index, sequence in streams]
        back_lows = []
        for (index, sequence), block in zip(streams, blocks):
            grad = load(grad_ref, index, sequence).astype(jnp.float32)
            output = raw_ref[block]
            scale = lax.rsqrt(jnp.mean(output * output, -1, keepdims=True) + 1e-05)
            unit = output * scale
            inner = grad * gain_ref[0:1, :]
            gain_grad_ref[0:1, :] += jnp.sum(grad * unit, 0, keepdims=True)
            back = scale * (inner - unit * jnp.mean(inner * unit, -1, keepdims=True))
            back_lows.append(low(back))
        pulls = [tn(score_ref[block], back_low) for block, back_low in zip(blocks, back_lows)]
        rights = []
        for (index, sequence), back_low, pull in zip(streams, back_lows, pulls):
            _, place = columns_of(pos_ref, index, sequence)
            carried = place > row.astype(jnp.float32)
            beta = jax.nn.sigmoid(load(proj_ref, index, sequence, slice(384, 512)))
            rights.append(
                jnp.concatenate([jnp.where(carried, back_low, 0.0), low(-beta * pull)], 0)
            )
        enters = [
            tn(jnp.concatenate([load(query_ref, *stream), kc_ref[block]], 0), right)
            for stream, block, right in zip(streams, blocks, rights)
        ]
        for block, back_low, pull, enter in zip(blocks, back_lows, pulls, enters):
            enter_ref[block] = enter
            back_ref[block] = back_low
            pull_ref[block] = pull

    prepare()
    between()
    flow = jnp.zeros((CHUNK, CHUNK), jnp.float32)
    for index in reversed(range(8)):
        block = index * 2 + which
        flow_low = low(flow)
        flow_ref[block] = flow_low
        flow = tn(step_ref[block], flow_low) + enter_ref[block]

    def collect(double, carry):
        streams = [(double * 4 + item, which) for item in range(4)]
        blocks = [index * 2 + sequence for index, sequence in streams]
        lines, places, betas, carrieds, closings = ([] for _ in range(5))
        for index, sequence in streams:
            line, place = columns_of(pos_ref, index, sequence)
            lines.append(line)
            places.append(place)
            betas.append(jax.nn.sigmoid(load(proj_ref, index, sequence, slice(384, 512))))
            carrieds.append(place > row.astype(jnp.float32))
            closings.append((127 - row).astype(jnp.float32) <= line[:, 127:128])
        queries = [load(query_ref, *stream) for stream in streams]
        keys_all = [load(key_ref, *stream) for stream in streams]
        updates = [update_ref[block].astype(jnp.float32) for block in blocks]
        weighted = [beta * update for beta, update in zip(betas, updates)]
        flows = [flow_ref[block] for block in blocks]
        states = [state_ref[block] for block in blocks]
        backs = [back_ref[block] for block in blocks]
        key_flows = [nn(keys, flow) for keys, flow in zip(keys_all, flows)]
        score_grads = [nt(back, low(weight)) for back, weight in zip(backs, weighted)]
        grams = [nt(keys, keys) for keys in keys_all]
        weight_grads = [
            pull_ref[block] + jnp.where(closing, key_flow, 0.0)
            for block, closing, key_flow in zip(blocks, closings, key_flows)
        ]
        right_grads = [
            tn(inv_ref[block], low(beta * weight_grad))
            for block, beta, weight_grad in zip(blocks, betas, weight_grads)
        ]
        score_lows = [
            low(jnp.where((depth >= 0) & (depth.astype(jnp.float32) <= place), score_grad, 0.0))
            for place, score_grad in zip(places, score_grads)
        ]
        query_grads = [
            nt(jnp.where(carried, back, 0.0), state) + nn(score_low, keys)
            for carried, back, state, score_low, keys in zip(
                carrieds, backs, states, score_lows, keys_all
            )
        ]
        mixing_grads = [
            jnp.where((depth < 0) & ((-depth).astype(jnp.float32) <= line), -nt(low(update), low(right_grad)), 0.0)
            for line, update, right_grad in zip(lines, updates, right_grads)
        ]
        gram_lows = [low(beta * mixing_grad) for beta, mixing_grad in zip(betas, mixing_grads)]
        key_grads = [
            nt(
                jnp.concatenate(
                    [low(jnp.where(closing, weight, 0.0)), low(jnp.where(carried, -right_grad, 0.0))], 1
                ),
                jnp.concatenate([flow, state], 1),
            )
            for closing, weight, carried, right_grad, flow, state in zip(
                closings, weighted, carrieds, right_grads, flows, states
            )
        ]
        key_grads = [
            key_grad
            + tn(jnp.concatenate([score_low, gram_low], 0), jnp.concatenate([query, keys], 0))
            + nn(gram_low, keys)
            for key_grad, score_low, gram_low, query, keys in zip(
                key_grads, score_lows, gram_lows, queries, keys_all
            )
        ]
        for item, (index, sequence) in enumerate(streams):
            total, moved = convolve(proj_ref, taps_ref, index, sequence, places[item])
            sigma, query, query_scale, keys, key_scale, _ = activate(total)
            beta = betas[item]
            beta_grad = jnp.sum(
                weight_grads[item] * updates[item] + mixing_grads[item] * grams[item], -1, keepdims=True
            )
            query_grad = query_grads[item] * 128 ** (-0.5)
            query_act = query_scale * (
                query_grad - query * jnp.sum(query * query_grad, -1, keepdims=True)
            )
            key_act = key_scale * (
                key_grads[item] - keys * jnp.sum(keys * key_grads[item], -1, keepdims=True)
            )
            act_grad = jnp.concatenate([query_act, key_act, right_grads[item]], 1)
            pre_grad = act_grad * (sigma * (1.0 + total * (1.0 - sigma)))
            for offset in range(4):
                taps_grad_ref[offset : offset + 1, :] += jnp.sum(
                    pre_grad * moved[offset], 0, keepdims=True
                )
            pre_ref[pl.ds(pl.multiple_of(index * CHUNK, CHUNK), CHUNK), :] = pre_grad
            logit_grad = jnp.where(column == 0, beta_grad * beta * (1.0 - beta), 0.0)
            store(out_ref, index, sequence, low(logit_grad), slice(384, 512))
        return carry

    lax.fori_loop(0, 2, collect, 0)
    after()

    def spread(pair_index, carry):
        for item in range(2):
            index, sequence = pair_index * 2 + item, which
            after = pl.multiple_of(jnp.minimum(index * CHUNK + CHUNK, 896), CHUNK)
            live = jnp.where(index == 7, 0.0, 1.0)
            current = pre_ref[pl.ds(pl.multiple_of(index * CHUNK, CHUNK), CHUNK), :]
            window = jnp.concatenate([current, pre_ref[pl.ds(after, 8), :] * live], 0)
            _, place = columns_of(pos_ref, index, sequence)
            _, follow = columns_of(pos_ref, jnp.minimum(index + 1, 7), sequence)
            places = jnp.concatenate([place, follow[0:8]], 0)[:, 0:1]
            total = current * taps_ref[0:1, :]
            for offset in range(1, 4):
                masked = window * (places >= offset).astype(jnp.float32)
                total = total + masked[offset : offset + CHUNK] * taps_ref[offset : offset + 1, :]
            store(out_ref, index, sequence, low(total), slice(0, 384))
        return carry

    lax.fori_loop(0, 4, spread, 0)


def saved_shapes():
    rows = jax.ShapeDtypeStruct((2048, CHUNK), jnp.bfloat16)
    small = jax.ShapeDtypeStruct((16, CHUNK, CHUNK), jnp.bfloat16)
    wide = jax.ShapeDtypeStruct((16, CHUNK, CHUNK), jnp.float32)
    return (rows, rows, small, small, small, small, small, small, wide)


def spot(y, z, core):
    return (y * 2 + z) * 2 + core


class Neighbours:
    def __init__(self):
        index = lax.axis_index("tensor")
        self.core = index % 2
        self.z = (index // 2) % 2
        self.y = index // 4
        up, down, far = (self.y + 1) % 4, (self.y + 3) % 4, (self.y + 2) % 4
        other = 1 - self.z
        self.up = spot(up, self.z, self.core)
        self.down = spot(down, self.z, self.core)
        self.side = spot(self.y, other, self.core)
        self.twin = spot(self.y, self.z, 1 - self.core)
        self.chips = {
            "own": self.y * 2 + self.z,
            "side": self.y * 2 + other,
            "down": down * 2 + self.z,
            "up": up * 2 + self.z,
            "downside": down * 2 + other,
            "upside": up * 2 + other,
            "far": far * 2 + self.z,
            "farside": far * 2 + other,
        }

    def mine(self, name):
        return self.chips[name] * 2 + self.core

    def twins(self, name):
        return self.chips[name] * 2 + 1 - self.core

    def quarter_at(self, step):
        quarter = step % 4
        shift = quarter + quarter // 2 - 2 * (quarter // 3)
        return (self.y + shift) % 4


def greet(devices):
    barrier = pltpu.get_barrier_semaphore()
    for device in devices:
        pl.semaphore_signal(barrier, inc=1, device_id=device, device_id_type=MESH)
    pl.semaphore_wait(barrier, len(devices))


def remote(source, target, send_sem, recv_sem, device):
    return pltpu.make_async_remote_copy(
        src_ref=source, dst_ref=target, send_sem=send_sem, recv_sem=recv_sem,
        device_id=device, device_id_type=MESH,
    )


NAMES = ("own", "side", "down", "up", "downside", "upside", "far", "farside")
ORDER = (("own", "side"), ("up", "upside"), ("down", "downside"), ("far", "farside"))


class Rows:
    def __init__(self, first, count):
        self.first, self.count = first, count
        self.whole = pl.ds(first, count)
        self.top = pl.ds(first, count // 2)
        self.bottom = pl.ds(first + count // 2, count // 2)


ALL, HALVES = Rows(0, 128), (Rows(0, 64), Rows(64, 64))


class Gather:
    copies = 17

    def __init__(self, near, buffer, sends, receives, rows=ALL):
        self.near, self.buffer, self.sends, self.receives = near, buffer, sends, receives
        self.rows = rows

    def piece(self, key, name):
        rows = self.rows
        part = {5: rows.top, 6: rows.bottom, 7: rows.top, 8: rows.bottom}.get(key, rows.whole)
        return self.buffer.at[self.near.mine(name), part]

    def copy(self, key, piece, device):
        return remote(piece, piece, self.sends.at[key], self.receives.at[key], {"tensor": device})

    def send(self, key, name, device):
        self.copy(key, self.piece(key, name), device).start()

    def arrive(self, key, name):
        self.copy(key, self.piece(key, name), self.near.twin).wait_recv()

    def to_twin(self, name):
        self.send(9 + NAMES.index(name), name, self.near.twin)

    def from_twin(self, *names):
        for name in names:
            piece = self.buffer.at[self.near.twins(name), self.rows.whole]
            self.copy(9 + NAMES.index(name), piece, self.near.twin).wait_recv()

    def start(self):
        near = self.near
        self.send(1, "own", near.up)
        self.send(2, "own", near.down)
        self.send(0, "own", near.side)
        self.to_twin("own")

    def from_down(self):
        self.arrive(1, "down")
        self.send(5, "down", self.near.up)
        self.to_twin("down")

    def from_up(self):
        self.arrive(2, "up")
        self.send(6, "up", self.near.down)
        self.to_twin("up")

    def from_side(self):
        self.arrive(0, "side")
        self.send(3, "side", self.near.up)
        self.send(4, "side", self.near.down)
        self.to_twin("side")

    def second(self):
        self.from_down()
        self.from_up()
        self.from_side()

    def third(self):
        self.arrive(5, "far")
        self.send(7, "far", self.near.side)
        self.arrive(6, "far")
        self.send(8, "far", self.near.side)
        self.to_twin("far")

    def fourth(self):
        self.arrive(4, "upside")
        self.to_twin("upside")
        self.arrive(3, "downside")
        self.to_twin("downside")

    def fifth(self):
        self.arrive(7, "farside")
        self.arrive(8, "farside")
        self.to_twin("farside")

    def finish(self):
        names = ("own", "own", "own", "side", "side", "down", "up", "far", "far") + NAMES
        for key, name in enumerate(names):
            self.copy(key, self.piece(key, name), self.near.twin).wait_send()


def add_rows(target, sources, count=128):
    def piece(index, carry):
        rows = pl.ds(pl.multiple_of(index * 16, 16), 16)
        total = target[rows].astype(jnp.float32)
        for source in sources:
            total = total + source[rows].astype(jnp.float32)
        target[rows] = total.astype(target.dtype)
        return carry

    lax.fori_loop(0, count // 16, piece, 0)


class Scatter:
    copies = 16

    def __init__(self, near, part, twin_part, slot, sends, receives, rows=ALL):
        self.near, self.part, self.twin_part, self.slot = near, part, twin_part, slot
        self.sends, self.receives, self.rows = sends, receives, rows

    def describe(self, key, source, target, device):
        return remote(source, target, self.sends.at[key], self.receives.at[key], {"tensor": device})

    def twin_copy(self, chip):
        whole = self.rows.whole
        return self.describe(
            8 + chip, self.part.at[chip * 2 + 1 - self.near.core, whole],
            self.twin_part.at[chip, whole], self.near.twin,
        )

    def to_twin(self, chip):
        self.twin_copy(chip).start()

    def mine(self, name, rows=None):
        return self.part.at[self.near.mine(name), self.rows.whole if rows is None else rows]

    def chip_sum(self, name):
        chip = self.near.chips[name]
        self.twin_copy(chip).wait_recv()
        add_rows(self.mine(name), [self.twin_part.at[chip, self.rows.whole]], self.rows.count)

    def outgoing(self, key):
        near, slot, rows = self.near, self.slot, self.rows
        name, place, part, device = (
            ("farside", 0, rows.whole, near.side),
            ("far", 1, rows.top, near.down),
            ("far", 1, rows.bottom, near.up),
            ("downside", 2, rows.whole, near.down),
            ("upside", 3, rows.whole, near.up),
            ("down", 4, rows.whole, near.down),
            ("up", 5, rows.whole, near.up),
            ("side", 6, rows.whole, near.side),
        )[key]
        return self.describe(key, self.mine(name, part), slot.at[place, part], device)

    def send(self, key):
        self.outgoing(key).start()

    def arrive(self, key):
        self.outgoing(key).wait_recv()

    def sums(self, *names):
        for name in names:
            self.chip_sum(name)
            key = {"farside": 0, "downside": 3, "upside": 4}.get(name)
            if key is not None:
                self.send(key)

    def first(self):
        self.sums("farside", "downside", "upside", "far", "down", "up", "side")

    def second(self):
        self.arrive(0)
        add_rows(self.mine("far"), [self.slot.at[0, self.rows.whole]], self.rows.count)
        self.send(1)
        self.send(2)

    def to_side(self):
        slot, rows = self.slot, self.rows
        self.arrive(3)
        self.arrive(4)
        add_rows(self.mine("side"), [slot.at[2, rows.whole], slot.at[3, rows.whole]], rows.count)
        self.send(7)

    def to_down(self):
        rows = self.rows
        self.arrive(1)
        add_rows(self.mine("down", rows.top), [self.slot.at[1, rows.top]], rows.count // 2)
        self.send(5)

    def to_up(self):
        rows = self.rows
        self.arrive(2)
        add_rows(self.mine("up", rows.bottom), [self.slot.at[1, rows.bottom]], rows.count // 2)
        self.send(6)

    def third(self):
        self.to_side()
        self.to_down()
        self.to_up()

    def fourth(self):
        self.twin_copy(self.near.chips["own"]).wait_recv()
        for key in (7, 5, 6):
            self.arrive(key)

    def total(self, rows):
        chip = self.near.chips["own"]
        value = self.part[chip * 2 + self.near.core, rows].astype(jnp.float32)
        value = value + self.twin_part[chip, rows].astype(jnp.float32)
        for place in (4, 5, 6):
            value = value + self.slot[place, rows].astype(jnp.float32)
        return value

    def finish(self):
        for chip in range(8):
            self.twin_copy(chip).wait_send()
        for key in range(8):
            self.outgoing(key).wait_send()


def at_steps(step, table):
    for moment, actions in table.items():

        @pl.when(step == moment)
        def _(actions=actions):
            for action in actions:
                action()


def pair(items, names):
    return lambda: items.from_twin(*names)


def summing(items, *names):
    return lambda: items.sums(*names)


HIDDEN = 384


def sigmoid(value):
    return 1.0 / (1.0 + jnp.exp(-value))


def rows_of(half, quarter):
    return pl.ds(pl.multiple_of(half * 1024 + quarter * 256, 256), 256)


def half_of(half):
    return pl.ds(pl.multiple_of(half * 64, 64), 64)


def quarter_rows(buffer, half, quarter):
    return buffer[pl.ds(quarter * 4, 4), half_of(half)].reshape(256, buffer.shape[2])


def lanes(block):
    return pl.ds(pl.multiple_of(block * 256, 256), 256)


def token_column(buffer, block):
    first = buffer[:, 0:64, lanes(block)].reshape(1024, 256)
    return jnp.concatenate([first, buffer[:, 64:128, lanes(block)].reshape(1024, 256)], 0)


def scatter_quarter(scatters, half, quarter, partial, part):
    part[pl.ds(quarter * 4, 4), half_of(half)] = partial.reshape(4, 64, partial.shape[1])
    for index, scatter in enumerate(scatters):

        @pl.when(half == index)
        def _(scatter=scatter):
            scatter.to_twin(quarter * 2)
            scatter.to_twin(quarter * 2 + 1)


def ffn_kernel(
    input_ref, hidden_ref, teacher_ref, mask_ref, gate_up_ref, down_shard_ref,
    block_ref, grad_ref, back_ref, square_ref, weight_ref, down_grad_ref,
    tokens, grads, both, act_t, both_t, part, twin_part, slot, down_ref, down_part, down_slot, down_staged,
    down_send, down_recv, leave_send, leave_recv, *sems,
):
    near = Neighbours()
    data = lax.axis_index("dp")
    neighbours = [{"tensor": device} for device in (near.up, near.down, near.side, near.twin)]
    neighbours = neighbours + [{"dp": device} for device in data_neighbours()]
    own = near.mine("own")
    tokens[own] = input_ref[...]
    down_ref[lanes(data)] = down_shard_ref[...]
    greet(neighbours)
    a, g = (
        [Gather(near, buffer, sems[k + 2 * h], sems[k + 2 * h + 1], HALVES[h]) for h in range(2)]
        for buffer, k in ((tokens, 0), (grads, 4))
    )
    r, b = (
        [Scatter(near, part, twin_part, slot, sems[k + 2 * h], sems[k + 2 * h + 1], HALVES[h]) for h in range(2)]
        for k in (8, 12)
    )
    a[0].start()
    down = DataGather(down_shard_ref, lambda block: down_ref.at[lanes(block)], down_send, down_recv)
    down.start()

    def forward(step, carry):
        at_steps(step, {
            0: [a[0].second, a[1].start, down.relay, a[0].third, a[1].from_side, a[0].fourth, down.arrive, pair(a[0], ORDER[0])],
            1: [pair(a[0], ORDER[1])],
            2: [a[0].fifth, summing(r[0], "side"), pair(a[0], ORDER[2])],
            3: [summing(r[0], "up", "upside"), a[1].from_down, a[1].from_up, pair(a[0], ORDER[3])],
            4: [summing(r[0], "downside", "down"), a[1].fourth, pair(a[1], ORDER[0])],
            5: [summing(r[0], "farside", "far"), pair(a[1], ORDER[1])],
            6: [summing(r[1], "side"), a[1].third, r[0].to_side, pair(a[1], ORDER[2])],
            7: [
                summing(r[1], "upside"), r[0].second, summing(r[1], "up", "down", "downside"), r[0].to_down,
                a[1].fifth, pair(a[1], ORDER[3]),
            ],
        })
        half, quarter = step // 4, near.quarter_at(step)
        rows = rows_of(half, quarter)
        product = nn(quarter_rows(tokens, half, quarter), gate_up_ref[...])
        both[rows, :] = product
        gate, up = product[:, :HIDDEN], product[:, HIDDEN:]
        act = low(gate * sigmoid(gate) * up)
        act_t[:, rows] = act.T
        scatter_quarter(r, half, quarter, low(nt(act, down_ref[...])), part)
        return carry

    lax.fori_loop(0, 8, forward, 0)
    square_ref[...] = jnp.zeros_like(square_ref)

    def middle(half):
        def piece(index, carry):
            rows = pl.ds(pl.multiple_of(half * 64 + index * 16, 16), 16)
            output = hidden_ref[rows] + r[half].total(rows)
            block_ref[rows] = low(output)
            diff = output - teacher_ref[rows].astype(jnp.float32)
            weight = mask_ref[0, rows, 0:1]
            grad = mask_ref[1, rows, 0:1] * diff
            grad_ref[rows] = grad
            grads[own, rows] = low(grad)
            squares = jnp.sum(weight * jnp.sum(diff * diff, -1, keepdims=True), 0, keepdims=True)
            square_ref[...] += jnp.broadcast_to(squares, (8, 128))
            return carry

        lax.fori_loop(0, 4, piece, 0)

    r[0].to_up()
    r[1].to_side()
    r[1].sums("far", "farside")
    r[0].fourth()
    middle(0)
    g[0].start()
    r[1].second()
    g[0].from_down()
    g[0].from_up()
    r[1].to_down()
    r[1].to_up()
    g[0].from_side()
    g[0].third()
    r[0].finish()

    def turn():
        r[1].fourth()
        middle(1)
        r[1].finish()

    def backward(step, carry):
        at_steps(step, {
            0: [pair(g[0], ORDER[0])],
            1: [turn, summing(b[0], "side"), g[1].start, g[0].fifth, g[0].fourth, pair(g[0], ORDER[1])],
            2: [g[1].second, pair(g[0], ORDER[2])],
            3: [summing(b[0], "upside", "up"), pair(g[0], ORDER[3])],
            4: [summing(b[0], "downside", "down"), g[1].third, pair(g[1], ORDER[0])],
            5: [summing(b[0], "farside", "far"), g[1].fourth, summing(b[1], "side"), pair(g[1], ORDER[1])],
            6: [b[0].to_side, g[1].fifth, pair(g[1], ORDER[2])],
            7: [b[0].second, summing(b[1], "upside", "up"), pair(g[1], ORDER[3])],
        })
        half, quarter = step // 4, near.quarter_at(step)
        rows = rows_of(half, quarter)
        act_grad = nn(quarter_rows(grads, half, quarter), down_ref[...])
        gate, up = both[rows, :HIDDEN], both[rows, HIDDEN:]
        sigma = sigmoid(gate)
        gate_low = low(act_grad * up * sigma * (1.0 + gate * (1.0 - sigma)))
        up_low = low(act_grad * gate * sigma)
        both_low = jnp.concatenate([gate_low, up_low], 1)
        both_t[:, rows] = both_low.T
        scatter_quarter(b, half, quarter, low(nt(both_low, gate_up_ref[...])), part)
        return carry

    lax.fori_loop(0, 8, backward, 0)
    b[1].sums("downside", "down")
    b[0].to_down()
    b[0].to_up()

    def down_weights(step, carry):
        at_steps(step, {2: [summing(b[1], "far", "farside")]})
        down_part[:, lanes(step)] = low(nn(act_t[...], token_column(grads, step)))
        return carry

    lax.fori_loop(0, 8, down_weights, 0)
    place = DataPlace()
    leave = DataScatter(
        lambda block: down_part.at[:, lanes(block)],
        lambda other, rows: down_part[rows, lanes(place.block(0, other))],
        down_slot, down_staged, leave_send, leave_recv,
    )
    leave.start()

    def ending(half):
        b[half].fourth()

        def piece(index, carry):
            rows = pl.ds(pl.multiple_of(half * 64 + index * 16, 16), 16)
            back_ref[rows] = b[half].total(rows)
            return carry

        lax.fori_loop(0, 4, piece, 0)

    def weights(step, carry):
        at_steps(step, {3: [b[1].to_side], 7: [b[1].second]})
        weight_ref[:, lanes(step)] = low(nn(both_t[...], token_column(tokens, step)))
        return carry

    lax.fori_loop(0, 8, weights, 0)
    ending(0)
    b[1].to_down()
    b[1].to_up()
    leave.relay()
    ending(1)
    leave.result(down_grad_ref)
    for item in (down, leave, a[0], a[1], g[0], g[1], b[0], b[1]):
        item.finish()


def data_neighbours():
    place = DataPlace()
    return [place.block(shift, 0) for shift in range(1, 4)] + [place.block(0, 1)]


def run_ffn(ffn_in, hidden, teacher, mask, gate_up, down_shard):
    rows, features = ffn_in.shape
    wide = jax.ShapeDtypeStruct((rows, features), jnp.float32)
    vmem = pl.BlockSpec(memory_space=pltpu.VMEM)
    counts = [7] * 4 + [Gather.copies] * 8 + [Scatter.copies] * 8
    semaphores = [pltpu.SemaphoreType.DMA((count,)) for count in counts]
    return pl.pallas_call(
        ffn_kernel,
        out_shape=(
            jax.ShapeDtypeStruct((rows, features), jnp.bfloat16),
            wide,
            wide,
            jax.ShapeDtypeStruct((8, 128), jnp.float32),
            jax.ShapeDtypeStruct((2 * HIDDEN, features), jnp.bfloat16),
            jax.ShapeDtypeStruct((HIDDEN, 256), jnp.float32),
        ),
        in_specs=[vmem] * 6,
        out_specs=[vmem] * 6,
        scratch_shapes=[
            pltpu.VMEM((16, 128, 2048), jnp.bfloat16),
            pltpu.VMEM((16, 128, 2048), jnp.bfloat16),
            pltpu.VMEM((2048, 2 * HIDDEN), jnp.float32),
            pltpu.VMEM((HIDDEN, 2048), jnp.bfloat16),
            pltpu.VMEM((2 * HIDDEN, 2048), jnp.bfloat16),
            pltpu.VMEM((16, 128, 2048), jnp.bfloat16),
            pltpu.VMEM((8, 128, 2048), jnp.bfloat16),
            pltpu.VMEM((7, 128, 2048), jnp.bfloat16),
            pltpu.VMEM((2048, HIDDEN), jnp.bfloat16),
            pltpu.VMEM((HIDDEN, 2048), jnp.bfloat16),
            pltpu.VMEM((7, HIDDEN, 256), jnp.bfloat16),
            pltpu.VMEM((HIDDEN, 256), jnp.bfloat16),
        ]
        + semaphores,
        compiler_params=pltpu.CompilerParams(
            collective_id=1, has_side_effects=True, vmem_limit_bytes=63 << 20
        ),
        cost_estimate=pl.CostEstimate(flops=160 << 30, bytes_accessed=16 << 20, transcendentals=0),
        name="feed_forward",
    )(ffn_in, hidden, teacher, mask, gate_up, down_shard)


def everyone():
    tensor, data = lax.axis_index("tensor"), lax.axis_index("dp")
    devices = [{"tensor": (tensor + shift) % 16} for shift in range(1, 16)]
    return devices + [{"dp": (data + shift) % 8} for shift in range(1, 8)]


class Fan:
    def __init__(self, axis, count, source, target, sends, receives):
        self.axis, self.count, self.source, self.target = axis, count, source, target
        self.sends, self.receives = sends, receives
        self.index = lax.axis_index(axis)

    def copy(self, shift):
        peer = (self.index + shift) % self.count
        return remote(
            self.source(peer), self.target(self.index), self.sends.at[shift],
            self.receives.at[shift], {self.axis: peer},
        )

    def start(self):
        for shift in range(1, self.count):
            self.copy(shift).start()

    def arrive(self):
        for shift in range(1, self.count):
            piece = self.target((self.index + self.count - shift) % self.count)
            peer = (self.index + shift) % self.count
            remote(
                piece, piece, self.sends.at[shift], self.receives.at[shift], {self.axis: peer}
            ).wait_recv()

    def finish(self):
        for shift in range(1, self.count):
            self.copy(shift).wait_send()


class DataPlace:
    def __init__(self):
        index = lax.axis_index("dp")
        self.x, self.z = index % 4, index // 4

    def block(self, shift, other):
        return ((self.z + other) % 2) * 4 + (self.x + shift) % 4


class DataGather:
    copies = 7

    def __init__(self, source, target, sends, receives):
        self.place = DataPlace()
        self.source, self.target, self.sends, self.receives = source, target, sends, receives

    def describe(self, key):
        place = self.place
        if key == 0:
            return self.copy(key, self.source, place.block(0, 0), place.block(0, 1))
        if key < 4:
            return self.copy(key, self.source, place.block(0, 0), place.block(key, 0))
        partner = place.block(0, 1)
        return self.copy(key, self.target(partner), partner, place.block(key - 3, 0))

    def copy(self, key, source, block, peer):
        return remote(
            source, self.target(block), self.sends.at[key], self.receives.at[key], {"dp": peer}
        )

    def start(self):
        for key in range(4):
            self.describe(key).start()

    def wait(self, key, block):
        piece = self.target(block)
        self.copy(key, piece, block, self.place.block(0, 1)).wait_recv()

    def relay(self):
        self.wait(0, self.place.block(0, 1))
        for key in range(4, 7):
            self.describe(key).start()

    def arrive(self):
        for shift in range(1, 4):
            self.wait(shift, self.place.block(4 - shift, 0))
            self.wait(3 + shift, self.place.block(4 - shift, 1))

    def finish(self):
        for key in range(7):
            self.describe(key).wait_send()


class DataScatter:
    copies = 7

    def __init__(self, part, own, slot, staged, sends, receives):
        self.place = DataPlace()
        self.part, self.own, self.slot, self.staged = part, own, slot, staged
        self.sends, self.receives = sends, receives

    def describe(self, key):
        place = self.place
        if key == 6:
            source, peer = self.staged, place.block(0, 1)
        else:
            shift, other = key // 2 + 1, key % 2
            source, peer = self.part(place.block(shift, other)), place.block(shift, 0)
        return remote(
            source, self.slot.at[key], self.sends.at[key], self.receives.at[key], {"dp": peer}
        )

    def start(self):
        for key in range(6):
            self.describe(key).start()

    def summed(self, other, rows, extra):
        total = self.own(other, rows).astype(jnp.float32)
        for key in range(other, 6, 2):
            total = total + self.slot[key, rows].astype(jnp.float32)
        if extra:
            total = total + self.slot[6, rows].astype(jnp.float32)
        return total

    def relay(self):
        for key in (1, 3, 5):
            self.describe(key).wait_recv()

        def piece(index, carry):
            rows = pl.ds(pl.multiple_of(index * 16, 16), 16)
            self.staged[rows] = low(self.summed(1, rows, False))
            return carry

        lax.fori_loop(0, self.staged.shape[0] // 16, piece, 0)
        self.describe(6).start()

    def result(self, output):
        for key in (0, 2, 4, 6):
            self.describe(key).wait_recv()

        def piece(index, carry):
            rows = pl.ds(pl.multiple_of(index * 16, 16), 16)
            output[rows] = self.summed(0, rows, True)
            return carry

        lax.fori_loop(0, self.staged.shape[0] // 16, piece, 0)

    def finish(self):
        for key in range(7):
            self.describe(key).wait_send()


def tile_sum(first, second, axes, sems):
    tensor, data = lax.axis_index("tensor"), lax.axis_index("dp")
    one = Fan("tensor", 16, lambda peer: first.at[tensor], lambda index: first.at[index], sems[0], sems[1])
    two = Fan("dp", 8, lambda peer: second.at[data], lambda index: second.at[index], sems[2], sems[3])
    return one, two


def entry_kernel(
    normed_ref, mix_ref, small_ref, count_ref, pos_ref, gate_up_ref, out_ref,
    gathered_ref, mix_full_ref, taps_ref, gain_ref, total_ref, gate_up_full_ref, out_full_ref,
    proj_ref, spread_ref, heads_ref,
    query_ref, key_ref, inv_ref, kc_ref, score_ref, step_ref, state_ref, update_ref, raw_ref,
    tokens, small, counts, count_rows, free_ref, shift_ref,
    mix_send, mix_recv, wide_send, wide_recv, small_send, small_recv,
    out_send, out_recv, all_send, all_recv, count_send, count_recv, row_send, row_recv, local, *sems,
):
    near = Neighbours()
    tensor, data = lax.axis_index("tensor"), lax.axis_index("dp")
    own = near.mine("own")
    block_rows = pl.ds(pl.multiple_of(data * 256, 256), 256)

    def rows_of_data(ref):
        return lambda block: ref.at[pl.ds(pl.multiple_of(block * 256, 256), 256)]

    def lanes_of_data(block):
        return out_full_ref.at[tensor, :, pl.ds(pl.multiple_of(block * 256, 256), 256)]

    wide_own = pltpu.make_async_copy(gate_up_ref, gate_up_full_ref.at[block_rows], local.at[0])
    out_own = pltpu.make_async_copy(out_ref, lanes_of_data(data), local.at[1])
    wide_own.start()
    out_own.start()
    tokens[own] = normed_ref[...]
    mix_full_ref[block_rows] = mix_ref[...]
    small[data] = small_ref[...]
    counts[tensor] = count_ref[...]
    greet(everyone())
    a = [Gather(near, tokens, sems[2 * h], sems[2 * h + 1], HALVES[h]) for h in range(2)]
    mix = DataGather(mix_ref, rows_of_data(mix_full_ref), mix_send, mix_recv)
    wide = DataGather(gate_up_ref, rows_of_data(gate_up_full_ref), wide_send, wide_recv)
    tiny = Fan("dp", 8, lambda peer: small.at[data], lambda index: small.at[index], small_send, small_recv)
    outs = Fan("dp", 8, lambda peer: out_ref, lanes_of_data, out_send, out_recv)
    one, two = tile_sum(counts, count_rows, None, (count_send, count_recv, row_send, row_recv))
    everything = Gather(near, out_full_ref, all_send, all_recv)
    a[0].start()
    outs.start()
    one.start()
    tiny.start()
    mix.start()

    def counted():
        one.arrive()
        count_rows[data] = jnp.sum(counts[...], 0)
        two.start()

    def outer():
        out_own.wait()
        outs.arrive()
        everything.start()

    def ready():
        tiny.arrive()
        two.arrive()
        total_ref[...] = jnp.sum(count_rows[...], 0)
        table = jnp.sum(small[...].astype(jnp.float32), 0)
        for tap in range(4):
            for field in range(3):
                row = tap * 3 + field
                taps_ref[tap : tap + 1, field * 128 : field * 128 + 128] = table[row : row + 1]
        gain_ref[0:1, :] = table[12:13]

    def head_rows(half):
        def place(block):
            return heads_ref.at[pl.ds(pl.multiple_of(block * 128 + half * 64, 64), 64)]

        return place

    def target_rows(half):
        return lambda index: spread_ref.at[index, HALVES[half].whole]

    exchanges = [
        Fan("tensor", 16, head_rows(h), target_rows(h), sems[4 + 2 * h], sems[5 + 2 * h]) for h in range(2)
    ]
    keep = pltpu.make_async_copy(tokens, gathered_ref, local.at[2])
    a[0].second()
    a[1].start()
    counted()
    mix.relay()
    a[0].third()
    a[0].fourth()
    outer()
    a[1].second()
    a[0].fifth()
    mix.arrive()
    wide.start()

    def per_sequence(sequence, carry):
        def project(step, inner):
            at_steps(sequence * 4 + step, {
                0: [pair(a[0], ORDER[0])],
                1: [pair(a[0], ORDER[1])],
                2: [pair(a[0], ORDER[2])],
                3: [a[1].third, a[1].fourth, pair(a[0], ORDER[3])],
                4: [pair(a[1], ORDER[0])],
                5: [pair(a[1], ORDER[1])],
                6: [pair(a[1], ORDER[2])],
                7: [pair(a[1], ORDER[3]), keep.start],
            })
            quarter = near.quarter_at(step)
            product = nn(quarter_rows(tokens, sequence, quarter), mix_full_ref[...])
            for item in range(4):
                rows = pl.ds(pl.multiple_of((quarter * 4 + item) * 128 + sequence * 64, 64), 64)
                proj_ref[rows, :] = product[item * 64 : item * 64 + 64]
            return inner

        lax.fori_loop(0, 4, project, 0)
        at_steps(sequence, {0: [ready]})
        mixer_forward(
            proj_ref, pos_ref, taps_ref, gain_ref,
            heads_ref, query_ref, key_ref, inv_ref, kc_ref, score_ref, step_ref, state_ref, update_ref, raw_ref,
            free_ref, shift_ref, sequence,
            lambda: at_steps(sequence, {0: [a[1].fifth, everything.second, wide.relay], 1: [everything.fourth]}),
        )
        at_steps(sequence, {
            0: [exchanges[0].start, everything.third],
            1: [exchanges[1].start, everything.fifth],
        })
        return carry

    lax.fori_loop(0, 2, per_sequence, 0)
    spread_ref[tensor] = heads_ref[pl.ds(pl.multiple_of(tensor * 128, 128), 128)]
    everything.from_twin(*NAMES)
    wide.arrive()
    wide_own.wait()
    keep.wait()
    for exchange in exchanges:
        exchange.arrive()
    for item in (a[0], a[1], mix, wide, tiny, outs, one, two, everything, exchanges[0], exchanges[1]):
        item.finish()


def dma(*counts):
    return [pltpu.SemaphoreType.DMA((count,)) for count in counts]


def run_entry(normed, mix_shard, small, count, pos, gate_up, out_weight):
    vmem, hbm = pl.BlockSpec(memory_space=pltpu.VMEM), pl.BlockSpec(memory_space=pl.ANY)
    half, full = jnp.bfloat16, jnp.float32
    shape = jax.ShapeDtypeStruct
    return pl.pallas_call(
        entry_kernel,
        out_shape=(
            shape((16, 128, 2048), half),
            shape((2048, WIDE), half),
            shape((8, 384), full),
            shape((8, CHUNK), full),
            shape((8, 128), full),
            shape((2048, 2 * HIDDEN), half),
            shape((16, 128, 2048), half),
            shape((2048, WIDE), full),
            shape((16, 128, CHUNK), half),
            shape((2048, CHUNK), half),
        )
        + saved_shapes(),
        in_specs=[vmem] * 5 + [hbm] * 2,
        out_specs=[hbm, vmem, vmem, vmem, vmem, hbm, hbm] + [vmem] * 12,
        scratch_shapes=[
            pltpu.VMEM((16, 128, 2048), half),
            pltpu.VMEM((8, 16, 128), half),
            pltpu.VMEM((16, 8, 128), full),
            pltpu.VMEM((8, 8, 128), full),
            pltpu.VMEM((16, CHUNK, CHUNK), full),
            pltpu.VMEM((16, CHUNK, CHUNK), full),
        ]
        + dma(7, 7, 7, 7, 8, 8, 8, 8, 17, 17, 16, 16, 8, 8, 3, 17, 17, 17, 17, 16, 16, 16, 16),
        compiler_params=pltpu.CompilerParams(
            collective_id=2, has_side_effects=True, vmem_limit_bytes=62 << 20
        ),
        cost_estimate=pl.CostEstimate(flops=60 << 30, bytes_accessed=16 << 20, transcendentals=0),
        name="entry",
    )(normed, mix_shard, small, count, pos, gate_up, out_weight)


SMALL = 16


def exit_kernel(
    heads_grad_ref, attention_ref, ffn_part_ref, gathered_ref, proj_ref, pos_ref, taps_ref, gain_ref,
    mix_ref, heads_ref, unit_ref, sums_ref,
    query_ref, key_ref, inv_ref, kc_ref, score_ref, step_ref, state_ref, update_ref, raw_ref,
    attn_ref, ffn_ref, weight_ref, total_ref,
    grad, attention, proj_low, taps_grad, gain_grad,
    back_ref, pull_ref, flow_ref, enter_ref, pre_ref,
    part, twin_part, slot, ffn_own, ffn_slot, ffn_staged, parts, part_slot, part_staged, proj_t, tile,
    sums, sum_rows,
    head_send, head_recv, gather_send, gather_recv, ffn_send, ffn_recv, mix_send, mix_recv,
    sum_send, sum_recv, row_send, row_recv, local, *sems,
):
    near = Neighbours()
    tensor, data = lax.axis_index("tensor"), lax.axis_index("dp")
    own = near.mine("own")
    place = DataPlace()

    loads = [
        pltpu.make_async_copy(ffn_part_ref.at[:, lanes(place.block(0, other))], ffn_own.at[other], local.at[other])
        for other in range(2)
    ]
    for copy in loads:
        copy.start()
    attention[own] = attention_ref[...]
    greet(everyone())

    def head_rows(block):
        return grad.at[pl.ds(pl.multiple_of(block * 128, 128), 128)]

    exchange = Fan("tensor", 16, lambda peer: heads_grad_ref.at[peer], head_rows, head_send, head_recv)
    exchange.start()
    gather = Gather(near, attention, gather_send, gather_recv)
    gather.start()
    ffn = DataScatter(
        lambda block: ffn_part_ref.at[:, lanes(block)], lambda other, rows: ffn_own[other, rows],
        ffn_slot, ffn_staged, ffn_send, ffn_recv,
    )
    ffn.start()
    grad[pl.ds(pl.multiple_of(tensor * 128, 128), 128)] = heads_grad_ref[tensor]
    exchange.arrive()
    taps_grad[...] = jnp.zeros_like(taps_grad)
    gain_grad[...] = jnp.zeros_like(gain_grad)
    scatters = [
        Scatter(near, part, twin_part, slot, sems[2 * h], sems[2 * h + 1], HALVES[h]) for h in range(2)
    ]

    def per_sequence(sequence, carry):
        mixer_backward(
            grad, proj_ref, pos_ref, taps_ref, gain_ref,
            query_ref, key_ref, inv_ref, kc_ref, score_ref, step_ref, state_ref, update_ref, raw_ref,
            proj_low, taps_grad, gain_grad,
            back_ref, pull_ref, flow_ref, enter_ref, pre_ref, sequence,
            lambda: at_steps(sequence, {}),
            lambda: at_steps(sequence, {0: [gather.second], 1: [gather.third, scatters[0].second]}),
        )

        def backward(step, inner):
            quarter = near.quarter_at(step)
            pieces = []
            for item in range(4):
                rows = pl.ds(pl.multiple_of((quarter * 4 + item) * 128 + sequence * 64, 64), 64)
                pieces.append(proj_low[rows, :])
            values = jnp.concatenate(pieces, 0)
            keep = lax.broadcasted_iota(jnp.int32, (256, WIDE), 1) <= 384
            proj_t[:, rows_of(sequence, quarter)] = values.T[:400]
            partial = low(nt(jnp.where(keep, values, jnp.zeros_like(values)), mix_ref[...]))
            scatter_quarter(scatters, sequence, quarter, partial, part)
            return inner

        lax.fori_loop(0, 4, backward, 0)
        at_steps(sequence, {0: [scatters[0].first], 1: [gather.fourth, scatters[1].first]})
        return carry

    lax.fori_loop(0, 2, per_sequence, 0)
    units = pltpu.make_async_copy(unit_ref, enter_ref, local.at[4])
    units.start()

    def fetch(step):
        return pltpu.make_async_copy(gathered_ref.at[:, :, lanes(step)], tile.at[step % 2], local.at[2 + step % 2])

    fetch(0).start()
    table = jnp.concatenate([taps_grad[...], gain_grad[...]], 1)

    def weights(step, carry):
        @pl.when(step < 7)
        def _():
            fetch(step + 1).start()

        fetch(step).wait()
        first = tile[step % 2, :, 0:64].reshape(1024, 256)
        column = jnp.concatenate([first, tile[step % 2, :, 64:128].reshape(1024, 256)], 0)
        product = nn(proj_t[...], column)
        parts[0:400, lanes(step)] = low(product)
        at_steps(step, {3: [scatters[0].third], 5: [gather.fifth], 7: [scatters[1].second]})
        return carry

    lax.fori_loop(0, 8, weights, 0)
    gather.from_twin(*NAMES)

    def out_weights(step, carry):
        parts[400:528, lanes(step)] = low(tn(heads_ref[...], attention[:, :, lanes(step)].reshape(2048, 256)))
        return carry

    lax.fori_loop(0, 8, out_weights, 0)
    pick_row = lax.broadcasted_iota(jnp.int32, (CHUNK, 2048), 0)
    pick_lane = lax.broadcasted_iota(jnp.int32, (CHUNK, 2048), 1)
    wanted = (pick_lane // 256) * 16 + pick_lane % 256
    select = ((pick_row == wanted) & (pick_lane % 256 < 16)).astype(jnp.bfloat16)
    for tap in range(4):
        for field in range(3):
            row = tap * 3 + field
            pull_ref[0, row : row + 1, :] = taps_grad[tap : tap + 1, field * 128 : field * 128 + 128]
    pull_ref[0, 12:13, :] = gain_grad[0:1, :]
    small = nn(low(pull_ref[0, 0:16, :]), select)
    small_row = lax.broadcasted_iota(jnp.int32, (16, 2048), 0)
    moved = jnp.concatenate([small[15:16], small[0:15]], 0)
    beta_row = parts[384:400, :].astype(jnp.float32)
    parts[384:400, :] = low(jnp.where(small_row == 0, beta_row, moved))
    mix = DataScatter(
        lambda block: parts.at[:, lanes(block)],
        lambda other, rows: parts[rows, lanes(place.block(0, other))],
        part_slot, part_staged, mix_send, mix_recv,
    )
    mix.start()
    for copy in loads:
        copy.wait()
    units.wait()
    scatters[1].third()
    ffn.relay()

    def ending(half):
        def piece(index, total):
            rows = pl.ds(pl.multiple_of(half * 64 + index * 16, 16), 16)
            value = scatters[half].total(rows)
            attn_ref[rows] = value
            return total + value * jnp.concatenate([enter_ref[block, rows] for block in range(16)], 1)

        scatters[half].fourth()
        return lax.fori_loop(0, 4, piece, jnp.zeros((16, 2048), jnp.float32))

    total = ending(0)
    mix.relay()
    total = total + ending(1)
    total = jnp.sum(total, 0, keepdims=True)
    sums[tensor, 8:24] = sums_ref[8:24]
    for piece in range(8):
        sums[tensor, piece : piece + 1] = total[:, piece * 256 : piece * 256 + 256]
    one, two = tile_sum(sums, sum_rows, None, (sum_send, sum_recv, row_send, row_recv))
    one.start()
    one.arrive()
    sum_rows[data] = jnp.sum(sums[...], 0)
    two.start()
    ffn.result(ffn_ref)
    two.arrive()
    total_ref[...] = jnp.sum(sum_rows[...], 0)
    mix.result(weight_ref)
    for item in (exchange, gather, ffn, scatters[0], scatters[1], mix, one, two):
        item.finish()


def run_exit(heads_grad, attention, ffn_part, gathered, proj, pos, taps, gain, mix, heads, unit, sums, saved):
    vmem, hbm = pl.BlockSpec(memory_space=pltpu.VMEM), pl.BlockSpec(memory_space=pl.ANY)
    half, full = jnp.bfloat16, jnp.float32
    shape = jax.ShapeDtypeStruct
    return pl.pallas_call(
        exit_kernel,
        out_shape=(
            shape((128, 2048), full),
            shape((2 * HIDDEN, 256), full),
            shape((528, 256), full),
            shape((24, 256), full),
        ),
        in_specs=[vmem] * 2 + [hbm] * 2 + [vmem] * 6 + [hbm] + [vmem] * 10,
        out_specs=[vmem] * 4,
        scratch_shapes=[
            pltpu.VMEM((2048, CHUNK), half),
            pltpu.VMEM((16, 128, 2048), half),
            pltpu.VMEM((2048, WIDE), half),
            pltpu.VMEM((8, 384), full),
            pltpu.VMEM((8, CHUNK), full),
            pltpu.VMEM((16, CHUNK, CHUNK), half),
            pltpu.VMEM((16, CHUNK, CHUNK), full),
            pltpu.VMEM((16, CHUNK, CHUNK), half),
            pltpu.VMEM((16, CHUNK, CHUNK), full),
            pltpu.VMEM((1024, 384), full),
            pltpu.VMEM((16, 128, 2048), half),
            pltpu.VMEM((8, 128, 2048), half),
            pltpu.VMEM((7, 128, 2048), half),
            pltpu.VMEM((2, 2 * HIDDEN, 256), half),
            pltpu.VMEM((7, 2 * HIDDEN, 256), half),
            pltpu.VMEM((2 * HIDDEN, 256), half),
            pltpu.VMEM((528, 2048), half),
            pltpu.VMEM((7, 528, 256), half),
            pltpu.VMEM((528, 256), half),
            pltpu.VMEM((400, 2048), half),
            pltpu.VMEM((2, 16, 128, 256), half),
            pltpu.VMEM((16, 24, 256), full),
            pltpu.VMEM((8, 24, 256), full),
        ]
        + dma(16, 16, 17, 17, 7, 7, 7, 7, 16, 16, 8, 8, 5, 16, 16, 16, 16),
        compiler_params=pltpu.CompilerParams(
            collective_id=3, has_side_effects=True, vmem_limit_bytes=63 << 20
        ),
        cost_estimate=pl.CostEstimate(flops=60 << 30, bytes_accessed=16 << 20, transcendentals=0),
        name="exit",
    )(heads_grad, attention, ffn_part, gathered, proj, pos, taps, gain, mix, heads, unit, sums, *saved)


def token_places(segment):
    length = segment.shape[1]
    before = jnp.sum((segment[:, None, :] < segment[:, :, None]).astype(jnp.int32), -1)
    place = jnp.arange(length, dtype=jnp.int32)[None, :] - before
    return jnp.transpose(place.reshape(2, 8, CHUNK), (1, 0, 2)).reshape(16, CHUNK).astype(jnp.float32)


def pad_lanes(array, width):
    return jnp.pad(array, ((0, 0), (0, width - array.shape[1])))


def f32(value):
    return value.astype(jnp.float32)


def body(
    inputs, teacher, segment_ids, padding, attn_gain, qkv_weight, beta_weight, conv_taps, head_gain,
    out_weight, mlp_gain, gate_weight, up_weight, down_weight,
):
    hidden_units = gate_weight.shape[1]
    rows = 128
    features = inputs.shape[2]

    small = jnp.concatenate([conv_taps.reshape(12, 16), head_gain.reshape(1, 16)], 0)
    lane = jnp.arange(CHUNK)[None, :] // 16 == lax.axis_index("dp")
    small = jnp.where(lane, jnp.tile(jnp.pad(small, ((0, 3), (0, 0))), (1, 8)), 0)
    mix_shard = jnp.concatenate(
        [qkv_weight.reshape(256, 384), jnp.broadcast_to(beta_weight, (256, CHUNK))], 1
    )
    gate_up_shard = jnp.concatenate([pad_lanes(gate_weight, HIDDEN), pad_lanes(up_weight, HIDDEN)], 1)
    down_shard = pad_lanes(jnp.transpose(down_weight), HIDDEN)
    count = jnp.broadcast_to(f32(jnp.sum(padding)), (8, 128))

    tokens = f32(inputs.reshape(rows, features))
    attn_scale = lax.rsqrt(jnp.mean(tokens * tokens, -1, keepdims=True) + 1e-06)
    attn_unit = tokens * attn_scale
    normed = (attn_unit * attn_gain).astype(jnp.bfloat16)
    pos = token_places(segment_ids)
    (
        gathered, mix_full, taps, gain, total, gate_up, out_full, proj, spread, heads, *saved
    ) = run_entry(normed, mix_shard, small, count, pos, gate_up_shard, out_weight)
    out_full = out_full.reshape(features, features)
    valid = total[0, 0]
    scale = 16 * 1024 / valid
    heads_rows = jnp.transpose(spread, (1, 0, 2)).reshape(rows, features)
    hidden = tokens + nn(heads_rows, out_full)

    mlp_scale = lax.rsqrt(jnp.mean(hidden * hidden, -1, keepdims=True) + 1e-06)
    mlp_unit = hidden * mlp_scale
    ffn_in = (mlp_unit * mlp_gain).astype(jnp.bfloat16)
    mask = f32(padding.reshape(rows, 1))
    masks = jnp.broadcast_to(jnp.stack([mask, scale * mask]), (2, rows, CHUNK))
    output, block_grad, mlp_grad, square_tile, ffn_part, down_grad = run_ffn(
        ffn_in, hidden, teacher.reshape(rows, features), masks, gate_up, down_shard
    )

    mlp_sum = jnp.sum(mlp_grad * mlp_unit, 0)
    mlp_inner = mlp_grad * mlp_gain
    hidden_grad = block_grad + mlp_scale * (
        mlp_inner - mlp_unit * jnp.mean(mlp_inner * mlp_unit, -1, keepdims=True)
    )
    attention_low = hidden_grad.astype(jnp.bfloat16)
    heads_grad_rows = nt(attention_low, out_full).astype(jnp.bfloat16)
    heads_grad = jnp.transpose(heads_grad_rows.reshape(rows, 16, CHUNK), (1, 0, 2))
    sums = jnp.concatenate(
        [jnp.zeros((8, 256)), mlp_sum.reshape(8, 256), jnp.broadcast_to(square_tile[0:1, 0:1], (8, 256))], 0
    )
    units = jnp.transpose(attn_unit.reshape(rows, 16, CHUNK), (1, 0, 2))
    attn_grad, ffn_grads, mix_grads, totals = run_exit(
        heads_grad, attention_low, ffn_part, gathered, proj, pos, taps, gain, mix_full, heads, units, sums, saved
    )
    attn_inner = attn_grad * attn_gain
    input_grad = hidden_grad + attn_scale * (
        attn_inner - attn_unit * jnp.mean(attn_inner * attn_unit, -1, keepdims=True)
    )
    loss = totals[16, 0] / (valid * features)
    small_grad = mix_grads[385:398, :16]
    shape = (2, 64, features)
    return (
        output.reshape(shape),
        loss,
        input_grad.reshape(shape),
        totals[:8].reshape(features),
        jnp.transpose(mix_grads[:384]).reshape(256, 3, CHUNK),
        jnp.transpose(mix_grads[384:385]),
        small_grad[:12].reshape(4, 3, 1, 16),
        small_grad[12:].reshape(1, 16),
        mix_grads[400:],
        totals[8:16].reshape(features),
        jnp.transpose(ffn_grads[:hidden_units]),
        jnp.transpose(ffn_grads[HIDDEN : HIDDEN + hidden_units]),
        down_grad[:hidden_units],
    )


def solution(mesh):
    in_specs = (
        P("dp", "tensor", None),
        P("dp", "tensor", None),
        P("dp", None),
        P("dp", "tensor"),
        P(),
        P("dp", None, "tensor"),
        P("dp", "tensor"),
        P(None, None, "tensor", "dp"),
        P("tensor", "dp"),
        P("tensor", "dp"),
        P(),
        P("dp", "tensor"),
        P("dp", "tensor"),
        P("tensor", "dp"),
    )
    out_specs = (
        P("dp", "tensor", None),
        P(),
        P("dp", "tensor", None),
        P(),
        P("dp", None, "tensor"),
        P("dp", "tensor"),
        P(None, None, "tensor", "dp"),
        P("tensor", "dp"),
        P("tensor", "dp"),
        P(),
        P("dp", "tensor"),
        P("dp", "tensor"),
        P("tensor", "dp"),
    )
    return jax.shard_map(body, mesh=mesh, in_specs=in_specs, out_specs=out_specs, check_vma=False)
```

```python
import jax
import jax.numpy as jnp
from jax import lax
from jax.experimental import pallas as pl
from jax.experimental.pallas import tpu as pltpu
from jax.sharding import PartitionSpec as P

MESH = pl.DeviceIdType.MESH
CHUNK = 128
WIDE = 512
PARAMS = pltpu.CompilerParams(vmem_limit_bytes=56 << 20)


def nn(a, b):
    return jnp.dot(a, b, preferred_element_type=jnp.float32)


def nt(a, b):
    return lax.dot_general(a, b, (((1,), (1,)), ((), ())), preferred_element_type=jnp.float32)


def tn(a, b):
    return lax.dot_general(a, b, (((0,), (0,)), ((), ())), preferred_element_type=jnp.float32)


def low(value):
    return value.astype(jnp.bfloat16)


def split(value):
    high = low(value)
    return high, low(value - high.astype(jnp.float32))


def fine(product, a, b):
    a_high, a_rest = a
    b_high, b_rest = b
    return product(a_high, b_high) + (product(a_high, b_rest) + product(a_rest, b_high))


def grid_masks():
    row = lax.broadcasted_iota(jnp.int32, (CHUNK, CHUNK), 0)
    column = lax.broadcasted_iota(jnp.int32, (CHUNK, CHUNK), 1)
    return row, column


def chunk_rows(index, sequence):
    first = pl.multiple_of(index * 256 + sequence * 64, 64)
    second = pl.multiple_of(index * 256 + 128 + sequence * 64, 64)
    return first, second


def load(ref, index, sequence, lanes=slice(None)):
    first, second = chunk_rows(index, sequence)
    return jnp.concatenate([ref[pl.ds(first, 64), lanes], ref[pl.ds(second, 64), lanes]], 0)


def store(ref, index, sequence, value, lanes=slice(None)):
    first, second = chunk_rows(index, sequence)
    ref[pl.ds(first, 64), lanes] = value[:64]
    ref[pl.ds(second, 64), lanes] = value[64:]


def columns_of(pos_ref, index, sequence):
    line = pos_ref[pl.ds(index * 2 + sequence, 1), :]
    return line, jnp.broadcast_to(line, (CHUNK, CHUNK)).T


def convolve(proj_ref, taps_ref, index, sequence, place):
    fields = slice(0, 384)
    current = load(proj_ref, index, sequence, fields)
    before = pl.multiple_of(jnp.maximum(index * 256 - 128 + sequence * 64 + 56, 0), 8)
    window = jnp.concatenate([proj_ref[pl.ds(before, 8), fields], current], 0)
    total = current * taps_ref[0:1, :]
    moved = [current]
    for offset in range(1, 4):
        keep = (place[:, 0:1] >= offset).astype(jnp.float32)
        shifted = window[8 - offset : 8 - offset + CHUNK] * keep
        moved.append(shifted)
        total = total + shifted * taps_ref[offset : offset + 1, :]
    return total, moved


def activate(total):
    sigma = jax.nn.sigmoid(total)
    act = total * sigma
    query, keys, values = act[:, :128], act[:, 128:256], act[:, 256:]
    query_scale = lax.rsqrt(jnp.sum(query * query, -1, keepdims=True) + 1e-06)
    key_scale = lax.rsqrt(jnp.sum(keys * keys, -1, keepdims=True) + 1e-06)
    return sigma, query * query_scale, query_scale, keys * key_scale, key_scale, values


def inverses(mixings, row, column):
    eye = (row == column).astype(jnp.float32)
    pair = (row // 2) == (column // 2)
    totals = [eye - jnp.where(pair, mixing, 0.0) for mixing in mixings]
    size = 2
    while size < CHUNK:
        corner = (
            ((row // (2 * size)) == (column // (2 * size)))
            & (((row // size) % 2) == 1)
            & (((column // size) % 2) == 0)
        )
        corners = [low(jnp.where(corner, mixing, 0.0)) for mixing in mixings]
        helds = [low(total) for total in totals]
        inners = [low(nn(held, part)) for held, part in zip(helds, corners)]
        totals = [total - nn(inner, held) for total, inner, held in zip(totals, inners, helds)]
        size *= 2
    helds = [split(total) for total in totals]
    rests = [
        low(eye - total - fine(nn, split(mixing), held))
        for total, mixing, held in zip(totals, mixings, helds)
    ]
    return [total + nn(held[0], rest) for total, held, rest in zip(totals, helds, rests)]


def mixer_forward(
    proj_ref, pos_ref, taps_ref, gain_ref,
    heads_ref, query_ref, key_ref, inv_ref, kc_ref, score_ref, step_ref, state_ref, update_ref, raw_ref,
    free_ref, shift_ref, which, between,
):
    row, column = grid_masks()
    depth = row - column

    streams = [(index, which) for index in range(8)]

    def prepare():
        lines, queries, keys_all, values_all, betas, withins, carrieds, mixings = ([] for _ in range(8))
        for index, sequence in streams:
            line, place = columns_of(pos_ref, index, sequence)
            total, _ = convolve(proj_ref, taps_ref, index, sequence, place)
            _, query, _, keys, _, values = activate(total)
            lines.append(line[:, 127:128])
            queries.append(low(query * 128 ** (-0.5)))
            keys_all.append(keys)
            values_all.append(low(values))
            betas.append(jax.nn.sigmoid(load(proj_ref, index, sequence, slice(384, 512))))
            withins.append((depth >= 0) & (depth.astype(jnp.float32) <= place))
            carrieds.append(place > row.astype(jnp.float32))
        grams = [fine(nt, split(keys), split(keys * beta)) for keys, beta in zip(keys_all, betas)]
        mixings = [jnp.where(within & (depth > 0), gram, 0.0) for within, gram in zip(withins, grams)]
        solved_all = [low(solved) for solved in inverses(mixings, row, column)]
        boths = [
            nn(solved, jnp.concatenate([low(jnp.where(carried, keys, 0.0)), values], 1))
            for solved, carried, keys, values in zip(solved_all, carrieds, keys_all, values_all)
        ]
        key_lows = [low(keys) for keys in keys_all]
        scores = [nt(query, key_low) for query, key_low in zip(queries, key_lows)]
        weights = [
            jnp.where((127 - row).astype(jnp.float32) <= last, beta, 0.0)
            for last, beta in zip(lines, betas)
        ]
        ends_all = [
            tn(key_low, low(jnp.concatenate([weight, weight], 1) * both))
            for key_low, weight, both in zip(key_lows, weights, boths)
        ]
        for item, (index, sequence) in enumerate(streams):
            block = index * 2 + sequence
            through = jnp.where((row == column) & (lines[item] > 127.0), 1.0, 0.0)
            store(query_ref, index, sequence, queries[item])
            store(key_ref, index, sequence, key_lows[item])
            inv_ref[block] = solved_all[item]
            kc_ref[block] = low(boths[item][:, :128])
            free_ref[block] = boths[item][:, 128:]
            score_ref[block] = low(jnp.where(withins[item], scores[item], 0.0))
            step_ref[block] = low(through - ends_all[item][:, :128])
            shift_ref[block] = ends_all[item][:, 128:]

    prepare()
    between()
    state = jnp.zeros((CHUNK, CHUNK), jnp.float32)
    for index in range(8):
        block = index * 2 + which
        state_low = low(state)
        state_ref[block] = state_low
        state = nn(step_ref[block], state_low) + shift_ref[block]

    def finish():
        blocks = [index * 2 + sequence for index, sequence in streams]
        states = [state_ref[block] for block in blocks]
        recalls = [nn(kc_ref[block], state) for block, state in zip(blocks, states)]
        reads = [nn(load(query_ref, *stream), state) for stream, state in zip(streams, states)]
        updates = [free_ref[block] - recall for block, recall in zip(blocks, recalls)]
        weighted = [
            low(jax.nn.sigmoid(load(proj_ref, *stream, slice(384, 512))) * update)
            for stream, update in zip(streams, updates)
        ]
        mixed = [nn(score_ref[block], weight) for block, weight in zip(blocks, weighted)]
        for item, (index, sequence) in enumerate(streams):
            _, place = columns_of(pos_ref, index, sequence)
            output = jnp.where(place > row.astype(jnp.float32), reads[item], 0.0) + mixed[item]
            scale = lax.rsqrt(jnp.mean(output * output, -1, keepdims=True) + 1e-05)
            update_ref[blocks[item]] = low(updates[item])
            raw_ref[blocks[item]] = output
            store(heads_ref, index, sequence, low(output * scale * gain_ref[0:1, :]))

    finish()


def mixer_backward(
    grad_ref, proj_ref, pos_ref, taps_ref, gain_ref,
    query_ref, key_ref, inv_ref, kc_ref, score_ref, step_ref, state_ref, update_ref, raw_ref,
    out_ref, taps_grad_ref, gain_grad_ref,
    back_ref, pull_ref, flow_ref, enter_ref, pre_ref, which, between, after,
):
    row, column = grid_masks()
    depth = row - column

    def prepare():
        streams = [(index, which) for index in range(8)]
        blocks = [index * 2 + sequence for index, sequence in streams]
        back_lows = []
        for (index, sequence), block in zip(streams, blocks):
            grad = load(grad_ref, index, sequence).astype(jnp.float32)
            output = raw_ref[block]
            scale = lax.rsqrt(jnp.mean(output * output, -1, keepdims=True) + 1e-05)
            unit = output * scale
            inner = grad * gain_ref[0:1, :]
            gain_grad_ref[0:1, :] += jnp.sum(grad * unit, 0, keepdims=True)
            back = scale * (inner - unit * jnp.mean(inner * unit, -1, keepdims=True))
            back_lows.append(low(back))
        pulls = [tn(score_ref[block], back_low) for block, back_low in zip(blocks, back_lows)]
        rights = []
        for (index, sequence), back_low, pull in zip(streams, back_lows, pulls):
            _, place = columns_of(pos_ref, index, sequence)
            carried = place > row.astype(jnp.float32)
            beta = jax.nn.sigmoid(load(proj_ref, index, sequence, slice(384, 512)))
            rights.append(
                jnp.concatenate([jnp.where(carried, back_low, 0.0), low(-beta * pull)], 0)
            )
        enters = [
            tn(jnp.concatenate([load(query_ref, *stream), kc_ref[block]], 0), right)
            for stream, block, right in zip(streams, blocks, rights)
        ]
        for block, back_low, pull, enter in zip(blocks, back_lows, pulls, enters):
            enter_ref[block] = enter
            back_ref[block] = back_low
            pull_ref[block] = pull

    prepare()
    between()
    flow = jnp.zeros((CHUNK, CHUNK), jnp.float32)
    for index in reversed(range(8)):
        block = index * 2 + which
        flow_low = low(flow)
        flow_ref[block] = flow_low
        flow = tn(step_ref[block], flow_low) + enter_ref[block]

    def collect(double, carry):
        streams = [(double * 4 + item, which) for item in range(4)]
        blocks = [index * 2 + sequence for index, sequence in streams]
        lines, places, betas, carrieds, closings = ([] for _ in range(5))
        for index, sequence in streams:
            line, place = columns_of(pos_ref, index, sequence)
            lines.append(line)
            places.append(place)
            betas.append(jax.nn.sigmoid(load(proj_ref, index, sequence, slice(384, 512))))
            carrieds.append(place > row.astype(jnp.float32))
            closings.append((127 - row).astype(jnp.float32) <= line[:, 127:128])
        queries = [load(query_ref, *stream) for stream in streams]
        keys_all = [load(key_ref, *stream) for stream in streams]
        updates = [update_ref[block].astype(jnp.float32) for block in blocks]
        weighted = [beta * update for beta, update in zip(betas, updates)]
        flows = [flow_ref[block] for block in blocks]
        states = [state_ref[block] for block in blocks]
        backs = [back_ref[block] for block in blocks]
        key_flows = [nn(keys, flow) for keys, flow in zip(keys_all, flows)]
        score_grads = [nt(back, low(weight)) for back, weight in zip(backs, weighted)]
        grams = [nt(keys, keys) for keys in keys_all]
        weight_grads = [
            pull_ref[block] + jnp.where(closing, key_flow, 0.0)
            for block, closing, key_flow in zip(blocks, closings, key_flows)
        ]
        right_grads = [
            tn(inv_ref[block], low(beta * weight_grad))
            for block, beta, weight_grad in zip(blocks, betas, weight_grads)
        ]
        score_lows = [
            low(jnp.where((depth >= 0) & (depth.astype(jnp.float32) <= place), score_grad, 0.0))
            for place, score_grad in zip(places, score_grads)
        ]
        query_grads = [
            nt(jnp.where(carried, back, 0.0), state) + nn(score_low, keys)
            for carried, back, state, score_low, keys in zip(
                carrieds, backs, states, score_lows, keys_all
            )
        ]
        mixing_grads = [
            jnp.where((depth < 0) & ((-depth).astype(jnp.float32) <= line), -nt(low(update), low(right_grad)), 0.0)
            for line, update, right_grad in zip(lines, updates, right_grads)
        ]
        gram_lows = [low(beta * mixing_grad) for beta, mixing_grad in zip(betas, mixing_grads)]
        key_grads = [
            nt(
                jnp.concatenate(
                    [low(jnp.where(closing, weight, 0.0)), low(jnp.where(carried, -right_grad, 0.0))], 1
                ),
                jnp.concatenate([flow, state], 1),
            )
            for closing, weight, carried, right_grad, flow, state in zip(
                closings, weighted, carrieds, right_grads, flows, states
            )
        ]
        key_grads = [
            key_grad
            + tn(jnp.concatenate([score_low, gram_low], 0), jnp.concatenate([query, keys], 0))
            + nn(gram_low, keys)
            for key_grad, score_low, gram_low, query, keys in zip(
                key_grads, score_lows, gram_lows, queries, keys_all
            )
        ]
        for item, (index, sequence) in enumerate(streams):
            total, moved = convolve(proj_ref, taps_ref, index, sequence, places[item])
            sigma, query, query_scale, keys, key_scale, _ = activate(total)
            beta = betas[item]
            beta_grad = jnp.sum(
                weight_grads[item] * updates[item] + mixing_grads[item] * grams[item], -1, keepdims=True
            )
            query_grad = query_grads[item] * 128 ** (-0.5)
            query_act = query_scale * (
                query_grad - query * jnp.sum(query * query_grad, -1, keepdims=True)
            )
            key_act = key_scale * (
                key_grads[item] - keys * jnp.sum(keys * key_grads[item], -1, keepdims=True)
            )
            act_grad = jnp.concatenate([query_act, key_act, right_grads[item]], 1)
            pre_grad = act_grad * (sigma * (1.0 + total * (1.0 - sigma)))
            for offset in range(4):
                taps_grad_ref[offset : offset + 1, :] += jnp.sum(
                    pre_grad * moved[offset], 0, keepdims=True
                )
            pre_ref[pl.ds(pl.multiple_of(index * CHUNK, CHUNK), CHUNK), :] = pre_grad
            logit_grad = jnp.where(column == 0, beta_grad * beta * (1.0 - beta), 0.0)
            store(out_ref, index, sequence, low(logit_grad), slice(384, 512))
        return carry

    lax.fori_loop(0, 2, collect, 0)
    after()

    def spread(pair_index, carry):
        for item in range(2):
            index, sequence = pair_index * 2 + item, which
            after = pl.multiple_of(jnp.minimum(index * CHUNK + CHUNK, 896), CHUNK)
            live = jnp.where(index == 7, 0.0, 1.0)
            current = pre_ref[pl.ds(pl.multiple_of(index * CHUNK, CHUNK), CHUNK), :]
            window = jnp.concatenate([current, pre_ref[pl.ds(after, 8), :] * live], 0)
            _, place = columns_of(pos_ref, index, sequence)
            _, follow = columns_of(pos_ref, jnp.minimum(index + 1, 7), sequence)
            places = jnp.concatenate([place, follow[0:8]], 0)[:, 0:1]
            total = current * taps_ref[0:1, :]
            for offset in range(1, 4):
                masked = window * (places >= offset).astype(jnp.float32)
                total = total + masked[offset : offset + CHUNK] * taps_ref[offset : offset + 1, :]
            store(out_ref, index, sequence, low(total), slice(0, 384))
        return carry

    lax.fori_loop(0, 4, spread, 0)


def saved_shapes():
    rows = jax.ShapeDtypeStruct((2048, CHUNK), jnp.bfloat16)
    small = jax.ShapeDtypeStruct((16, CHUNK, CHUNK), jnp.bfloat16)
    wide = jax.ShapeDtypeStruct((16, CHUNK, CHUNK), jnp.float32)
    return (rows, rows, small, small, small, small, small, small, wide)


def spot(y, z, core):
    return (y * 2 + z) * 2 + core


class Neighbours:
    def __init__(self):
        index = lax.axis_index("tensor")
        self.core = index % 2
        self.z = (index // 2) % 2
        self.y = index // 4
        up, down, far = (self.y + 1) % 4, (self.y + 3) % 4, (self.y + 2) % 4
        other = 1 - self.z
        self.up = spot(up, self.z, self.core)
        self.down = spot(down, self.z, self.core)
        self.side = spot(self.y, other, self.core)
        self.twin = spot(self.y, self.z, 1 - self.core)
        self.chips = {
            "own": self.y * 2 + self.z,
            "side": self.y * 2 + other,
            "down": down * 2 + self.z,
            "up": up * 2 + self.z,
            "downside": down * 2 + other,
            "upside": up * 2 + other,
            "far": far * 2 + self.z,
            "farside": far * 2 + other,
        }

    def mine(self, name):
        return self.chips[name] * 2 + self.core

    def twins(self, name):
        return self.chips[name] * 2 + 1 - self.core

    def quarter_at(self, step):
        quarter = step % 4
        shift = quarter + quarter // 2 - 2 * (quarter // 3)
        return (self.y + shift) % 4


def greet(devices):
    barrier = pltpu.get_barrier_semaphore()
    for device in devices:
        pl.semaphore_signal(barrier, inc=1, device_id=device, device_id_type=MESH)
    pl.semaphore_wait(barrier, len(devices))


def remote(source, target, send_sem, recv_sem, device):
    return pltpu.make_async_remote_copy(
        src_ref=source, dst_ref=target, send_sem=send_sem, recv_sem=recv_sem,
        device_id=device, device_id_type=MESH,
    )


NAMES = ("own", "side", "down", "up", "downside", "upside", "far", "farside")
ORDER = (("own", "side"), ("up", "upside"), ("down", "downside"), ("far", "farside"))


class Rows:
    def __init__(self, first, count):
        self.first, self.count = first, count
        self.whole = pl.ds(first, count)
        self.top = pl.ds(first, count // 2)
        self.bottom = pl.ds(first + count // 2, count // 2)


ALL, HALVES = Rows(0, 128), (Rows(0, 64), Rows(64, 64))


class Gather:
    copies = 17

    def __init__(self, near, buffer, sends, receives, rows=ALL):
        self.near, self.buffer, self.sends, self.receives = near, buffer, sends, receives
        self.rows = rows

    def piece(self, key, name):
        rows = self.rows
        part = {5: rows.top, 6: rows.bottom, 7: rows.top, 8: rows.bottom}.get(key, rows.whole)
        return self.buffer.at[self.near.mine(name), part]

    def copy(self, key, piece, device):
        return remote(piece, piece, self.sends.at[key], self.receives.at[key], {"tensor": device})

    def send(self, key, name, device):
        self.copy(key, self.piece(key, name), device).start()

    def arrive(self, key, name):
        self.copy(key, self.piece(key, name), self.near.twin).wait_recv()

    def to_twin(self, name):
        self.send(9 + NAMES.index(name), name, self.near.twin)

    def from_twin(self, *names):
        for name in names:
            piece = self.buffer.at[self.near.twins(name), self.rows.whole]
            self.copy(9 + NAMES.index(name), piece, self.near.twin).wait_recv()

    def start(self):
        near = self.near
        self.send(1, "own", near.up)
        self.send(2, "own", near.down)
        self.send(0, "own", near.side)
        self.to_twin("own")

    def from_down(self):
        self.arrive(1, "down")
        self.send(5, "down", self.near.up)
        self.to_twin("down")

    def from_up(self):
        self.arrive(2, "up")
        self.send(6, "up", self.near.down)
        self.to_twin("up")

    def from_side(self):
        self.arrive(0, "side")
        self.send(3, "side", self.near.up)
        self.send(4, "side", self.near.down)
        self.to_twin("side")

    def second(self):
        self.from_down()
        self.from_up()
        self.from_side()

    def third(self):
        self.arrive(5, "far")
        self.send(7, "far", self.near.side)
        self.arrive(6, "far")
        self.send(8, "far", self.near.side)
        self.to_twin("far")

    def fourth(self):
        self.arrive(4, "upside")
        self.to_twin("upside")
        self.arrive(3, "downside")
        self.to_twin("downside")

    def fifth(self):
        self.arrive(7, "farside")
        self.arrive(8, "farside")
        self.to_twin("farside")

    def finish(self):
        names = ("own", "own", "own", "side", "side", "down", "up", "far", "far") + NAMES
        for key, name in enumerate(names):
            self.copy(key, self.piece(key, name), self.near.twin).wait_send()


def add_rows(target, sources, count=128):
    def piece(index, carry):
        rows = pl.ds(pl.multiple_of(index * 16, 16), 16)
        total = target[rows].astype(jnp.float32)
        for source in sources:
            total = total + source[rows].astype(jnp.float32)
        target[rows] = total.astype(target.dtype)
        return carry

    lax.fori_loop(0, count // 16, piece, 0)


class Scatter:
    copies = 16

    def __init__(self, near, part, twin_part, slot, sends, receives, rows=ALL):
        self.near, self.part, self.twin_part, self.slot = near, part, twin_part, slot
        self.sends, self.receives, self.rows = sends, receives, rows

    def describe(self, key, source, target, device):
        return remote(source, target, self.sends.at[key], self.receives.at[key], {"tensor": device})

    def twin_copy(self, chip):
        whole = self.rows.whole
        return self.describe(
            8 + chip, self.part.at[chip * 2 + 1 - self.near.core, whole],
            self.twin_part.at[chip, whole], self.near.twin,
        )

    def to_twin(self, chip):
        self.twin_copy(chip).start()

    def mine(self, name, rows=None):
        return self.part.at[self.near.mine(name), self.rows.whole if rows is None else rows]

    def chip_sum(self, name):
        chip = self.near.chips[name]
        self.twin_copy(chip).wait_recv()
        add_rows(self.mine(name), [self.twin_part.at[chip, self.rows.whole]], self.rows.count)

    def outgoing(self, key):
        near, slot, rows = self.near, self.slot, self.rows
        name, place, part, device = (
            ("farside", 0, rows.whole, near.side),
            ("far", 1, rows.top, near.down),
            ("far", 1, rows.bottom, near.up),
            ("downside", 2, rows.whole, near.down),
            ("upside", 3, rows.whole, near.up),
            ("down", 4, rows.whole, near.down),
            ("up", 5, rows.whole, near.up),
            ("side", 6, rows.whole, near.side),
        )[key]
        return self.describe(key, self.mine(name, part), slot.at[place, part], device)

    def send(self, key):
        self.outgoing(key).start()

    def arrive(self, key):
        self.outgoing(key).wait_recv()

    def sums(self, *names):
        for name in names:
            self.chip_sum(name)
            key = {"farside": 0, "downside": 3, "upside": 4}.get(name)
            if key is not None:
                self.send(key)

    def first(self):
        self.sums("farside", "downside", "upside", "far", "down", "up", "side")

    def second(self):
        self.arrive(0)
        add_rows(self.mine("far"), [self.slot.at[0, self.rows.whole]], self.rows.count)
        self.send(1)
        self.send(2)

    def to_side(self):
        slot, rows = self.slot, self.rows
        self.arrive(3)
        self.arrive(4)
        add_rows(self.mine("side"), [slot.at[2, rows.whole], slot.at[3, rows.whole]], rows.count)
        self.send(7)

    def to_down(self):
        rows = self.rows
        self.arrive(1)
        add_rows(self.mine("down", rows.top), [self.slot.at[1, rows.top]], rows.count // 2)
        self.send(5)

    def to_up(self):
        rows = self.rows
        self.arrive(2)
        add_rows(self.mine("up", rows.bottom), [self.slot.at[1, rows.bottom]], rows.count // 2)
        self.send(6)

    def third(self):
        self.to_side()
        self.to_down()
        self.to_up()

    def fourth(self):
        self.twin_copy(self.near.chips["own"]).wait_recv()
        for key in (7, 5, 6):
            self.arrive(key)

    def total(self, rows):
        chip = self.near.chips["own"]
        value = self.part[chip * 2 + self.near.core, rows].astype(jnp.float32)
        value = value + self.twin_part[chip, rows].astype(jnp.float32)
        for place in (4, 5, 6):
            value = value + self.slot[place, rows].astype(jnp.float32)
        return value

    def finish(self):
        for chip in range(8):
            self.twin_copy(chip).wait_send()
        for key in range(8):
            self.outgoing(key).wait_send()


def strips(count, body, start=0):
    def piece(index, carry):
        return body(pl.ds(pl.multiple_of(start + index * 16, 16), 16), carry)

    return lambda carry: lax.fori_loop(0, count // 16, piece, carry)


def normalise(values):
    scale = lax.rsqrt(jnp.mean(values * values, -1, keepdims=True) + 1e-06)
    return values * scale, scale


def norm_into(source, gain_ref, target):
    def strip(rows, carry):
        unit, _ = normalise(source[rows].astype(jnp.float32))
        target[rows] = low(unit * gain_ref[0:1, :])
        return carry

    strips(128, strip)(0)


def norm_back(values, unit, scale, gain_ref):
    inner = values * gain_ref[0:1, :]
    return scale * (inner - unit * jnp.mean(inner * unit, -1, keepdims=True))


def at_steps(step, table):
    for moment, actions in table.items():

        @pl.when(step == moment)
        def _(actions=actions):
            for action in actions:
                action()


def pair(items, names):
    return lambda: items.from_twin(*names)


def summing(items, *names):
    return lambda: items.sums(*names)


HIDDEN = 384
FF_UNITS = 352


def sigmoid(value):
    return 1.0 / (1.0 + jnp.exp(-value))


def rows_of(half, quarter):
    return pl.ds(pl.multiple_of(half * 1024 + quarter * 256, 256), 256)


def half_of(half):
    return pl.ds(pl.multiple_of(half * 64, 64), 64)


def quarter_rows(buffer, half, quarter):
    return buffer[pl.ds(quarter * 4, 4), half_of(half)].reshape(256, buffer.shape[2])


def lanes(block):
    return pl.ds(pl.multiple_of(block * 256, 256), 256)


def token_column(buffer, block):
    first = buffer[:, 0:64, lanes(block)].reshape(1024, 256)
    return jnp.concatenate([first, buffer[:, 64:128, lanes(block)].reshape(1024, 256)], 0)


def scatter_quarter(scatters, half, quarter, partial, part):
    part[pl.ds(quarter * 4, 4), half_of(half)] = partial.reshape(4, 64, partial.shape[1])
    for index, scatter in enumerate(scatters):

        @pl.when(half == index)
        def _(scatter=scatter):
            scatter.to_twin(quarter * 2)
            scatter.to_twin(quarter * 2 + 1)


def ffn_kernel(
    hidden_ref, mlp_gain_ref, teacher_ref, mask_ref, gate_up_src, down_shard_ref,
    block_ref, back_ref, back_low_ref, sums_ref, weight_ref, down_grad_ref,
    tokens, grads, both, act_t, both_t, part, twin_part, slot, down_ref, down_part, down_slot, down_staged,
    grad_ref, square_ref, gain_sum, gate_up_ref, local,
    down_send, down_recv, leave_send, leave_recv, *sems,
):
    near = Neighbours()
    data = lax.axis_index("dp")
    neighbours = [{"tensor": device} for device in (near.up, near.down, near.side, near.twin)]
    neighbours = neighbours + [{"dp": device} for device in data_neighbours()]
    own = near.mine("own")
    norm_into(hidden_ref, mlp_gain_ref, tokens.at[own])
    fills = [
        pltpu.make_async_copy(
            gate_up_src.at[index * FF_UNITS : index * FF_UNITS + FF_UNITS],
            gate_up_ref.at[index * HIDDEN : index * HIDDEN + FF_UNITS], local.at[index],
        )
        for index in range(2)
    ]
    for fill in fills:
        fill.start()
    blank = jnp.zeros((HIDDEN - FF_UNITS, 2048), jnp.bfloat16)
    gate_up_ref[FF_UNITS:HIDDEN] = blank
    gate_up_ref[HIDDEN + FF_UNITS : 2 * HIDDEN] = blank
    down_ref[FF_UNITS:HIDDEN] = blank
    down_ref[0:FF_UNITS, lanes(data)] = down_shard_ref[...]
    greet(neighbours)
    a, g = (
        [Gather(near, buffer, sems[k + 2 * h], sems[k + 2 * h + 1], HALVES[h]) for h in range(2)]
        for buffer, k in ((tokens, 0), (grads, 4))
    )
    r, b = (
        [Scatter(near, part, twin_part, slot, sems[k + 2 * h], sems[k + 2 * h + 1], HALVES[h]) for h in range(2)]
        for k in (8, 12)
    )
    a[0].start()
    down = DataGather(down_shard_ref, lambda block: down_ref.at[0:FF_UNITS, lanes(block)], down_send, down_recv)
    down.start()
    for fill in fills:
        fill.wait()

    def forward(step, carry):
        at_steps(step, {
            0: [a[0].second, a[1].start, down.relay, a[0].third, a[1].from_side, a[0].fourth, down.arrive, pair(a[0], ORDER[0])],
            1: [pair(a[0], ORDER[1])],
            2: [a[0].fifth, summing(r[0], "side"), pair(a[0], ORDER[2])],
            3: [summing(r[0], "up", "upside"), a[1].from_down, a[1].from_up, pair(a[0], ORDER[3])],
            4: [summing(r[0], "downside", "down"), a[1].fourth, pair(a[1], ORDER[0])],
            5: [summing(r[0], "farside", "far"), pair(a[1], ORDER[1])],
            6: [summing(r[1], "side"), a[1].third, r[0].to_side, pair(a[1], ORDER[2])],
            7: [
                summing(r[1], "upside"), r[0].second, summing(r[1], "up", "down", "downside"), r[0].to_down,
                a[1].fifth, pair(a[1], ORDER[3]),
            ],
        })
        half, quarter = step // 4, near.quarter_at(step)
        rows = rows_of(half, quarter)
        product = nt(quarter_rows(tokens, half, quarter), gate_up_ref[...])
        both[rows, :] = product
        gate, up = product[:, :HIDDEN], product[:, HIDDEN:]
        act = low(gate * sigmoid(gate) * up)
        act_t[:, rows] = act.T
        scatter_quarter(r, half, quarter, low(nn(act, down_ref[...])), part)
        return carry

    lax.fori_loop(0, 8, forward, 0)
    square_ref[...] = jnp.zeros_like(square_ref)
    gain_sum[...] = jnp.zeros_like(gain_sum)

    def middle(half):
        def piece(index, carry):
            rows = pl.ds(pl.multiple_of(half * 64 + index * 16, 16), 16)
            output = hidden_ref[rows] + r[half].total(rows)
            block_ref[rows] = low(output)
            diff = output - teacher_ref[rows].astype(jnp.float32)
            weight = mask_ref[0, rows, 0:1]
            grad = mask_ref[1, rows, 0:1] * diff
            grad_ref[rows] = grad
            grads[own, rows] = low(grad)
            squares = jnp.sum(weight * jnp.sum(diff * diff, -1, keepdims=True), 0, keepdims=True)
            square_ref[...] += jnp.broadcast_to(squares, (8, 128))
            return carry

        lax.fori_loop(0, 4, piece, 0)

    r[0].to_up()
    r[1].to_side()
    r[1].sums("far", "farside")
    r[0].fourth()
    middle(0)
    g[0].start()
    r[1].second()
    g[0].from_down()
    g[0].from_up()
    r[1].to_down()
    r[1].to_up()
    g[0].from_side()
    g[0].third()
    r[0].finish()

    def turn():
        r[1].fourth()
        middle(1)
        r[1].finish()

    def backward(step, carry):
        at_steps(step, {
            0: [pair(g[0], ORDER[0])],
            1: [turn, summing(b[0], "side"), g[1].start, g[0].fifth, g[0].fourth, pair(g[0], ORDER[1])],
            2: [g[1].second, pair(g[0], ORDER[2])],
            3: [summing(b[0], "upside", "up"), pair(g[0], ORDER[3])],
            4: [summing(b[0], "downside", "down"), g[1].third, pair(g[1], ORDER[0])],
            5: [summing(b[0], "farside", "far"), g[1].fourth, summing(b[1], "side"), pair(g[1], ORDER[1])],
            6: [b[0].to_side, g[1].fifth, pair(g[1], ORDER[2])],
            7: [b[0].second, summing(b[1], "upside", "up"), pair(g[1], ORDER[3])],
        })
        half, quarter = step // 4, near.quarter_at(step)
        rows = rows_of(half, quarter)
        act_grad = nt(quarter_rows(grads, half, quarter), down_ref[...])
        gate, up = both[rows, :HIDDEN], both[rows, HIDDEN:]
        sigma = sigmoid(gate)
        gate_low = low(act_grad * up * sigma * (1.0 + gate * (1.0 - sigma)))
        up_low = low(act_grad * gate * sigma)
        both_low = jnp.concatenate([gate_low, up_low], 1)
        both_t[:, rows] = both_low.T
        scatter_quarter(b, half, quarter, low(nn(both_low, gate_up_ref[...])), part)
        return carry

    lax.fori_loop(0, 8, backward, 0)
    b[1].sums("downside", "down")
    b[0].to_down()
    b[0].to_up()

    def down_weights(step, carry):
        at_steps(step, {2: [summing(b[1], "far", "farside")]})
        down_part[:, lanes(step)] = low(nn(act_t[...], token_column(grads, step)))
        return carry

    lax.fori_loop(0, 8, down_weights, 0)
    place = DataPlace()
    leave = DataScatter(
        lambda block: down_part.at[:, lanes(block)],
        lambda other, rows: down_part[rows, lanes(place.block(0, other))],
        down_slot, down_staged, leave_send, leave_recv,
    )
    leave.start()

    def ending(half):
        b[half].fourth()

        def piece(index, carry):
            rows = pl.ds(pl.multiple_of(half * 64 + index * 16, 16), 16)
            value = b[half].total(rows)
            unit, scale = normalise(hidden_ref[rows])
            gain_sum[...] += value * unit
            grad = grad_ref[rows] + norm_back(value, unit, scale, mlp_gain_ref)
            back_ref[rows] = grad
            back_low_ref[rows] = low(grad)
            return carry

        lax.fori_loop(0, 4, piece, 0)

    def weights(step, carry):
        at_steps(step, {3: [b[1].to_side], 7: [b[1].second]})
        weight_ref[:, lanes(step)] = low(nn(both_t[...], token_column(tokens, step)))
        return carry

    lax.fori_loop(0, 8, weights, 0)
    ending(0)
    b[1].to_down()
    b[1].to_up()
    leave.relay()
    ending(1)
    total = jnp.sum(gain_sum[...], 0, keepdims=True)
    sums_ref[0:8, :] = jnp.zeros((8, 256), jnp.float32)
    for piece in range(8):
        sums_ref[8 + piece : 9 + piece, :] = total[:, piece * 256 : piece * 256 + 256]
    sums_ref[16:24, :] = jnp.concatenate([square_ref[...], square_ref[...]], 1)
    leave.result(down_grad_ref)
    for item in (down, leave, a[0], a[1], g[0], g[1], b[0], b[1]):
        item.finish()


def data_neighbours():
    place = DataPlace()
    return [place.block(shift, 0) for shift in range(1, 4)] + [place.block(0, 1)]


def run_ffn(hidden, gain, teacher, mask, gate_up, down_shard):
    rows, features = hidden.shape
    wide = jax.ShapeDtypeStruct((rows, features), jnp.float32)
    vmem = pl.BlockSpec(memory_space=pltpu.VMEM)
    counts = [7] * 4 + [Gather.copies] * 8 + [Scatter.copies] * 8
    semaphores = [pltpu.SemaphoreType.DMA((count,)) for count in counts]
    return pl.pallas_call(
        ffn_kernel,
        out_shape=(
            jax.ShapeDtypeStruct((rows, features), jnp.bfloat16),
            wide,
            jax.ShapeDtypeStruct((rows, features), jnp.bfloat16),
            jax.ShapeDtypeStruct((24, 256), jnp.float32),
            jax.ShapeDtypeStruct((2 * HIDDEN, features), jnp.bfloat16),
            jax.ShapeDtypeStruct((HIDDEN, 256), jnp.float32),
        ),
        in_specs=[vmem] * 4 + [pl.BlockSpec(memory_space=pl.ANY), vmem],
        out_specs=[vmem] * 6,
        scratch_shapes=[
            pltpu.VMEM((16, 128, 2048), jnp.bfloat16),
            pltpu.VMEM((16, 128, 2048), jnp.bfloat16),
            pltpu.VMEM((2048, 2 * HIDDEN), jnp.float32),
            pltpu.VMEM((HIDDEN, 2048), jnp.bfloat16),
            pltpu.VMEM((2 * HIDDEN, 2048), jnp.bfloat16),
            pltpu.VMEM((16, 128, 2048), jnp.bfloat16),
            pltpu.VMEM((8, 128, 2048), jnp.bfloat16),
            pltpu.VMEM((7, 128, 2048), jnp.bfloat16),
            pltpu.VMEM((HIDDEN, 2048), jnp.bfloat16),
            pltpu.VMEM((HIDDEN, 2048), jnp.bfloat16),
            pltpu.VMEM((7, HIDDEN, 256), jnp.bfloat16),
            pltpu.VMEM((HIDDEN, 256), jnp.bfloat16),
            pltpu.VMEM((128, 2048), jnp.float32),
            pltpu.VMEM((8, 128), jnp.float32),
            pltpu.VMEM((16, 2048), jnp.float32),
            pltpu.VMEM((2 * HIDDEN, 2048), jnp.bfloat16),
            pltpu.SemaphoreType.DMA((2,)),
        ]
        + semaphores,
        compiler_params=pltpu.CompilerParams(
            collective_id=1, has_side_effects=True, vmem_limit_bytes=63 << 20
        ),
        cost_estimate=pl.CostEstimate(flops=160 << 30, bytes_accessed=16 << 20, transcendentals=0),
        name="feed_forward",
    )(hidden, gain, teacher, mask, gate_up, down_shard)


def everyone():
    tensor, data = lax.axis_index("tensor"), lax.axis_index("dp")
    devices = [{"tensor": (tensor + shift) % 16} for shift in range(1, 16)]
    return devices + [{"dp": (data + shift) % 8} for shift in range(1, 8)]


class Fan:
    def __init__(self, axis, count, source, target, sends, receives):
        self.axis, self.count, self.source, self.target = axis, count, source, target
        self.sends, self.receives = sends, receives
        self.index = lax.axis_index(axis)

    def copy(self, shift):
        peer = (self.index + shift) % self.count
        return remote(
            self.source(peer), self.target(self.index), self.sends.at[shift],
            self.receives.at[shift], {self.axis: peer},
        )

    def start(self):
        for shift in range(1, self.count):
            self.copy(shift).start()

    def arrive(self):
        for shift in range(1, self.count):
            piece = self.target((self.index + self.count - shift) % self.count)
            peer = (self.index + shift) % self.count
            remote(
                piece, piece, self.sends.at[shift], self.receives.at[shift], {self.axis: peer}
            ).wait_recv()

    def finish(self):
        for shift in range(1, self.count):
            self.copy(shift).wait_send()


class DataPlace:
    def __init__(self):
        index = lax.axis_index("dp")
        self.x, self.z = index % 4, index // 4

    def block(self, shift, other):
        return ((self.z + other) % 2) * 4 + (self.x + shift) % 4


class DataGather:
    copies = 7

    def __init__(self, source, target, sends, receives):
        self.place = DataPlace()
        self.source, self.target, self.sends, self.receives = source, target, sends, receives

    def describe(self, key):
        place = self.place
        if key == 0:
            return self.copy(key, self.source, place.block(0, 0), place.block(0, 1))
        if key < 4:
            return self.copy(key, self.source, place.block(0, 0), place.block(key, 0))
        partner = place.block(0, 1)
        return self.copy(key, self.target(partner), partner, place.block(key - 3, 0))

    def copy(self, key, source, block, peer):
        return remote(
            source, self.target(block), self.sends.at[key], self.receives.at[key], {"dp": peer}
        )

    def start(self):
        for key in range(4):
            self.describe(key).start()

    def wait(self, key, block):
        piece = self.target(block)
        self.copy(key, piece, block, self.place.block(0, 1)).wait_recv()

    def relay(self):
        self.wait(0, self.place.block(0, 1))
        for key in range(4, 7):
            self.describe(key).start()

    def arrive(self):
        for shift in range(1, 4):
            self.wait(shift, self.place.block(4 - shift, 0))
            self.wait(3 + shift, self.place.block(4 - shift, 1))

    def finish(self):
        for key in range(7):
            self.describe(key).wait_send()


class DataScatter:
    copies = 7

    def __init__(self, part, own, slot, staged, sends, receives):
        self.place = DataPlace()
        self.part, self.own, self.slot, self.staged = part, own, slot, staged
        self.sends, self.receives = sends, receives

    def describe(self, key):
        place = self.place
        if key == 6:
            source, peer = self.staged, place.block(0, 1)
        else:
            shift, other = key // 2 + 1, key % 2
            source, peer = self.part(place.block(shift, other)), place.block(shift, 0)
        return remote(
            source, self.slot.at[key], self.sends.at[key], self.receives.at[key], {"dp": peer}
        )

    def start(self):
        for key in range(6):
            self.describe(key).start()

    def summed(self, other, rows, extra):
        total = self.own(other, rows).astype(jnp.float32)
        for key in range(other, 6, 2):
            total = total + self.slot[key, rows].astype(jnp.float32)
        if extra:
            total = total + self.slot[6, rows].astype(jnp.float32)
        return total

    def relay(self):
        for key in (1, 3, 5):
            self.describe(key).wait_recv()

        def piece(index, carry):
            rows = pl.ds(pl.multiple_of(index * 16, 16), 16)
            self.staged[rows] = low(self.summed(1, rows, False))
            return carry

        lax.fori_loop(0, self.staged.shape[0] // 16, piece, 0)
        self.describe(6).start()

    def result(self, output):
        for key in (0, 2, 4, 6):
            self.describe(key).wait_recv()

        def piece(index, carry):
            rows = pl.ds(pl.multiple_of(index * 16, 16), 16)
            output[rows] = self.summed(0, rows, True)
            return carry

        lax.fori_loop(0, self.staged.shape[0] // 16, piece, 0)

    def finish(self):
        for key in range(7):
            self.describe(key).wait_send()


def tile_sum(first, second, axes, sems):
    tensor, data = lax.axis_index("tensor"), lax.axis_index("dp")
    one = Fan("tensor", 16, lambda peer: first.at[tensor], lambda index: first.at[index], sems[0], sems[1])
    two = Fan("dp", 8, lambda peer: second.at[data], lambda index: second.at[index], sems[2], sems[3])
    return one, two


def entry_kernel(
    input_ref, attn_gain_ref, mix_ref, small_ref, count_ref, pos_ref, gate_ref, up_ref, out_ref,
    gathered_ref, taps_ref, gain_ref, total_ref, gate_up_full_ref, out_full_ref, spread_ref,
    far0, far1, far2, far3, far4, far5, far6, far7, far8, far9, far10, far11,
    proj_ref, mix_full_ref, heads_ref,
    query_ref, key_ref, inv_ref, kc_ref, score_ref, step_ref, state_ref, update_ref, raw_ref, save_sems, mix_parts,
    tokens, small, counts, count_rows, free_ref, shift_ref,
    mix_send, mix_recv, wide_send, wide_recv, small_send, small_recv,
    out_send, out_recv, all_send, all_recv, count_send, count_recv, row_send, row_recv, local, *sems,
):
    near = Neighbours()
    tensor, data = lax.axis_index("tensor"), lax.axis_index("dp")
    own = near.mine("own")
    block_rows = pl.ds(pl.multiple_of(data * 256, 256), 256)

    def mix_rows(block):
        return mix_parts.at[:, pl.ds(pl.multiple_of(block * 256, 256), 256)]

    def gate_lanes(block):
        return gate_up_full_ref.at[0:FF_UNITS, pl.ds(pl.multiple_of(block * 256, 256), 256)]

    def up_lanes(block):
        return gate_up_full_ref.at[FF_UNITS : 2 * FF_UNITS, pl.ds(pl.multiple_of(block * 256, 256), 256)]

    def lanes_of_data(block):
        return out_full_ref.at[tensor, :, pl.ds(pl.multiple_of(block * 256, 256), 256)]

    gate_own = pltpu.make_async_copy(gate_ref, gate_lanes(data), local.at[0])
    up_own = pltpu.make_async_copy(up_ref, up_lanes(data), local.at[3])
    out_own = pltpu.make_async_copy(out_ref, lanes_of_data(data), local.at[1])
    gate_own.start()
    up_own.start()
    out_own.start()
    norm_into(input_ref, attn_gain_ref, tokens.at[own])
    mix_parts[:, block_rows] = mix_ref[...]
    small[data] = small_ref[...]
    counts[tensor] = count_ref[...]
    greet(everyone())
    a = [Gather(near, tokens, sems[2 * h], sems[2 * h + 1], HALVES[h]) for h in range(2)]
    mix = DataGather(mix_ref, mix_rows, mix_send, mix_recv)
    wide = DataGather(gate_ref, gate_lanes, wide_send, wide_recv)
    wide_up = DataGather(up_ref, up_lanes, sems[8], sems[9])
    tiny = Fan("dp", 8, lambda peer: small.at[data], lambda index: small.at[index], small_send, small_recv)
    outs = Fan("dp", 8, lambda peer: out_ref, lanes_of_data, out_send, out_recv)
    one, two = tile_sum(counts, count_rows, None, (count_send, count_recv, row_send, row_recv))
    everything = Gather(near, out_full_ref, all_send, all_recv)
    a[0].start()
    outs.start()
    tiny.start()
    mix.start()
    one.start()

    def counted():
        one.arrive()
        count_rows[data] = jnp.sum(counts[...], 0)
        two.start()

    def outer():
        out_own.wait()
        outs.arrive()
        everything.start()

    def ready():
        tiny.arrive()
        two.arrive()
        total_ref[...] = jnp.sum(count_rows[...], 0)
        table = jnp.sum(small[:, 0:16].astype(jnp.float32), 0)
        for block in range(8):
            for part in range(2):
                line = small[block, 16:32].astype(jnp.float32)[part : part + 1]
                first = block * 256 + part * 128
                mix_full_ref[first : first + 128, 384:512] = low(jnp.broadcast_to(line, (128, 128)).T)
        for tap in range(4):
            for field in range(3):
                row = tap * 3 + field
                taps_ref[tap : tap + 1, field * 128 : field * 128 + 128] = table[row : row + 1]
        gain_ref[0:1, :] = table[12:13]

    def head_rows(half):
        def place(block):
            return heads_ref.at[pl.ds(pl.multiple_of(block * 128 + half * 64, 64), 64)]

        return place

    def target_rows(half):
        return lambda index: spread_ref.at[index, HALVES[half].whole]

    exchanges = [
        Fan("tensor", 16, head_rows(h), target_rows(h), sems[4 + 2 * h], sems[5 + 2 * h]) for h in range(2)
    ]
    keep = pltpu.make_async_copy(tokens, gathered_ref, local.at[2])
    saves = [
        pltpu.make_async_copy(source, target, save_sems.at[index])
        for index, (source, target) in enumerate(zip(
            (
                proj_ref, mix_full_ref, heads_ref, query_ref, key_ref, inv_ref, kc_ref, score_ref, step_ref,
                state_ref, update_ref, raw_ref,
            ),
            (far0, far1, far2, far3, far4, far5, far6, far7, far8, far9, far10, far11),
        ))
    ]
    a[0].second()
    a[1].start()
    outer()
    counted()
    mix.relay()
    a[0].third()
    a[0].fourth()
    ready()
    a[1].second()
    a[0].fifth()
    mix.arrive()
    wide.start()
    wide_up.start()
    for field in range(3):
        mix_full_ref[:, field * 128 : field * 128 + 128] = mix_parts[field]

    def per_sequence(sequence, carry):
        def project(step, inner):
            at_steps(sequence * 4 + step, {
                0: [pair(a[0], ORDER[0])],
                1: [pair(a[0], ORDER[1])],
                2: [pair(a[0], ORDER[2])],
                3: [a[1].third, pair(a[0], ORDER[3])],
                4: [pair(a[1], ORDER[0])],
                5: [pair(a[1], ORDER[1])],
                6: [pair(a[1], ORDER[2])],
                7: [pair(a[1], ORDER[3]), keep.start, saves[1].start],
            })
            quarter = near.quarter_at(step)
            product = nn(quarter_rows(tokens, sequence, quarter), mix_full_ref[...])
            for item in range(4):
                rows = pl.ds(pl.multiple_of((quarter * 4 + item) * 128 + sequence * 64, 64), 64)
                proj_ref[rows, :] = product[item * 64 : item * 64 + 64]
            return inner

        lax.fori_loop(0, 4, project, 0)
        mixer_forward(
            proj_ref, pos_ref, taps_ref, gain_ref,
            heads_ref, query_ref, key_ref, inv_ref, kc_ref, score_ref, step_ref, state_ref, update_ref, raw_ref,
            free_ref, shift_ref, sequence,
            lambda: at_steps(sequence, {0: [a[1].fourth, everything.second, wide.relay, wide_up.relay], 1: [everything.third, saves[0].start]}),
        )
        at_steps(sequence, {
            0: [exchanges[0].start, a[1].fifth],
            1: [exchanges[1].start, everything.fourth],
        })
        return carry

    lax.fori_loop(0, 2, per_sequence, 0)
    spread_ref[tensor] = heads_ref[pl.ds(pl.multiple_of(tensor * 128, 128), 128)]
    for save in (saves[2:]):
        save.start()
    everything.fifth()
    everything.from_twin(*NAMES)
    wide.arrive()
    wide_up.arrive()
    for save in saves:
        save.wait()
    gate_own.wait()
    up_own.wait()
    keep.wait()
    for exchange in exchanges:
        exchange.arrive()
    for item in (a[0], a[1], mix, wide, wide_up, tiny, outs, one, two, everything, exchanges[0], exchanges[1]):
        item.finish()


def dma(*counts):
    return [pltpu.SemaphoreType.DMA((count,)) for count in counts]


def kept_shapes():
    shape = jax.ShapeDtypeStruct
    rows = shape((2048, CHUNK), jnp.bfloat16)
    return (shape((2048, WIDE), jnp.float32), shape((2048, WIDE), jnp.bfloat16), rows) + saved_shapes()


def kept_buffers():
    return [pltpu.VMEM(item.shape, item.dtype) for item in kept_shapes()]


def run_entry(tokens, attn_gain, mix_shard, small, count, pos, gate_t, up_t, out_weight):
    vmem, hbm = pl.BlockSpec(memory_space=pltpu.VMEM), pl.BlockSpec(memory_space=pl.ANY)
    half, full = jnp.bfloat16, jnp.float32
    shape = jax.ShapeDtypeStruct
    return pl.pallas_call(
        entry_kernel,
        out_shape=(
            shape((16, 128, 2048), half),
            shape((8, 384), full),
            shape((8, CHUNK), full),
            shape((8, 128), full),
            shape((2 * FF_UNITS, 2048), half),
            shape((16, 128, 2048), half),
            shape((16, 128, CHUNK), half),
        )
        + kept_shapes(),
        in_specs=[vmem] * 6 + [hbm] * 3,
        out_specs=[hbm, vmem, vmem, vmem, hbm, hbm, vmem] + [hbm] * 12,
        scratch_shapes=kept_buffers()
        + dma(12)
        + [
            pltpu.VMEM((3, 2048, CHUNK), half),
            pltpu.VMEM((16, 128, 2048), half),
            pltpu.VMEM((8, 32, 128), half),
            pltpu.VMEM((16, 8, 128), full),
            pltpu.VMEM((8, 8, 128), full),
            pltpu.VMEM((16, CHUNK, CHUNK), full),
            pltpu.VMEM((16, CHUNK, CHUNK), full),
        ]
        + dma(7, 7, 7, 7, 8, 8, 8, 8, 17, 17, 16, 16, 8, 8, 4, 17, 17, 17, 17, 16, 16, 16, 16, 7, 7),
        compiler_params=pltpu.CompilerParams(
            collective_id=2, has_side_effects=True, vmem_limit_bytes=62 << 20
        ),
        cost_estimate=pl.CostEstimate(flops=60 << 30, bytes_accessed=16 << 20, transcendentals=0),
        name="entry",
    )(tokens, attn_gain, mix_shard, small, count, pos, gate_t, up_t, out_weight)


SMALL = 16


def exit_kernel(
    out_full_ref, attention_ref, ffn_part_ref, gathered_ref, hidden_grad_ref, pos_ref, taps_ref, gain_ref, input_ref, attn_gain_ref, sums_ref,
    far0, far1, far2, far3, far4, far5, far6, far7, far8, far9, far10, far11,
    input_grad_ref, ffn_ref, qkv_grad_ref, small_grad_ref, out_grad_ref, total_ref,
    proj_ref, mix_ref, heads_ref,
    query_ref, key_ref, inv_ref, kc_ref, score_ref, step_ref, state_ref, update_ref, raw_ref, load_sems, weight_ref,
    grad, attention, proj_low, taps_grad, gain_grad,
    back_ref, pull_ref, flow_ref, enter_ref, pre_ref,
    part, twin_part, slot, ffn_own, ffn_slot, ffn_staged, parts, part_slot, part_staged, outs, out_slot, out_staged,
    proj_t, tile, sums, sum_rows,
    head_send, head_recv, gather_send, gather_recv, ffn_send, ffn_recv, mix_send, mix_recv,
    outs_send, outs_recv, sum_send, sum_recv, row_send, row_recv, local, *sems,
):
    near = Neighbours()
    tensor, data = lax.axis_index("tensor"), lax.axis_index("dp")
    own = near.mine("own")
    place = DataPlace()

    loads = [
        pltpu.make_async_copy(ffn_part_ref.at[:, lanes(place.block(0, other))], ffn_own.at[other], local.at[other])
        for other in range(2)
    ]
    for copy in loads:
        copy.start()
    fill = pltpu.make_async_copy(out_full_ref, part, local.at[5])
    fill.start()
    sources = (far0, far1, far2, far3, far4, far5, far6, far7, far8, far9, far10, far11)
    places = (
        proj_ref, mix_ref, heads_ref, query_ref, key_ref, inv_ref, kc_ref, score_ref, step_ref, state_ref,
        update_ref, raw_ref,
    )
    saves = [
        pltpu.make_async_copy(source, target, load_sems.at[index])
        for index, (source, target) in enumerate(zip(sources, places))
    ]
    for copy in saves:
        copy.start()
    base = pltpu.make_async_copy(hidden_grad_ref, input_grad_ref, local.at[4])
    base.start()
    attention[own] = attention_ref[...]
    greet(everyone())
    fill.wait()

    def head_grads(head, carry):
        flow_ref[head] = low(nt(attention_ref[...], part[head]))
        return carry

    lax.fori_loop(0, 16, head_grads, 0)

    def head_rows(block):
        return grad.at[pl.ds(pl.multiple_of(block * 128, 128), 128)]

    exchange = Fan("tensor", 16, lambda peer: flow_ref.at[peer], head_rows, head_send, head_recv)
    exchange.start()
    gather = Gather(near, attention, gather_send, gather_recv)
    gather.start()
    ffn = DataScatter(
        lambda block: ffn_part_ref.at[:, lanes(block)], lambda other, rows: ffn_own[other, rows],
        ffn_slot, ffn_staged, ffn_send, ffn_recv,
    )
    ffn.start()
    grad[pl.ds(pl.multiple_of(tensor * 128, 128), 128)] = flow_ref[tensor]
    exchange.arrive()
    exchange.finish()
    for copy in saves:
        copy.wait()
    taps_grad[...] = jnp.zeros_like(taps_grad)
    gain_grad[...] = jnp.zeros_like(gain_grad)
    scatters = [
        Scatter(near, part, twin_part, slot, sems[2 * h], sems[2 * h + 1], HALVES[h]) for h in range(2)
    ]

    def per_sequence(sequence, carry):
        mixer_backward(
            grad, proj_ref, pos_ref, taps_ref, gain_ref,
            query_ref, key_ref, inv_ref, kc_ref, score_ref, step_ref, state_ref, update_ref, raw_ref,
            proj_low, taps_grad, gain_grad,
            back_ref, pull_ref, flow_ref, enter_ref, pre_ref, sequence,
            lambda: at_steps(sequence, {}),
            lambda: at_steps(sequence, {0: [gather.second], 1: [gather.third, scatters[0].second]}),
        )

        def flip(step, inner):
            quarter = near.quarter_at(step)
            proj_t[:, rows_of(sequence, quarter)] = quarter_values(sequence, quarter).T[:400]
            return inner

        lax.fori_loop(0, 4, flip, 0)
        at_steps(sequence, {0: [lambda: partials(0), scatters[0].first]})
        return carry

    def quarter_values(sequence, quarter):
        pieces = []
        for item in range(4):
            rows = pl.ds(pl.multiple_of((quarter * 4 + item) * 128 + sequence * 64, 64), 64)
            pieces.append(proj_low[rows, :])
        return jnp.concatenate(pieces, 0)

    def partials(sequence):
        def backward(step, inner):
            quarter = near.quarter_at(step)
            values = quarter_values(sequence, quarter)
            keep = lax.broadcasted_iota(jnp.int32, (256, WIDE), 1) <= 384
            partial = low(nt(jnp.where(keep, values, jnp.zeros_like(values)), mix_ref[...]))
            scatter_quarter(scatters, sequence, quarter, partial, part)
            return inner

        lax.fori_loop(0, 4, backward, 0)

    lax.fori_loop(0, 2, per_sequence, 0)

    def fetch(step):
        return pltpu.make_async_copy(gathered_ref.at[:, :, lanes(step)], tile.at[step % 2], local.at[2 + step % 2])

    fetch(0).start()
    partials(1)
    table = jnp.concatenate([taps_grad[...], gain_grad[...]], 1)

    def weights(step, carry):
        @pl.when(step < 7)
        def _():
            fetch(step + 1).start()

        fetch(step).wait()
        first = tile[step % 2, :, 0:64].reshape(1024, 256)
        column = jnp.concatenate([first, tile[step % 2, :, 64:128].reshape(1024, 256)], 0)
        product = nn(proj_t[...], column)
        parts[0:400, lanes(step)] = low(product)
        at_steps(step, {1: [scatters[1].first], 3: [gather.fourth], 5: [scatters[0].third]})
        return carry

    lax.fori_loop(0, 8, weights, 0)
    pick_row = lax.broadcasted_iota(jnp.int32, (CHUNK, 2048), 0)
    pick_lane = lax.broadcasted_iota(jnp.int32, (CHUNK, 2048), 1)
    wanted = (pick_lane // 256) * 16 + pick_lane % 256
    select = ((pick_row == wanted) & (pick_lane % 256 < 16)).astype(jnp.bfloat16)
    for tap in range(4):
        for field in range(3):
            row = tap * 3 + field
            pull_ref[0, row : row + 1, :] = taps_grad[tap : tap + 1, field * 128 : field * 128 + 128]
    pull_ref[0, 12:13, :] = gain_grad[0:1, :]
    small = nn(low(pull_ref[0, 0:16, :]), select)
    small_row = lax.broadcasted_iota(jnp.int32, (16, 2048), 0)
    moved = jnp.concatenate([small[15:16], small[0:15]], 0)
    beta_row = parts[384:400, :].astype(jnp.float32)
    parts[384:400, :] = low(jnp.where(small_row == 0, beta_row, moved))
    mix = DataScatter(
        lambda block: parts.at[:, lanes(block)],
        lambda other, rows: parts[rows, lanes(place.block(0, other))],
        part_slot, part_staged, mix_send, mix_recv,
    )
    mix.start()
    scatters[1].second()
    gather.fifth()
    gather.from_twin(*NAMES)

    def out_weights(step, carry):
        outs[:, lanes(step)] = low(tn(heads_ref[...], attention[:, :, lanes(step)].reshape(2048, 256)))
        return carry

    lax.fori_loop(0, 8, out_weights, 0)
    out_scatter = DataScatter(
        lambda block: outs.at[:, lanes(block)],
        lambda other, rows: outs[rows, lanes(place.block(0, other))],
        out_slot, out_staged, outs_send, outs_recv,
    )
    out_scatter.start()
    for copy in loads:
        copy.wait()
    ffn.relay()
    base.wait()

    def ending(half):
        def strip(rows, total):
            value = scatters[half].total(rows)
            unit, scale = normalise(input_ref[rows].astype(jnp.float32))
            input_grad_ref[rows] += norm_back(value, unit, scale, attn_gain_ref)
            return total + value * unit

        scatters[half].fourth()
        return strips(64, strip, half * 64)(jnp.zeros((16, 2048), jnp.float32))

    total = ending(0)
    scatters[1].third()
    mix.relay()
    out_scatter.relay()
    total = total + ending(1)
    total = jnp.sum(total, 0, keepdims=True)
    sums[tensor, 8:24] = sums_ref[8:24]
    for piece in range(8):
        sums[tensor, piece : piece + 1] = total[:, piece * 256 : piece * 256 + 256]
    one, two = tile_sum(sums, sum_rows, None, (sum_send, sum_recv, row_send, row_recv))
    one.start()
    one.arrive()
    sum_rows[data] = jnp.sum(sums[...], 0)
    two.start()
    ffn.result(ffn_ref)
    two.arrive()
    total_ref[...] = jnp.sum(sum_rows[...], 0)
    mix.result(weight_ref)
    for field in range(3):
        qkv_grad_ref[field] = weight_ref[field * 128 : field * 128 + 128, :].T
    small_grad_ref[...] = weight_ref[384:400, :]
    out_scatter.result(out_grad_ref)
    for item in (gather, ffn, scatters[0], scatters[1], mix, out_scatter, one, two):
        item.finish()


def run_exit(
    out_full, attention, ffn_part, gathered, hidden_grad, proj, pos, taps, gain, mix, heads, tokens, attn_gain, sums, saved
):
    vmem, hbm = pl.BlockSpec(memory_space=pltpu.VMEM), pl.BlockSpec(memory_space=pl.ANY)
    half, full = jnp.bfloat16, jnp.float32
    shape = jax.ShapeDtypeStruct
    return pl.pallas_call(
        exit_kernel,
        out_shape=(
            shape((128, 2048), full),
            shape((2 * HIDDEN, 256), full),
            shape((3, 256, CHUNK), full),
            shape((16, 256), full),
            shape((CHUNK, 256), full),
            shape((24, 256), full),
        ),
        in_specs=[hbm, vmem] + [hbm] * 3 + [vmem] * 6 + [hbm] * 12,
        out_specs=[vmem] * 6,
        scratch_shapes=kept_buffers()
        + dma(12)
        + [
            pltpu.VMEM((400, 256), full),
            pltpu.VMEM((2048, CHUNK), half),
            pltpu.VMEM((16, 128, 2048), half),
            pltpu.VMEM((2048, WIDE), half),
            pltpu.VMEM((8, 384), full),
            pltpu.VMEM((8, CHUNK), full),
            pltpu.VMEM((16, CHUNK, CHUNK), half),
            pltpu.VMEM((16, CHUNK, CHUNK), full),
            pltpu.VMEM((16, CHUNK, CHUNK), half),
            pltpu.VMEM((16, CHUNK, CHUNK), full),
            pltpu.VMEM((1024, 384), full),
            pltpu.VMEM((16, 128, 2048), half),
            pltpu.VMEM((8, 128, 2048), half),
            pltpu.VMEM((7, 128, 2048), half),
            pltpu.VMEM((2, 2 * HIDDEN, 256), half),
            pltpu.VMEM((7, 2 * HIDDEN, 256), half),
            pltpu.VMEM((2 * HIDDEN, 256), half),
            pltpu.VMEM((400, 2048), half),
            pltpu.VMEM((7, 400, 256), half),
            pltpu.VMEM((400, 256), half),
            pltpu.VMEM((CHUNK, 2048), half),
            pltpu.VMEM((7, CHUNK, 256), half),
            pltpu.VMEM((CHUNK, 256), half),
            pltpu.VMEM((400, 2048), half),
            pltpu.VMEM((2, 16, 128, 256), half),
            pltpu.VMEM((16, 24, 256), full),
            pltpu.VMEM((8, 24, 256), full),
        ]
        + dma(16, 16, 17, 17, 7, 7, 7, 7, 7, 7, 16, 16, 8, 8, 6, 16, 16, 16, 16),
        compiler_params=pltpu.CompilerParams(
            collective_id=3, has_side_effects=True, vmem_limit_bytes=63 << 20
        ),
        cost_estimate=pl.CostEstimate(flops=60 << 30, bytes_accessed=16 << 20, transcendentals=0),
        name="exit",
    )(
        out_full, attention, ffn_part, gathered, hidden_grad, pos, taps, gain, tokens, attn_gain, sums, proj, mix, heads,
        *saved,
    )


def token_places(segment):
    length = segment.shape[1]
    before = jnp.sum((segment[:, None, :] < segment[:, :, None]).astype(jnp.int32), -1)
    place = jnp.arange(length, dtype=jnp.int32)[None, :] - before
    return jnp.transpose(place.reshape(2, 8, CHUNK), (1, 0, 2)).reshape(16, CHUNK).astype(jnp.float32)


def f32(value):
    return value.astype(jnp.float32)


def body(
    inputs, teacher, segment_ids, padding, attn_gain, qkv_weight, beta_weight, conv_taps, head_gain,
    out_weight, mlp_gain, gate_weight, up_weight, down_weight,
):
    hidden_units = gate_weight.shape[1]
    rows = 128
    features = inputs.shape[2]

    small = jnp.concatenate([conv_taps.reshape(12, 16), head_gain.reshape(1, 16)], 0)
    lane = jnp.arange(CHUNK)[None, :] // 16 == lax.axis_index("dp")
    small = jnp.where(lane, jnp.tile(jnp.pad(small, ((0, 3), (0, 0))), (1, 8)), 0)
    small = jnp.concatenate([small, jnp.pad(beta_weight.reshape(2, CHUNK), ((0, 14), (0, 0)))], 0)
    mix_shard = jnp.transpose(qkv_weight, (1, 0, 2))
    gate_t, up_t = jnp.transpose(gate_weight), jnp.transpose(up_weight)
    count = jnp.broadcast_to(f32(jnp.sum(padding)), (8, 128))

    tokens = inputs.reshape(rows, features)
    attn_gain_row = attn_gain.reshape(1, features)
    mlp_gain_row = mlp_gain.reshape(1, features)
    pos = token_places(segment_ids)
    (
        gathered, taps, gain, total, gate_up, out_full, spread, proj, mix_full, heads, *saved
    ) = run_entry(tokens, attn_gain_row, mix_shard, small, count, pos, gate_t, up_t, out_weight)
    valid = total[0, 0]
    scale = 16 * 1024 / valid
    heads_rows = jnp.transpose(spread, (1, 0, 2)).reshape(rows, features)
    hidden = f32(tokens) + nn(heads_rows, out_full.reshape(features, features))

    mask = f32(padding.reshape(rows, 1))
    masks = jnp.broadcast_to(jnp.stack([mask, scale * mask]), (2, rows, CHUNK))
    output, hidden_grad, attention_low, sums, ffn_part, down_grad = run_ffn(
        hidden, mlp_gain_row, teacher.reshape(rows, features), masks, gate_up, down_weight
    )
    input_grad, ffn_grads, qkv_grad, small_grads, out_grad, totals = run_exit(
        out_full, attention_low, ffn_part, gathered, hidden_grad, proj, pos, taps, gain, mix_full, heads, tokens,
        attn_gain_row, sums, saved,
    )
    loss = totals[16, 0] / (valid * features)
    small_grad = small_grads[1:14, :16]
    shape = (2, 64, features)
    return (
        output.reshape(shape),
        loss,
        input_grad.reshape(shape),
        totals[:8].reshape(features),
        jnp.transpose(qkv_grad, (1, 0, 2)),
        jnp.transpose(small_grads[0:1]),
        small_grad[:12].reshape(4, 3, 1, 16),
        small_grad[12:].reshape(1, 16),
        out_grad,
        totals[8:16].reshape(features),
        jnp.transpose(ffn_grads[:hidden_units]),
        jnp.transpose(ffn_grads[HIDDEN : HIDDEN + hidden_units]),
        down_grad[:hidden_units],
    )


def solution(mesh):
    in_specs = (
        P("dp", "tensor", None),
        P("dp", "tensor", None),
        P("dp", None),
        P("dp", "tensor"),
        P(),
        P("dp", None, "tensor"),
        P("dp", "tensor"),
        P(None, None, "tensor", "dp"),
        P("tensor", "dp"),
        P("tensor", "dp"),
        P(),
        P("dp", "tensor"),
        P("dp", "tensor"),
        P("tensor", "dp"),
    )
    out_specs = (
        P("dp", "tensor", None),
        P(),
        P("dp", "tensor", None),
        P(),
        P("dp", None, "tensor"),
        P("dp", "tensor"),
        P(None, None, "tensor", "dp"),
        P("tensor", "dp"),
        P("tensor", "dp"),
        P(),
        P("dp", "tensor"),
        P("dp", "tensor"),
        P("tensor", "dp"),
    )
    return jax.shard_map(body, mesh=mesh, in_specs=in_specs, out_specs=out_specs, check_vma=False)
```

```python
import jax
import jax.numpy as jnp
from jax import lax
from jax.experimental import pallas as pl
from jax.experimental.pallas import tpu as pltpu
from jax.sharding import PartitionSpec as P

MESH = pl.DeviceIdType.MESH
CHUNK = 128
WIDE = 512
PARAMS = pltpu.CompilerParams(vmem_limit_bytes=56 << 20)


def nn(a, b):
    return jnp.dot(a, b, preferred_element_type=jnp.float32)


def nt(a, b):
    return lax.dot_general(a, b, (((1,), (1,)), ((), ())), preferred_element_type=jnp.float32)


def tn(a, b):
    return lax.dot_general(a, b, (((0,), (0,)), ((), ())), preferred_element_type=jnp.float32)


def low(value):
    return value.astype(jnp.bfloat16)


def split(value):
    high = low(value)
    return high, low(value - high.astype(jnp.float32))


def fine(product, a, b):
    a_high, a_rest = a
    b_high, b_rest = b
    return product(a_high, b_high) + (product(a_high, b_rest) + product(a_rest, b_high))


def grid_masks():
    row = lax.broadcasted_iota(jnp.int32, (CHUNK, CHUNK), 0)
    column = lax.broadcasted_iota(jnp.int32, (CHUNK, CHUNK), 1)
    return row, column


def chunk_rows(index, sequence):
    first = pl.multiple_of(index * 256 + sequence * 64, 64)
    second = pl.multiple_of(index * 256 + 128 + sequence * 64, 64)
    return first, second


def load(ref, index, sequence, lanes=slice(None)):
    first, second = chunk_rows(index, sequence)
    return jnp.concatenate([ref[pl.ds(first, 64), lanes], ref[pl.ds(second, 64), lanes]], 0)


def store(ref, index, sequence, value, lanes=slice(None)):
    first, second = chunk_rows(index, sequence)
    ref[pl.ds(first, 64), lanes] = value[:64]
    ref[pl.ds(second, 64), lanes] = value[64:]


def columns_of(pos_ref, index, sequence):
    line = pos_ref[pl.ds(index * 2 + sequence, 1), :]
    return line, jnp.broadcast_to(line, (CHUNK, CHUNK)).T


def convolve(proj_ref, taps_ref, index, sequence, place):
    fields = slice(0, 384)
    current = load(proj_ref, index, sequence, fields)
    before = pl.multiple_of(jnp.maximum(index * 256 - 128 + sequence * 64 + 56, 0), 8)
    window = jnp.concatenate([proj_ref[pl.ds(before, 8), fields], current], 0)
    total = current * taps_ref[0:1, :]
    moved = [current]
    for offset in range(1, 4):
        keep = (place[:, 0:1] >= offset).astype(jnp.float32)
        shifted = window[8 - offset : 8 - offset + CHUNK] * keep
        moved.append(shifted)
        total = total + shifted * taps_ref[offset : offset + 1, :]
    return total, moved


def activate(total):
    sigma = sigmoid(total)
    act = total * sigma
    query, keys, values = act[:, :128], act[:, 128:256], act[:, 256:]
    query_scale = lax.rsqrt(jnp.sum(query * query, -1, keepdims=True) + 1e-06)
    key_scale = lax.rsqrt(jnp.sum(keys * keys, -1, keepdims=True) + 1e-06)
    return sigma, query * query_scale, query_scale, keys * key_scale, key_scale, values


def inverses(mixings, row, column):
    eye = (row == column).astype(jnp.float32)
    pair = (row // 2) == (column // 2)
    totals = [eye - jnp.where(pair, mixing, 0.0) for mixing in mixings]
    size = 2
    while size < CHUNK:
        corner = (
            ((row // (2 * size)) == (column // (2 * size)))
            & (((row // size) % 2) == 1)
            & (((column // size) % 2) == 0)
        )
        corners = [low(jnp.where(corner, mixing, 0.0)) for mixing in mixings]
        helds = [low(total) for total in totals]
        inners = [low(nn(held, part)) for held, part in zip(helds, corners)]
        totals = [total - nn(inner, held) for total, inner, held in zip(totals, inners, helds)]
        size *= 2
    helds = [split(total) for total in totals]
    rests = [
        low(eye - total - fine(nn, split(mixing), held))
        for total, mixing, held in zip(totals, mixings, helds)
    ]
    return [total + nn(held[0], rest) for total, held, rest in zip(totals, helds, rests)]


def mixer_forward(
    proj_ref, pos_ref, taps_ref, gain_ref,
    heads_ref, query_ref, key_ref, inv_ref, kc_ref, score_ref, step_ref, state_ref, update_ref, raw_ref,
    free_ref, shift_ref, which, between,
):
    row, column = grid_masks()
    depth = row - column

    streams = [(index, which) for index in range(8)]

    def prepare():
        lines, queries, keys_all, values_all, betas, withins, carrieds, mixings = ([] for _ in range(8))
        for index, sequence in streams:
            line, place = columns_of(pos_ref, index, sequence)
            total, _ = convolve(proj_ref, taps_ref, index, sequence, place)
            _, query, _, keys, _, values = activate(total)
            lines.append(line[:, 127:128])
            queries.append(low(query * 128 ** (-0.5)))
            keys_all.append(keys)
            values_all.append(low(values))
            betas.append(sigmoid(load(proj_ref, index, sequence, slice(384, 512))))
            withins.append((depth >= 0) & (depth.astype(jnp.float32) <= place))
            carrieds.append(place > row.astype(jnp.float32))
        grams = [fine(nt, split(keys), split(keys * beta)) for keys, beta in zip(keys_all, betas)]
        mixings = [jnp.where(within & (depth > 0), gram, 0.0) for within, gram in zip(withins, grams)]
        solved_all = [low(solved) for solved in inverses(mixings, row, column)]
        boths = [
            nn(solved, jnp.concatenate([low(jnp.where(carried, keys, 0.0)), values], 1))
            for solved, carried, keys, values in zip(solved_all, carrieds, keys_all, values_all)
        ]
        key_lows = [low(keys) for keys in keys_all]
        scores = [nt(query, key_low) for query, key_low in zip(queries, key_lows)]
        weights = [
            jnp.where((127 - row).astype(jnp.float32) <= last, beta, 0.0)
            for last, beta in zip(lines, betas)
        ]
        ends_all = [
            tn(key_low, low(jnp.concatenate([weight, weight], 1) * both))
            for key_low, weight, both in zip(key_lows, weights, boths)
        ]
        for item, (index, sequence) in enumerate(streams):
            block = index * 2 + sequence
            through = jnp.where((row == column) & (lines[item] > 127.0), 1.0, 0.0)
            store(query_ref, index, sequence, queries[item])
            store(key_ref, index, sequence, key_lows[item])
            inv_ref[block] = solved_all[item]
            kc_ref[block] = low(boths[item][:, :128])
            free_ref[block] = boths[item][:, 128:]
            score_ref[block] = low(jnp.where(withins[item], scores[item], 0.0))
            step_ref[block] = low(through - ends_all[item][:, :128])
            shift_ref[block] = ends_all[item][:, 128:]

    prepare()
    between()
    state = jnp.zeros((CHUNK, CHUNK), jnp.float32)
    for index in range(8):
        block = index * 2 + which
        state_low = low(state)
        state_ref[block] = state_low
        state = nn(step_ref[block], state_low) + shift_ref[block]

    def finish():
        blocks = [index * 2 + sequence for index, sequence in streams]
        states = [state_ref[block] for block in blocks]
        recalls = [nn(kc_ref[block], state) for block, state in zip(blocks, states)]
        reads = [nn(load(query_ref, *stream), state) for stream, state in zip(streams, states)]
        updates = [free_ref[block] - recall for block, recall in zip(blocks, recalls)]
        weighted = [
            low(sigmoid(load(proj_ref, *stream, slice(384, 512))) * update)
            for stream, update in zip(streams, updates)
        ]
        mixed = [nn(score_ref[block], weight) for block, weight in zip(blocks, weighted)]
        for item, (index, sequence) in enumerate(streams):
            _, place = columns_of(pos_ref, index, sequence)
            output = jnp.where(place > row.astype(jnp.float32), reads[item], 0.0) + mixed[item]
            scale = lax.rsqrt(jnp.mean(output * output, -1, keepdims=True) + 1e-05)
            update_ref[blocks[item]] = low(updates[item])
            raw_ref[blocks[item]] = output
            store(heads_ref, index, sequence, low(output * scale * gain_ref[0:1, :]))

    finish()


def mixer_backward(
    grad_ref, proj_ref, pos_ref, taps_ref, gain_ref,
    query_ref, key_ref, inv_ref, kc_ref, score_ref, step_ref, state_ref, update_ref, raw_ref,
    out_ref, taps_grad_ref, gain_grad_ref,
    back_ref, pull_ref, flow_ref, enter_ref, pre_ref, which, between, after,
):
    row, column = grid_masks()
    depth = row - column

    def prepare():
        streams = [(index, which) for index in range(8)]
        blocks = [index * 2 + sequence for index, sequence in streams]
        back_lows = []
        for (index, sequence), block in zip(streams, blocks):
            grad = load(grad_ref, index, sequence).astype(jnp.float32)
            output = raw_ref[block]
            scale = lax.rsqrt(jnp.mean(output * output, -1, keepdims=True) + 1e-05)
            unit = output * scale
            inner = grad * gain_ref[0:1, :]
            gain_grad_ref[0:1, :] += jnp.sum(grad * unit, 0, keepdims=True)
            back = scale * (inner - unit * jnp.mean(inner * unit, -1, keepdims=True))
            back_lows.append(low(back))
        pulls = [tn(score_ref[block], back_low) for block, back_low in zip(blocks, back_lows)]
        rights = []
        for (index, sequence), back_low, pull in zip(streams, back_lows, pulls):
            _, place = columns_of(pos_ref, index, sequence)
            carried = place > row.astype(jnp.float32)
            beta = sigmoid(load(proj_ref, index, sequence, slice(384, 512)))
            rights.append(
                jnp.concatenate([jnp.where(carried, back_low, 0.0), low(-beta * pull)], 0)
            )
        enters = [
            tn(jnp.concatenate([load(query_ref, *stream), kc_ref[block]], 0), right)
            for stream, block, right in zip(streams, blocks, rights)
        ]
        for block, back_low, pull, enter in zip(blocks, back_lows, pulls, enters):
            enter_ref[block] = enter
            back_ref[block] = back_low
            pull_ref[block] = pull

    prepare()
    between()
    flow = jnp.zeros((CHUNK, CHUNK), jnp.float32)
    for index in reversed(range(8)):
        block = index * 2 + which
        flow_low = low(flow)
        flow_ref[block] = flow_low
        flow = tn(step_ref[block], flow_low) + enter_ref[block]

    def collect(double, carry):
        streams = [(double * 4 + item, which) for item in range(4)]
        blocks = [index * 2 + sequence for index, sequence in streams]
        lines, places, betas, carrieds, closings = ([] for _ in range(5))
        for index, sequence in streams:
            line, place = columns_of(pos_ref, index, sequence)
            lines.append(line)
            places.append(place)
            betas.append(sigmoid(load(proj_ref, index, sequence, slice(384, 512))))
            carrieds.append(place > row.astype(jnp.float32))
            closings.append((127 - row).astype(jnp.float32) <= line[:, 127:128])
        queries = [load(query_ref, *stream) for stream in streams]
        keys_all = [load(key_ref, *stream) for stream in streams]
        updates = [update_ref[block].astype(jnp.float32) for block in blocks]
        weighted = [beta * update for beta, update in zip(betas, updates)]
        flows = [flow_ref[block] for block in blocks]
        states = [state_ref[block] for block in blocks]
        backs = [back_ref[block] for block in blocks]
        key_flows = [nn(keys, flow) for keys, flow in zip(keys_all, flows)]
        score_grads = [nt(back, low(weight)) for back, weight in zip(backs, weighted)]
        grams = [nt(keys, keys) for keys in keys_all]
        weight_grads = [
            pull_ref[block] + jnp.where(closing, key_flow, 0.0)
            for block, closing, key_flow in zip(blocks, closings, key_flows)
        ]
        right_grads = [
            tn(inv_ref[block], low(beta * weight_grad))
            for block, beta, weight_grad in zip(blocks, betas, weight_grads)
        ]
        score_lows = [
            low(jnp.where((depth >= 0) & (depth.astype(jnp.float32) <= place), score_grad, 0.0))
            for place, score_grad in zip(places, score_grads)
        ]
        query_grads = [
            nt(jnp.where(carried, back, 0.0), state) + nn(score_low, keys)
            for carried, back, state, score_low, keys in zip(
                carrieds, backs, states, score_lows, keys_all
            )
        ]
        mixing_grads = [
            jnp.where((depth < 0) & ((-depth).astype(jnp.float32) <= line), -nt(low(update), low(right_grad)), 0.0)
            for line, update, right_grad in zip(lines, updates, right_grads)
        ]
        gram_lows = [low(beta * mixing_grad) for beta, mixing_grad in zip(betas, mixing_grads)]
        key_grads = [
            nt(
                jnp.concatenate(
                    [low(jnp.where(closing, weight, 0.0)), low(jnp.where(carried, -right_grad, 0.0))], 1
                ),
                jnp.concatenate([flow, state], 1),
            )
            for closing, weight, carried, right_grad, flow, state in zip(
                closings, weighted, carrieds, right_grads, flows, states
            )
        ]
        key_grads = [
            key_grad
            + tn(jnp.concatenate([score_low, gram_low], 0), jnp.concatenate([query, keys], 0))
            + nn(gram_low, keys)
            for key_grad, score_low, gram_low, query, keys in zip(
                key_grads, score_lows, gram_lows, queries, keys_all
            )
        ]
        for item, (index, sequence) in enumerate(streams):
            total, moved = convolve(proj_ref, taps_ref, index, sequence, places[item])
            sigma, query, query_scale, keys, key_scale, _ = activate(total)
            beta = betas[item]
            beta_grad = jnp.sum(
                weight_grads[item] * updates[item] + mixing_grads[item] * grams[item], -1, keepdims=True
            )
            query_grad = query_grads[item] * 128 ** (-0.5)
            query_act = query_scale * (
                query_grad - query * jnp.sum(query * query_grad, -1, keepdims=True)
            )
            key_act = key_scale * (
                key_grads[item] - keys * jnp.sum(keys * key_grads[item], -1, keepdims=True)
            )
            act_grad = jnp.concatenate([query_act, key_act, right_grads[item]], 1)
            pre_grad = act_grad * (sigma * (1.0 + total * (1.0 - sigma)))
            for offset in range(4):
                taps_grad_ref[offset : offset + 1, :] += jnp.sum(
                    pre_grad * moved[offset], 0, keepdims=True
                )
            pre_ref[pl.ds(pl.multiple_of(index * CHUNK, CHUNK), CHUNK), :] = pre_grad
            logit_grad = jnp.where(column == 0, beta_grad * beta * (1.0 - beta), 0.0)
            store(out_ref, index, sequence, low(logit_grad), slice(384, 512))
        return carry

    lax.fori_loop(0, 2, collect, 0)
    after()

    def spread(pair_index, carry):
        for item in range(2):
            index, sequence = pair_index * 2 + item, which
            after = pl.multiple_of(jnp.minimum(index * CHUNK + CHUNK, 896), CHUNK)
            live = jnp.where(index == 7, 0.0, 1.0)
            current = pre_ref[pl.ds(pl.multiple_of(index * CHUNK, CHUNK), CHUNK), :]
            window = jnp.concatenate([current, pre_ref[pl.ds(after, 8), :] * live], 0)
            _, place = columns_of(pos_ref, index, sequence)
            _, follow = columns_of(pos_ref, jnp.minimum(index + 1, 7), sequence)
            places = jnp.concatenate([place, follow[0:8]], 0)[:, 0:1]
            total = current * taps_ref[0:1, :]
            for offset in range(1, 4):
                masked = window * (places >= offset).astype(jnp.float32)
                total = total + masked[offset : offset + CHUNK] * taps_ref[offset : offset + 1, :]
            store(out_ref, index, sequence, low(total), slice(0, 384))
        return carry

    lax.fori_loop(0, 4, spread, 0)


def saved_shapes():
    rows = jax.ShapeDtypeStruct((2048, CHUNK), jnp.bfloat16)
    small = jax.ShapeDtypeStruct((16, CHUNK, CHUNK), jnp.bfloat16)
    wide = jax.ShapeDtypeStruct((16, CHUNK, CHUNK), jnp.float32)
    return (rows, rows, small, small, small, small, small, small, wide)


def spot(y, z, core):
    return (y * 2 + z) * 2 + core


class Neighbours:
    def __init__(self):
        index = lax.axis_index("tensor")
        self.core = index % 2
        self.z = (index // 2) % 2
        self.y = index // 4
        up, down, far = (self.y + 1) % 4, (self.y + 3) % 4, (self.y + 2) % 4
        other = 1 - self.z
        self.up = spot(up, self.z, self.core)
        self.down = spot(down, self.z, self.core)
        self.side = spot(self.y, other, self.core)
        self.twin = spot(self.y, self.z, 1 - self.core)
        self.chips = {
            "own": self.y * 2 + self.z,
            "side": self.y * 2 + other,
            "down": down * 2 + self.z,
            "up": up * 2 + self.z,
            "downside": down * 2 + other,
            "upside": up * 2 + other,
            "far": far * 2 + self.z,
            "farside": far * 2 + other,
        }

    def mine(self, name):
        return self.chips[name] * 2 + self.core

    def twins(self, name):
        return self.chips[name] * 2 + 1 - self.core

    def quarter_at(self, step):
        quarter = step % 4
        shift = quarter + quarter // 2 - 2 * (quarter // 3)
        return (self.y + shift) % 4


def greet(devices):
    barrier = pltpu.get_barrier_semaphore()
    for device in devices:
        pl.semaphore_signal(barrier, inc=1, device_id=device, device_id_type=MESH)
    pl.semaphore_wait(barrier, len(devices))


def remote(source, target, send_sem, recv_sem, device):
    return pltpu.make_async_remote_copy(
        src_ref=source, dst_ref=target, send_sem=send_sem, recv_sem=recv_sem,
        device_id=device, device_id_type=MESH,
    )


NAMES = ("own", "side", "down", "up", "downside", "upside", "far", "farside")
ORDER = (("own", "side"), ("up", "upside"), ("down", "downside"), ("far", "farside"))


class Rows:
    def __init__(self, first, count):
        self.first, self.count = first, count
        self.whole = pl.ds(first, count)
        self.top = pl.ds(first, count // 2)
        self.bottom = pl.ds(first + count // 2, count // 2)


ALL, HALVES = Rows(0, 128), (Rows(0, 64), Rows(64, 64))


class Gather:
    copies = 17

    def __init__(self, near, buffer, sends, receives, rows=ALL):
        self.near, self.buffer, self.sends, self.receives = near, buffer, sends, receives
        self.rows = rows

    def piece(self, key, name):
        rows = self.rows
        part = {5: rows.top, 6: rows.bottom, 7: rows.top, 8: rows.bottom}.get(key, rows.whole)
        return self.buffer.at[self.near.mine(name), part]

    def copy(self, key, piece, device):
        return remote(piece, piece, self.sends.at[key], self.receives.at[key], {"tensor": device})

    def send(self, key, name, device):
        self.copy(key, self.piece(key, name), device).start()

    def arrive(self, key, name):
        self.copy(key, self.piece(key, name), self.near.twin).wait_recv()

    def to_twin(self, name):
        self.send(9 + NAMES.index(name), name, self.near.twin)

    def from_twin(self, *names):
        for name in names:
            piece = self.buffer.at[self.near.twins(name), self.rows.whole]
            self.copy(9 + NAMES.index(name), piece, self.near.twin).wait_recv()

    def start(self):
        near = self.near
        self.send(1, "own", near.up)
        self.send(2, "own", near.down)
        self.send(0, "own", near.side)
        self.to_twin("own")

    def from_down(self):
        self.arrive(1, "down")
        self.send(5, "down", self.near.up)
        self.to_twin("down")

    def from_up(self):
        self.arrive(2, "up")
        self.send(6, "up", self.near.down)
        self.to_twin("up")

    def from_side(self):
        self.arrive(0, "side")
        self.send(3, "side", self.near.up)
        self.send(4, "side", self.near.down)
        self.to_twin("side")

    def second(self):
        self.from_down()
        self.from_up()
        self.from_side()

    def third(self):
        self.arrive(5, "far")
        self.send(7, "far", self.near.side)
        self.arrive(6, "far")
        self.send(8, "far", self.near.side)
        self.to_twin("far")

    def fourth(self):
        self.arrive(4, "upside")
        self.to_twin("upside")
        self.arrive(3, "downside")
        self.to_twin("downside")

    def fifth(self):
        self.arrive(7, "farside")
        self.arrive(8, "farside")
        self.to_twin("farside")

    def finish(self):
        names = ("own", "own", "own", "side", "side", "down", "up", "far", "far") + NAMES
        for key, name in enumerate(names):
            self.copy(key, self.piece(key, name), self.near.twin).wait_send()


def add_rows(target, sources, count=128):
    def piece(index, carry):
        rows = pl.ds(pl.multiple_of(index * 16, 16), 16)
        total = target[rows].astype(jnp.float32)
        for source in sources:
            total = total + source[rows].astype(jnp.float32)
        target[rows] = total.astype(target.dtype)
        return carry

    lax.fori_loop(0, count // 16, piece, 0)


class Scatter:
    copies = 16

    def __init__(self, near, part, twin_part, slot, sends, receives, rows=ALL):
        self.near, self.part, self.twin_part, self.slot = near, part, twin_part, slot
        self.sends, self.receives, self.rows = sends, receives, rows

    def describe(self, key, source, target, device):
        return remote(source, target, self.sends.at[key], self.receives.at[key], {"tensor": device})

    def twin_copy(self, chip):
        whole = self.rows.whole
        return self.describe(
            8 + chip, self.part.at[chip * 2 + 1 - self.near.core, whole],
            self.twin_part.at[chip, whole], self.near.twin,
        )

    def to_twin(self, chip):
        self.twin_copy(chip).start()

    def mine(self, name, rows=None):
        return self.part.at[self.near.mine(name), self.rows.whole if rows is None else rows]

    def chip_sum(self, name):
        chip = self.near.chips[name]
        self.twin_copy(chip).wait_recv()
        add_rows(self.mine(name), [self.twin_part.at[chip, self.rows.whole]], self.rows.count)

    def outgoing(self, key):
        near, slot, rows = self.near, self.slot, self.rows
        name, place, part, device = (
            ("farside", 0, rows.whole, near.side),
            ("far", 1, rows.top, near.down),
            ("far", 1, rows.bottom, near.up),
            ("downside", 2, rows.whole, near.down),
            ("upside", 3, rows.whole, near.up),
            ("down", 4, rows.whole, near.down),
            ("up", 5, rows.whole, near.up),
            ("side", 6, rows.whole, near.side),
        )[key]
        return self.describe(key, self.mine(name, part), slot.at[place, part], device)

    def send(self, key):
        self.outgoing(key).start()

    def arrive(self, key):
        self.outgoing(key).wait_recv()

    def sums(self, *names):
        for name in names:
            self.chip_sum(name)
            key = {"farside": 0, "downside": 3, "upside": 4}.get(name)
            if key is not None:
                self.send(key)

    def first(self):
        self.sums("farside", "downside", "upside", "far", "down", "up", "side")

    def second(self):
        self.arrive(0)
        add_rows(self.mine("far"), [self.slot.at[0, self.rows.whole]], self.rows.count)
        self.send(1)
        self.send(2)

    def to_side(self):
        slot, rows = self.slot, self.rows
        self.arrive(3)
        self.arrive(4)
        add_rows(self.mine("side"), [slot.at[2, rows.whole], slot.at[3, rows.whole]], rows.count)
        self.send(7)

    def to_down(self):
        rows = self.rows
        self.arrive(1)
        add_rows(self.mine("down", rows.top), [self.slot.at[1, rows.top]], rows.count // 2)
        self.send(5)

    def to_up(self):
        rows = self.rows
        self.arrive(2)
        add_rows(self.mine("up", rows.bottom), [self.slot.at[1, rows.bottom]], rows.count // 2)
        self.send(6)

    def third(self):
        self.to_side()
        self.to_down()
        self.to_up()

    def fourth(self):
        self.twin_copy(self.near.chips["own"]).wait_recv()
        for key in (7, 5, 6):
            self.arrive(key)

    def total(self, rows):
        chip = self.near.chips["own"]
        value = self.part[chip * 2 + self.near.core, rows].astype(jnp.float32)
        value = value + self.twin_part[chip, rows].astype(jnp.float32)
        for place in (4, 5, 6):
            value = value + self.slot[place, rows].astype(jnp.float32)
        return value

    def finish(self):
        for chip in range(8):
            self.twin_copy(chip).wait_send()
        for key in range(8):
            self.outgoing(key).wait_send()


def strips(count, body, start=0):
    def piece(index, carry):
        return body(pl.ds(pl.multiple_of(start + index * 16, 16), 16), carry)

    return lambda carry: lax.fori_loop(0, count // 16, piece, carry)


def normalise(values):
    scale = lax.rsqrt(jnp.mean(values * values, -1, keepdims=True) + 1e-06)
    return values * scale, scale


def norm_into(source, gain_ref, target):
    def strip(rows, carry):
        unit, _ = normalise(source[rows].astype(jnp.float32))
        target[rows] = low(unit * gain_ref[0:1, :])
        return carry

    strips(128, strip)(0)


def norm_back(values, unit, scale, gain_ref):
    inner = values * gain_ref[0:1, :]
    return scale * (inner - unit * jnp.mean(inner * unit, -1, keepdims=True))


def at_steps(step, table):
    for moment, actions in table.items():

        @pl.when(step == moment)
        def _(actions=actions):
            for action in actions:
                action()


def pair(items, names):
    return lambda: items.from_twin(*names)


def summing(items, *names):
    return lambda: items.sums(*names)


HIDDEN = 384
FF_UNITS = 352


def sigmoid(value):
    return 1.0 / (1.0 + jnp.exp(-value))


def rows_of(half, quarter):
    return pl.ds(pl.multiple_of(half * 1024 + quarter * 256, 256), 256)


def half_of(half):
    return pl.ds(pl.multiple_of(half * 64, 64), 64)


def quarter_rows(buffer, half, quarter):
    return buffer[pl.ds(quarter * 4, 4), half_of(half)].reshape(256, buffer.shape[2])


def lanes(block):
    return pl.ds(pl.multiple_of(block * 256, 256), 256)


def token_column(buffer, block):
    first = buffer[:, 0:64, lanes(block)].reshape(1024, 256)
    return jnp.concatenate([first, buffer[:, 64:128, lanes(block)].reshape(1024, 256)], 0)


def scatter_quarter(scatters, half, quarter, partial, part):
    part[pl.ds(quarter * 4, 4), half_of(half)] = partial.reshape(4, 64, partial.shape[1])
    for index, scatter in enumerate(scatters):

        @pl.when(half == index)
        def _(scatter=scatter):
            scatter.to_twin(quarter * 2)
            scatter.to_twin(quarter * 2 + 1)


def ffn_kernel(
    hidden_ref, mlp_gain_ref, teacher_ref, mask_ref, gate_up_src, down_shard_ref,
    block_ref, back_ref, back_low_ref, sums_ref, weight_ref, down_grad_ref,
    tokens, grads, both, act_t, both_t, part, twin_part, slot, down_ref, down_part, down_slot, down_staged,
    grad_ref, square_ref, gain_sum, gate_up_ref, local,
    down_send, down_recv, leave_send, leave_recv, *sems,
):
    near = Neighbours()
    data = lax.axis_index("dp")
    neighbours = [{"tensor": device} for device in (near.up, near.down, near.side, near.twin)]
    neighbours = neighbours + [{"dp": device} for device in data_neighbours()]
    own = near.mine("own")
    norm_into(hidden_ref, mlp_gain_ref, tokens.at[own])
    fills = [
        pltpu.make_async_copy(
            gate_up_src.at[index * FF_UNITS : index * FF_UNITS + FF_UNITS],
            gate_up_ref.at[index * HIDDEN : index * HIDDEN + FF_UNITS], local.at[index],
        )
        for index in range(2)
    ]
    for fill in fills:
        fill.start()
    blank = jnp.zeros((HIDDEN - FF_UNITS, 2048), jnp.bfloat16)
    gate_up_ref[FF_UNITS:HIDDEN] = blank
    gate_up_ref[HIDDEN + FF_UNITS : 2 * HIDDEN] = blank
    down_ref[FF_UNITS:HIDDEN] = blank
    down_ref[0:FF_UNITS, lanes(data)] = down_shard_ref[...]
    greet(neighbours)
    a, g = (
        [Gather(near, buffer, sems[k + 2 * h], sems[k + 2 * h + 1], HALVES[h]) for h in range(2)]
        for buffer, k in ((tokens, 0), (grads, 4))
    )
    r, b = (
        [Scatter(near, part, twin_part, slot, sems[k + 2 * h], sems[k + 2 * h + 1], HALVES[h]) for h in range(2)]
        for k in (8, 12)
    )
    a[0].start()
    down = DataGather(down_shard_ref, lambda block: down_ref.at[0:FF_UNITS, lanes(block)], down_send, down_recv)
    down.start()
    for fill in fills:
        fill.wait()

    def forward(step, carry):
        at_steps(step, {
            0: [a[0].second, a[1].start, down.relay, a[0].third, a[1].from_side, a[0].fourth, down.arrive, pair(a[0], ORDER[0])],
            1: [pair(a[0], ORDER[1])],
            2: [a[0].fifth, summing(r[0], "side"), pair(a[0], ORDER[2])],
            3: [summing(r[0], "up", "upside"), a[1].from_down, a[1].from_up, pair(a[0], ORDER[3])],
            4: [summing(r[0], "downside", "down"), a[1].fourth, pair(a[1], ORDER[0])],
            5: [summing(r[0], "farside", "far"), pair(a[1], ORDER[1])],
            6: [summing(r[1], "side"), a[1].third, r[0].to_side, pair(a[1], ORDER[2])],
            7: [
                summing(r[1], "upside"), r[0].second, summing(r[1], "up", "down", "downside"), r[0].to_down,
                a[1].fifth, pair(a[1], ORDER[3]),
            ],
        })
        half, quarter = step // 4, near.quarter_at(step)
        rows = rows_of(half, quarter)
        product = nt(quarter_rows(tokens, half, quarter), gate_up_ref[...])
        both[rows, :] = product
        gate, up = product[:, :HIDDEN], product[:, HIDDEN:]
        act = low(gate * sigmoid(gate) * up)
        act_t[:, rows] = act.T
        scatter_quarter(r, half, quarter, low(nn(act, down_ref[...])), part)
        return carry

    lax.fori_loop(0, 8, forward, 0)
    square_ref[...] = jnp.zeros_like(square_ref)
    gain_sum[...] = jnp.zeros_like(gain_sum)

    def middle(half):
        def piece(index, carry):
            rows = pl.ds(pl.multiple_of(half * 64 + index * 16, 16), 16)
            output = hidden_ref[rows] + r[half].total(rows)
            block_ref[rows] = low(output)
            diff = output - teacher_ref[rows].astype(jnp.float32)
            weight = mask_ref[0, rows, 0:1]
            grad = mask_ref[1, rows, 0:1] * diff
            grad_ref[rows] = grad
            grads[own, rows] = low(grad)
            squares = jnp.sum(weight * jnp.sum(diff * diff, -1, keepdims=True), 0, keepdims=True)
            square_ref[...] += jnp.broadcast_to(squares, (8, 128))
            return carry

        lax.fori_loop(0, 4, piece, 0)

    r[0].to_up()
    r[1].to_side()
    r[1].sums("far", "farside")
    r[0].fourth()
    middle(0)
    g[0].start()
    r[1].second()
    g[0].from_down()
    g[0].from_up()
    r[1].to_down()
    r[1].to_up()
    g[0].from_side()
    g[0].third()
    r[0].finish()

    def turn():
        r[1].fourth()
        middle(1)
        r[1].finish()

    def backward(step, carry):
        at_steps(step, {
            0: [pair(g[0], ORDER[0])],
            1: [turn, summing(b[0], "side"), g[1].start, g[0].fifth, g[0].fourth, pair(g[0], ORDER[1])],
            2: [g[1].second, pair(g[0], ORDER[2])],
            3: [summing(b[0], "upside", "up"), pair(g[0], ORDER[3])],
            4: [summing(b[0], "downside", "down"), g[1].third, pair(g[1], ORDER[0])],
            5: [summing(b[0], "farside", "far"), g[1].fourth, summing(b[1], "side"), pair(g[1], ORDER[1])],
            6: [b[0].to_side, g[1].fifth, pair(g[1], ORDER[2])],
            7: [b[0].second, summing(b[1], "upside", "up"), pair(g[1], ORDER[3])],
        })
        half, quarter = step // 4, near.quarter_at(step)
        rows = rows_of(half, quarter)
        act_grad = nt(quarter_rows(grads, half, quarter), down_ref[...])
        gate, up = both[rows, :HIDDEN], both[rows, HIDDEN:]
        sigma = sigmoid(gate)
        gate_low = low(act_grad * up * sigma * (1.0 + gate * (1.0 - sigma)))
        up_low = low(act_grad * gate * sigma)
        both_low = jnp.concatenate([gate_low, up_low], 1)
        both_t[:, rows] = both_low.T
        scatter_quarter(b, half, quarter, low(nn(both_low, gate_up_ref[...])), part)
        return carry

    lax.fori_loop(0, 8, backward, 0)
    b[1].sums("downside", "down")
    b[0].to_down()
    b[0].to_up()

    def down_weights(step, carry):
        at_steps(step, {2: [summing(b[1], "far", "farside")]})
        down_part[:, lanes(step)] = low(nn(act_t[...], token_column(grads, step)))
        return carry

    lax.fori_loop(0, 8, down_weights, 0)
    place = DataPlace()
    leave = DataScatter(
        lambda block: down_part.at[:, lanes(block)],
        lambda other, rows: down_part[rows, lanes(place.block(0, other))],
        down_slot, down_staged, leave_send, leave_recv,
    )
    leave.start()

    def ending(half):
        b[half].fourth()

        def piece(index, carry):
            rows = pl.ds(pl.multiple_of(half * 64 + index * 16, 16), 16)
            value = b[half].total(rows)
            unit, scale = normalise(hidden_ref[rows])
            gain_sum[...] += value * unit
            grad = grad_ref[rows] + norm_back(value, unit, scale, mlp_gain_ref)
            back_ref[rows] = grad
            back_low_ref[rows] = low(grad)
            return carry

        lax.fori_loop(0, 4, piece, 0)

    def weights(step, carry):
        at_steps(step, {3: [b[1].to_side], 7: [b[1].second]})
        weight_ref[:, lanes(step)] = low(nn(both_t[...], token_column(tokens, step)))
        return carry

    lax.fori_loop(0, 8, weights, 0)
    ending(0)
    b[1].to_down()
    b[1].to_up()
    leave.relay()
    ending(1)
    total = jnp.sum(gain_sum[...], 0, keepdims=True)
    sums_ref[0:8, :] = jnp.zeros((8, 256), jnp.float32)
    for piece in range(8):
        sums_ref[8 + piece : 9 + piece, :] = total[:, piece * 256 : piece * 256 + 256]
    sums_ref[16:24, :] = jnp.concatenate([square_ref[...], square_ref[...]], 1)
    leave.result(down_grad_ref)
    for item in (down, leave, a[0], a[1], g[0], g[1], b[0], b[1]):
        item.finish()


def data_neighbours():
    place = DataPlace()
    return [place.block(shift, 0) for shift in range(1, 4)] + [place.block(0, 1)]


def run_ffn(hidden, gain, teacher, mask, gate_up, down_shard):
    rows, features = hidden.shape
    wide = jax.ShapeDtypeStruct((rows, features), jnp.float32)
    vmem = pl.BlockSpec(memory_space=pltpu.VMEM)
    counts = [7] * 4 + [Gather.copies] * 8 + [Scatter.copies] * 8
    semaphores = [pltpu.SemaphoreType.DMA((count,)) for count in counts]
    return pl.pallas_call(
        ffn_kernel,
        out_shape=(
            jax.ShapeDtypeStruct((rows, features), jnp.bfloat16),
            wide,
            jax.ShapeDtypeStruct((rows, features), jnp.bfloat16),
            jax.ShapeDtypeStruct((24, 256), jnp.float32),
            jax.ShapeDtypeStruct((2 * HIDDEN, features), jnp.bfloat16),
            jax.ShapeDtypeStruct((HIDDEN, 256), jnp.float32),
        ),
        in_specs=[vmem] * 4 + [pl.BlockSpec(memory_space=pl.ANY), vmem],
        out_specs=[vmem] * 6,
        scratch_shapes=[
            pltpu.VMEM((16, 128, 2048), jnp.bfloat16),
            pltpu.VMEM((16, 128, 2048), jnp.bfloat16),
            pltpu.VMEM((2048, 2 * HIDDEN), jnp.float32),
            pltpu.VMEM((HIDDEN, 2048), jnp.bfloat16),
            pltpu.VMEM((2 * HIDDEN, 2048), jnp.bfloat16),
            pltpu.VMEM((16, 128, 2048), jnp.bfloat16),
            pltpu.VMEM((8, 128, 2048), jnp.bfloat16),
            pltpu.VMEM((7, 128, 2048), jnp.bfloat16),
            pltpu.VMEM((HIDDEN, 2048), jnp.bfloat16),
            pltpu.VMEM((HIDDEN, 2048), jnp.bfloat16),
            pltpu.VMEM((7, HIDDEN, 256), jnp.bfloat16),
            pltpu.VMEM((HIDDEN, 256), jnp.bfloat16),
            pltpu.VMEM((128, 2048), jnp.float32),
            pltpu.VMEM((8, 128), jnp.float32),
            pltpu.VMEM((16, 2048), jnp.float32),
            pltpu.VMEM((2 * HIDDEN, 2048), jnp.bfloat16),
            pltpu.SemaphoreType.DMA((2,)),
        ]
        + semaphores,
        compiler_params=pltpu.CompilerParams(
            collective_id=1, has_side_effects=True, vmem_limit_bytes=63 << 20
        ),
        cost_estimate=pl.CostEstimate(flops=160 << 30, bytes_accessed=16 << 20, transcendentals=0),
        name="feed_forward",
    )(hidden, gain, teacher, mask, gate_up, down_shard)


def everyone():
    tensor, data = lax.axis_index("tensor"), lax.axis_index("dp")
    devices = [{"tensor": (tensor + shift) % 16} for shift in range(1, 16)]
    return devices + [{"dp": (data + shift) % 8} for shift in range(1, 8)]


class Fan:
    def __init__(self, axis, count, source, target, sends, receives):
        self.axis, self.count, self.source, self.target = axis, count, source, target
        self.sends, self.receives = sends, receives
        self.index = lax.axis_index(axis)

    def copy(self, shift):
        peer = (self.index + shift) % self.count
        return remote(
            self.source(peer), self.target(self.index), self.sends.at[shift],
            self.receives.at[shift], {self.axis: peer},
        )

    def start(self):
        for shift in range(1, self.count):
            self.copy(shift).start()

    def arrive(self):
        for shift in range(1, self.count):
            piece = self.target((self.index + self.count - shift) % self.count)
            peer = (self.index + shift) % self.count
            remote(
                piece, piece, self.sends.at[shift], self.receives.at[shift], {self.axis: peer}
            ).wait_recv()

    def finish(self):
        for shift in range(1, self.count):
            self.copy(shift).wait_send()


class DataPlace:
    def __init__(self):
        index = lax.axis_index("dp")
        self.x, self.z = index % 4, index // 4

    def block(self, shift, other):
        return ((self.z + other) % 2) * 4 + (self.x + shift) % 4


class DataGather:
    copies = 7

    def __init__(self, source, target, sends, receives):
        self.place = DataPlace()
        self.source, self.target, self.sends, self.receives = source, target, sends, receives

    def describe(self, key):
        place = self.place
        if key == 0:
            return self.copy(key, self.source, place.block(0, 0), place.block(0, 1))
        if key < 4:
            return self.copy(key, self.source, place.block(0, 0), place.block(key, 0))
        partner = place.block(0, 1)
        return self.copy(key, self.target(partner), partner, place.block(key - 3, 0))

    def copy(self, key, source, block, peer):
        return remote(
            source, self.target(block), self.sends.at[key], self.receives.at[key], {"dp": peer}
        )

    def start(self):
        for key in range(4):
            self.describe(key).start()

    def wait(self, key, block):
        piece = self.target(block)
        self.copy(key, piece, block, self.place.block(0, 1)).wait_recv()

    def relay(self):
        self.wait(0, self.place.block(0, 1))
        for key in range(4, 7):
            self.describe(key).start()

    def arrive(self):
        for shift in range(1, 4):
            self.wait(shift, self.place.block(4 - shift, 0))
            self.wait(3 + shift, self.place.block(4 - shift, 1))

    def finish(self):
        for key in range(7):
            self.describe(key).wait_send()


class DataScatter:
    copies = 7

    def __init__(self, part, own, slot, staged, sends, receives):
        self.place = DataPlace()
        self.part, self.own, self.slot, self.staged = part, own, slot, staged
        self.sends, self.receives = sends, receives

    def describe(self, key):
        place = self.place
        if key == 6:
            source, peer = self.staged, place.block(0, 1)
        else:
            shift, other = key // 2 + 1, key % 2
            source, peer = self.part(place.block(shift, other)), place.block(shift, 0)
        return remote(
            source, self.slot.at[key], self.sends.at[key], self.receives.at[key], {"dp": peer}
        )

    def start(self):
        for key in range(6):
            self.describe(key).start()

    def summed(self, other, rows, extra):
        total = self.own(other, rows).astype(jnp.float32)
        for key in range(other, 6, 2):
            total = total + self.slot[key, rows].astype(jnp.float32)
        if extra:
            total = total + self.slot[6, rows].astype(jnp.float32)
        return total

    def relay(self):
        for key in (1, 3, 5):
            self.describe(key).wait_recv()

        def piece(index, carry):
            rows = pl.ds(pl.multiple_of(index * 16, 16), 16)
            self.staged[rows] = low(self.summed(1, rows, False))
            return carry

        lax.fori_loop(0, self.staged.shape[0] // 16, piece, 0)
        self.describe(6).start()

    def result(self, output):
        for key in (0, 2, 4, 6):
            self.describe(key).wait_recv()

        def piece(index, carry):
            rows = pl.ds(pl.multiple_of(index * 16, 16), 16)
            output[rows] = self.summed(0, rows, True)
            return carry

        lax.fori_loop(0, self.staged.shape[0] // 16, piece, 0)

    def finish(self):
        for key in range(7):
            self.describe(key).wait_send()


def tile_sum(first, second, axes, sems):
    tensor, data = lax.axis_index("tensor"), lax.axis_index("dp")
    one = Fan("tensor", 16, lambda peer: first.at[tensor], lambda index: first.at[index], sems[0], sems[1])
    two = Fan("dp", 8, lambda peer: second.at[data], lambda index: second.at[index], sems[2], sems[3])
    return one, two


def entry_kernel(
    input_ref, attn_gain_ref, mix_ref, small_ref, count_ref, pos_ref, gate_ref, up_ref, out_ref,
    gathered_ref, taps_ref, gain_ref, total_ref, gate_up_full_ref, out_full_ref, spread_ref,
    far0, far1, far2, far3, far4, far5, far6, far7, far8, far9, far10, far11,
    proj_ref, mix_full_ref, heads_ref,
    query_ref, key_ref, inv_ref, kc_ref, score_ref, step_ref, state_ref, update_ref, raw_ref, save_sems, mix_parts,
    tokens, small, counts, count_rows, free_ref, shift_ref,
    mix_send, mix_recv, wide_send, wide_recv, small_send, small_recv,
    out_send, out_recv, all_send, all_recv, count_send, count_recv, row_send, row_recv, local, *sems,
):
    near = Neighbours()
    tensor, data = lax.axis_index("tensor"), lax.axis_index("dp")
    own = near.mine("own")
    block_rows = pl.ds(pl.multiple_of(data * 256, 256), 256)

    def mix_rows(block):
        return mix_parts.at[:, pl.ds(pl.multiple_of(block * 256, 256), 256)]

    def gate_lanes(block):
        return gate_up_full_ref.at[0:FF_UNITS, pl.ds(pl.multiple_of(block * 256, 256), 256)]

    def up_lanes(block):
        return gate_up_full_ref.at[FF_UNITS : 2 * FF_UNITS, pl.ds(pl.multiple_of(block * 256, 256), 256)]

    def lanes_of_data(block):
        return out_full_ref.at[tensor, :, pl.ds(pl.multiple_of(block * 256, 256), 256)]

    gate_own = pltpu.make_async_copy(gate_ref, gate_lanes(data), local.at[0])
    up_own = pltpu.make_async_copy(up_ref, up_lanes(data), local.at[3])
    out_own = pltpu.make_async_copy(out_ref, lanes_of_data(data), local.at[1])
    gate_own.start()
    up_own.start()
    out_own.start()
    norm_into(input_ref, attn_gain_ref, tokens.at[own])
    mix_parts[:, block_rows] = mix_ref[...]
    small[data] = small_ref[...]
    counts[tensor] = count_ref[...]
    greet(everyone())
    a = [Gather(near, tokens, sems[2 * h], sems[2 * h + 1], HALVES[h]) for h in range(2)]
    mix = DataGather(mix_ref, mix_rows, mix_send, mix_recv)
    wide = DataGather(gate_ref, gate_lanes, wide_send, wide_recv)
    wide_up = DataGather(up_ref, up_lanes, sems[8], sems[9])
    tiny = Fan("dp", 8, lambda peer: small.at[data], lambda index: small.at[index], small_send, small_recv)
    outs = Fan("dp", 8, lambda peer: out_ref, lanes_of_data, out_send, out_recv)
    one, two = tile_sum(counts, count_rows, None, (count_send, count_recv, row_send, row_recv))
    everything = Gather(near, out_full_ref, all_send, all_recv)
    a[0].start()
    outs.start()
    tiny.start()
    mix.start()
    one.start()

    def counted():
        one.arrive()
        count_rows[data] = jnp.sum(counts[...], 0)
        two.start()

    def outer():
        out_own.wait()
        outs.arrive()
        everything.start()

    def ready():
        tiny.arrive()
        table = jnp.sum(small[:, 0:16].astype(jnp.float32), 0)
        for block in range(8):
            for part in range(2):
                line = small[block, 16:32].astype(jnp.float32)[part : part + 1]
                first = block * 256 + part * 128
                mix_full_ref[first : first + 128, 384:512] = low(jnp.broadcast_to(line, (128, 128)).T)
        for tap in range(4):
            for field in range(3):
                row = tap * 3 + field
                taps_ref[tap : tap + 1, field * 128 : field * 128 + 128] = table[row : row + 1]
        gain_ref[0:1, :] = table[12:13]

    def head_rows(half):
        def place(block):
            return heads_ref.at[pl.ds(pl.multiple_of(block * 128 + half * 64, 64), 64)]

        return place

    def target_rows(half):
        return lambda index: spread_ref.at[index, HALVES[half].whole]

    exchanges = [
        Fan("tensor", 16, head_rows(h), target_rows(h), sems[4 + 2 * h], sems[5 + 2 * h]) for h in range(2)
    ]
    keep = pltpu.make_async_copy(tokens, gathered_ref, local.at[2])
    saves = [
        pltpu.make_async_copy(source, target, save_sems.at[index])
        for index, (source, target) in enumerate(zip(
            (
                proj_ref, mix_full_ref, heads_ref, query_ref, key_ref, inv_ref, kc_ref, score_ref, step_ref,
                state_ref, update_ref, raw_ref,
            ),
            (far0, far1, far2, far3, far4, far5, far6, far7, far8, far9, far10, far11),
        ))
    ]
    a[0].second()
    a[1].start()
    mix.relay()
    a[0].third()
    counted()
    a[0].fourth()
    ready()
    a[1].second()
    outer()
    a[0].fifth()
    mix.arrive()
    wide.start()
    wide_up.start()
    for field in range(3):
        mix_full_ref[:, field * 128 : field * 128 + 128] = mix_parts[field]

    def per_sequence(sequence, carry):
        def project(step, inner):
            at_steps(sequence * 4 + step, {
                0: [pair(a[0], ORDER[0])],
                1: [pair(a[0], ORDER[1])],
                2: [pair(a[0], ORDER[2])],
                3: [a[1].third, everything.second, pair(a[0], ORDER[3])],
                4: [pair(a[1], ORDER[0])],
                5: [pair(a[1], ORDER[1])],
                6: [pair(a[1], ORDER[2])],
                7: [pair(a[1], ORDER[3]), keep.start, saves[1].start],
            })
            quarter = near.quarter_at(step)
            product = nn(quarter_rows(tokens, sequence, quarter), mix_full_ref[...])
            for item in range(4):
                rows = pl.ds(pl.multiple_of((quarter * 4 + item) * 128 + sequence * 64, 64), 64)
                proj_ref[rows, :] = product[item * 64 : item * 64 + 64]
            return inner

        lax.fori_loop(0, 4, project, 0)
        mixer_forward(
            proj_ref, pos_ref, taps_ref, gain_ref,
            heads_ref, query_ref, key_ref, inv_ref, kc_ref, score_ref, step_ref, state_ref, update_ref, raw_ref,
            free_ref, shift_ref, sequence,
            lambda: at_steps(sequence, {0: [a[1].fourth, wide.relay, wide_up.relay], 1: [everything.fourth, saves[0].start]}),
        )
        at_steps(sequence, {
            0: [exchanges[0].start, everything.third, a[1].fifth],
            1: [exchanges[1].start],
        })
        return carry

    lax.fori_loop(0, 2, per_sequence, 0)
    spread_ref[tensor] = heads_ref[pl.ds(pl.multiple_of(tensor * 128, 128), 128)]
    for save in (saves[2:]):
        save.start()
    everything.fifth()
    two.arrive()
    total_ref[...] = jnp.sum(count_rows[...], 0)
    everything.from_twin(*NAMES)
    wide.arrive()
    wide_up.arrive()
    for save in saves:
        save.wait()
    gate_own.wait()
    up_own.wait()
    keep.wait()
    for exchange in exchanges:
        exchange.arrive()
    for item in (a[0], a[1], mix, wide, wide_up, tiny, outs, one, two, everything, exchanges[0], exchanges[1]):
        item.finish()


def dma(*counts):
    return [pltpu.SemaphoreType.DMA((count,)) for count in counts]


def kept_shapes():
    shape = jax.ShapeDtypeStruct
    rows = shape((2048, CHUNK), jnp.bfloat16)
    return (shape((2048, WIDE), jnp.float32), shape((2048, WIDE), jnp.bfloat16), rows) + saved_shapes()


def kept_buffers():
    return [pltpu.VMEM(item.shape, item.dtype) for item in kept_shapes()]


def run_entry(tokens, attn_gain, mix_shard, small, count, pos, gate_t, up_t, out_weight):
    vmem, hbm = pl.BlockSpec(memory_space=pltpu.VMEM), pl.BlockSpec(memory_space=pl.ANY)
    half, full = jnp.bfloat16, jnp.float32
    shape = jax.ShapeDtypeStruct
    return pl.pallas_call(
        entry_kernel,
        out_shape=(
            shape((16, 128, 2048), half),
            shape((8, 384), full),
            shape((8, CHUNK), full),
            shape((8, 128), full),
            shape((2 * FF_UNITS, 2048), half),
            shape((16, 128, 2048), half),
            shape((16, 128, CHUNK), half),
        )
        + kept_shapes(),
        in_specs=[vmem] * 6 + [hbm] * 3,
        out_specs=[hbm, vmem, vmem, vmem, hbm, hbm, vmem] + [hbm] * 12,
        scratch_shapes=kept_buffers()
        + dma(12)
        + [
            pltpu.VMEM((3, 2048, CHUNK), half),
            pltpu.VMEM((16, 128, 2048), half),
            pltpu.VMEM((8, 32, 128), half),
            pltpu.VMEM((16, 8, 128), full),
            pltpu.VMEM((8, 8, 128), full),
            pltpu.VMEM((16, CHUNK, CHUNK), full),
            pltpu.VMEM((16, CHUNK, CHUNK), full),
        ]
        + dma(7, 7, 7, 7, 8, 8, 8, 8, 17, 17, 16, 16, 8, 8, 4, 17, 17, 17, 17, 16, 16, 16, 16, 7, 7),
        compiler_params=pltpu.CompilerParams(
            collective_id=2, has_side_effects=True, vmem_limit_bytes=62 << 20
        ),
        cost_estimate=pl.CostEstimate(flops=60 << 30, bytes_accessed=16 << 20, transcendentals=0),
        name="entry",
    )(tokens, attn_gain, mix_shard, small, count, pos, gate_t, up_t, out_weight)


SMALL = 16


def exit_kernel(
    out_full_ref, attention_ref, ffn_part_ref, gathered_ref, hidden_grad_ref, pos_ref, taps_ref, gain_ref, input_ref, attn_gain_ref, sums_ref,
    far0, far1, far2, far3, far4, far5, far6, far7, far8, far9, far10, far11,
    input_grad_ref, ffn_ref, qkv_grad_ref, small_grad_ref, out_grad_ref, total_ref,
    proj_ref, mix_ref, heads_ref,
    query_ref, key_ref, inv_ref, kc_ref, score_ref, step_ref, state_ref, update_ref, raw_ref, load_sems, weight_ref,
    grad, attention, proj_low, taps_grad, gain_grad,
    back_ref, pull_ref, flow_ref, enter_ref, pre_ref,
    part, twin_part, slot, ffn_own, ffn_slot, ffn_staged, parts, part_slot, part_staged, outs, out_slot, out_staged,
    proj_t, tile, sums, sum_rows,
    head_send, head_recv, gather_send, gather_recv, ffn_send, ffn_recv, mix_send, mix_recv,
    outs_send, outs_recv, sum_send, sum_recv, row_send, row_recv, local, *sems,
):
    near = Neighbours()
    tensor, data = lax.axis_index("tensor"), lax.axis_index("dp")
    own = near.mine("own")
    place = DataPlace()

    loads = [
        pltpu.make_async_copy(ffn_part_ref.at[:, lanes(place.block(0, other))], ffn_own.at[other], local.at[other])
        for other in range(2)
    ]
    for copy in loads:
        copy.start()
    fill = pltpu.make_async_copy(out_full_ref, part, local.at[5])
    fill.start()
    sources = (far0, far1, far2, far3, far4, far5, far6, far7, far8, far9, far10, far11)
    places = (
        proj_ref, mix_ref, heads_ref, query_ref, key_ref, inv_ref, kc_ref, score_ref, step_ref, state_ref,
        update_ref, raw_ref,
    )
    saves = [
        pltpu.make_async_copy(source, target, load_sems.at[index])
        for index, (source, target) in enumerate(zip(sources, places))
    ]
    for copy in saves:
        copy.start()
    base = pltpu.make_async_copy(hidden_grad_ref, input_grad_ref, local.at[4])
    base.start()
    attention[own] = attention_ref[...]
    greet(everyone())
    ffn = DataScatter(
        lambda block: ffn_part_ref.at[:, lanes(block)], lambda other, rows: ffn_own[other, rows],
        ffn_slot, ffn_staged, ffn_send, ffn_recv,
    )
    ffn.start()
    gather = Gather(near, attention, gather_send, gather_recv)
    gather.start()
    fill.wait()

    def head_grads(head, carry):
        flow_ref[head] = low(nt(attention_ref[...], part[head]))
        return carry

    lax.fori_loop(0, 16, head_grads, 0)

    def head_rows(block):
        return grad.at[pl.ds(pl.multiple_of(block * 128, 128), 128)]

    exchange = Fan("tensor", 16, lambda peer: flow_ref.at[peer], head_rows, head_send, head_recv)
    exchange.start()
    grad[pl.ds(pl.multiple_of(tensor * 128, 128), 128)] = flow_ref[tensor]
    exchange.arrive()
    exchange.finish()
    for copy in saves:
        copy.wait()
    taps_grad[...] = jnp.zeros_like(taps_grad)
    gain_grad[...] = jnp.zeros_like(gain_grad)
    scatters = [
        Scatter(near, part, twin_part, slot, sems[2 * h], sems[2 * h + 1], HALVES[h]) for h in range(2)
    ]

    def per_sequence(sequence, carry):
        mixer_backward(
            grad, proj_ref, pos_ref, taps_ref, gain_ref,
            query_ref, key_ref, inv_ref, kc_ref, score_ref, step_ref, state_ref, update_ref, raw_ref,
            proj_low, taps_grad, gain_grad,
            back_ref, pull_ref, flow_ref, enter_ref, pre_ref, sequence,
            lambda: at_steps(sequence, {}),
            lambda: at_steps(sequence, {0: [gather.second], 1: [gather.third, scatters[0].second]}),
        )

        def flip(step, inner):
            quarter = near.quarter_at(step)
            proj_t[:, rows_of(sequence, quarter)] = quarter_values(sequence, quarter).T[:400]
            return inner

        lax.fori_loop(0, 4, flip, 0)
        at_steps(sequence, {0: [lambda: partials(0), scatters[0].first]})
        return carry

    def quarter_values(sequence, quarter):
        pieces = []
        for item in range(4):
            rows = pl.ds(pl.multiple_of((quarter * 4 + item) * 128 + sequence * 64, 64), 64)
            pieces.append(proj_low[rows, :])
        return jnp.concatenate(pieces, 0)

    def partials(sequence):
        def backward(step, inner):
            quarter = near.quarter_at(step)
            values = quarter_values(sequence, quarter)
            keep = lax.broadcasted_iota(jnp.int32, (256, WIDE), 1) <= 384
            partial = low(nt(jnp.where(keep, values, jnp.zeros_like(values)), mix_ref[...]))
            scatter_quarter(scatters, sequence, quarter, partial, part)
            return inner

        lax.fori_loop(0, 4, backward, 0)

    lax.fori_loop(0, 2, per_sequence, 0)

    def fetch(step):
        return pltpu.make_async_copy(gathered_ref.at[:, :, lanes(step)], tile.at[step % 2], local.at[2 + step % 2])

    fetch(0).start()
    partials(1)
    table = jnp.concatenate([taps_grad[...], gain_grad[...]], 1)

    def weights(step, carry):
        @pl.when(step < 7)
        def _():
            fetch(step + 1).start()

        fetch(step).wait()
        first = tile[step % 2, :, 0:64].reshape(1024, 256)
        column = jnp.concatenate([first, tile[step % 2, :, 64:128].reshape(1024, 256)], 0)
        product = nn(proj_t[...], column)
        parts[0:400, lanes(step)] = low(product)
        at_steps(step, {1: [scatters[1].first], 3: [gather.fourth], 5: [scatters[0].third]})
        return carry

    lax.fori_loop(0, 8, weights, 0)
    pick_row = lax.broadcasted_iota(jnp.int32, (CHUNK, 2048), 0)
    pick_lane = lax.broadcasted_iota(jnp.int32, (CHUNK, 2048), 1)
    wanted = (pick_lane // 256) * 16 + pick_lane % 256
    select = ((pick_row == wanted) & (pick_lane % 256 < 16)).astype(jnp.bfloat16)
    for tap in range(4):
        for field in range(3):
            row = tap * 3 + field
            pull_ref[0, row : row + 1, :] = taps_grad[tap : tap + 1, field * 128 : field * 128 + 128]
    pull_ref[0, 12:13, :] = gain_grad[0:1, :]
    small = nn(low(pull_ref[0, 0:16, :]), select)
    small_row = lax.broadcasted_iota(jnp.int32, (16, 2048), 0)
    moved = jnp.concatenate([small[15:16], small[0:15]], 0)
    beta_row = parts[384:400, :].astype(jnp.float32)
    parts[384:400, :] = low(jnp.where(small_row == 0, beta_row, moved))
    mix = DataScatter(
        lambda block: parts.at[:, lanes(block)],
        lambda other, rows: parts[rows, lanes(place.block(0, other))],
        part_slot, part_staged, mix_send, mix_recv,
    )
    mix.start()
    scatters[1].second()
    gather.fifth()
    gather.from_twin(*NAMES)

    def out_weights(step, carry):
        outs[:, lanes(step)] = low(tn(heads_ref[...], attention[:, :, lanes(step)].reshape(2048, 256)))
        return carry

    lax.fori_loop(0, 8, out_weights, 0)
    out_scatter = DataScatter(
        lambda block: outs.at[:, lanes(block)],
        lambda other, rows: outs[rows, lanes(place.block(0, other))],
        out_slot, out_staged, outs_send, outs_recv,
    )
    out_scatter.start()
    for copy in loads:
        copy.wait()
    ffn.relay()
    base.wait()

    def ending(half):
        def strip(rows, total):
            value = scatters[half].total(rows)
            unit, scale = normalise(input_ref[rows].astype(jnp.float32))
            input_grad_ref[rows] += norm_back(value, unit, scale, attn_gain_ref)
            return total + value * unit

        scatters[half].fourth()
        return strips(64, strip, half * 64)(jnp.zeros((16, 2048), jnp.float32))

    total = ending(0)
    scatters[1].third()
    mix.relay()
    out_scatter.relay()
    total = total + ending(1)
    total = jnp.sum(total, 0, keepdims=True)
    sums[tensor, 8:24] = sums_ref[8:24]
    for piece in range(8):
        sums[tensor, piece : piece + 1] = total[:, piece * 256 : piece * 256 + 256]
    one, two = tile_sum(sums, sum_rows, None, (sum_send, sum_recv, row_send, row_recv))
    one.start()
    one.arrive()
    sum_rows[data] = jnp.sum(sums[...], 0)
    two.start()
    ffn.result(ffn_ref)
    two.arrive()
    total_ref[...] = jnp.sum(sum_rows[...], 0)
    mix.result(weight_ref)
    for field in range(3):
        qkv_grad_ref[field] = weight_ref[field * 128 : field * 128 + 128, :].T
    small_grad_ref[...] = weight_ref[384:400, :]
    out_scatter.result(out_grad_ref)
    for item in (gather, ffn, scatters[0], scatters[1], mix, out_scatter, one, two):
        item.finish()


def run_exit(
    out_full, attention, ffn_part, gathered, hidden_grad, proj, pos, taps, gain, mix, heads, tokens, attn_gain, sums, saved
):
    vmem, hbm = pl.BlockSpec(memory_space=pltpu.VMEM), pl.BlockSpec(memory_space=pl.ANY)
    half, full = jnp.bfloat16, jnp.float32
    shape = jax.ShapeDtypeStruct
    return pl.pallas_call(
        exit_kernel,
        out_shape=(
            shape((128, 2048), full),
            shape((2 * HIDDEN, 256), full),
            shape((3, 256, CHUNK), full),
            shape((16, 256), full),
            shape((CHUNK, 256), full),
            shape((24, 256), full),
        ),
        in_specs=[hbm, vmem] + [hbm] * 3 + [vmem] * 6 + [hbm] * 12,
        out_specs=[vmem] * 6,
        scratch_shapes=kept_buffers()
        + dma(12)
        + [
            pltpu.VMEM((400, 256), full),
            pltpu.VMEM((2048, CHUNK), half),
            pltpu.VMEM((16, 128, 2048), half),
            pltpu.VMEM((2048, WIDE), half),
            pltpu.VMEM((8, 384), full),
            pltpu.VMEM((8, CHUNK), full),
            pltpu.VMEM((16, CHUNK, CHUNK), half),
            pltpu.VMEM((16, CHUNK, CHUNK), full),
            pltpu.VMEM((16, CHUNK, CHUNK), half),
            pltpu.VMEM((16, CHUNK, CHUNK), full),
            pltpu.VMEM((1024, 384), full),
            pltpu.VMEM((16, 128, 2048), half),
            pltpu.VMEM((8, 128, 2048), half),
            pltpu.VMEM((7, 128, 2048), half),
            pltpu.VMEM((2, 2 * HIDDEN, 256), half),
            pltpu.VMEM((7, 2 * HIDDEN, 256), half),
            pltpu.VMEM((2 * HIDDEN, 256), half),
            pltpu.VMEM((400, 2048), half),
            pltpu.VMEM((7, 400, 256), half),
            pltpu.VMEM((400, 256), half),
            pltpu.VMEM((CHUNK, 2048), half),
            pltpu.VMEM((7, CHUNK, 256), half),
            pltpu.VMEM((CHUNK, 256), half),
            pltpu.VMEM((400, 2048), half),
            pltpu.VMEM((2, 16, 128, 256), half),
            pltpu.VMEM((16, 24, 256), full),
            pltpu.VMEM((8, 24, 256), full),
        ]
        + dma(16, 16, 17, 17, 7, 7, 7, 7, 7, 7, 16, 16, 8, 8, 6, 16, 16, 16, 16),
        compiler_params=pltpu.CompilerParams(
            collective_id=3, has_side_effects=True, vmem_limit_bytes=63 << 20
        ),
        cost_estimate=pl.CostEstimate(flops=60 << 30, bytes_accessed=16 << 20, transcendentals=0),
        name="exit",
    )(
        out_full, attention, ffn_part, gathered, hidden_grad, pos, taps, gain, tokens, attn_gain, sums, proj, mix, heads,
        *saved,
    )


def token_places(segment):
    length = segment.shape[1]
    before = jnp.sum((segment[:, None, :] < segment[:, :, None]).astype(jnp.int32), -1)
    place = jnp.arange(length, dtype=jnp.int32)[None, :] - before
    return jnp.transpose(place.reshape(2, 8, CHUNK), (1, 0, 2)).reshape(16, CHUNK).astype(jnp.float32)


def f32(value):
    return value.astype(jnp.float32)


def body(
    inputs, teacher, segment_ids, padding, attn_gain, qkv_weight, beta_weight, conv_taps, head_gain,
    out_weight, mlp_gain, gate_weight, up_weight, down_weight,
):
    hidden_units = gate_weight.shape[1]
    rows = 128
    features = inputs.shape[2]

    small = jnp.concatenate([conv_taps.reshape(12, 16), head_gain.reshape(1, 16)], 0)
    lane = jnp.arange(CHUNK)[None, :] // 16 == lax.axis_index("dp")
    small = jnp.where(lane, jnp.tile(jnp.pad(small, ((0, 3), (0, 0))), (1, 8)), 0)
    small = jnp.concatenate([small, jnp.pad(beta_weight.reshape(2, CHUNK), ((0, 14), (0, 0)))], 0)
    mix_shard = jnp.transpose(qkv_weight, (1, 0, 2))
    gate_t, up_t = jnp.transpose(gate_weight), jnp.transpose(up_weight)
    count = jnp.broadcast_to(f32(jnp.sum(padding)), (8, 128))

    tokens = inputs.reshape(rows, features)
    attn_gain_row = attn_gain.reshape(1, features)
    mlp_gain_row = mlp_gain.reshape(1, features)
    pos = token_places(segment_ids)
    (
        gathered, taps, gain, total, gate_up, out_full, spread, proj, mix_full, heads, *saved
    ) = run_entry(tokens, attn_gain_row, mix_shard, small, count, pos, gate_t, up_t, out_weight)
    valid = total[0, 0]
    scale = 16 * 1024 / valid
    heads_rows = jnp.transpose(spread, (1, 0, 2)).reshape(rows, features)
    hidden = f32(tokens) + nn(heads_rows, out_full.reshape(features, features))

    mask = f32(padding.reshape(rows, 1))
    masks = jnp.broadcast_to(jnp.stack([mask, scale * mask]), (2, rows, CHUNK))
    output, hidden_grad, attention_low, sums, ffn_part, down_grad = run_ffn(
        hidden, mlp_gain_row, teacher.reshape(rows, features), masks, gate_up, down_weight
    )
    input_grad, ffn_grads, qkv_grad, small_grads, out_grad, totals = run_exit(
        out_full, attention_low, ffn_part, gathered, hidden_grad, proj, pos, taps, gain, mix_full, heads, tokens,
        attn_gain_row, sums, saved,
    )
    loss = totals[16, 0] / (valid * features)
    small_grad = small_grads[1:14, :16]
    shape = (2, 64, features)
    return (
        output.reshape(shape),
        loss,
        input_grad.reshape(shape),
        totals[:8].reshape(features),
        jnp.transpose(qkv_grad, (1, 0, 2)),
        jnp.transpose(small_grads[0:1]),
        small_grad[:12].reshape(4, 3, 1, 16),
        small_grad[12:].reshape(1, 16),
        out_grad,
        totals[8:16].reshape(features),
        jnp.transpose(ffn_grads[:hidden_units]),
        jnp.transpose(ffn_grads[HIDDEN : HIDDEN + hidden_units]),
        down_grad[:hidden_units],
    )


def solution(mesh):
    in_specs = (
        P("dp", "tensor", None),
        P("dp", "tensor", None),
        P("dp", None),
        P("dp", "tensor"),
        P(),
        P("dp", None, "tensor"),
        P("dp", "tensor"),
        P(None, None, "tensor", "dp"),
        P("tensor", "dp"),
        P("tensor", "dp"),
        P(),
        P("dp", "tensor"),
        P("dp", "tensor"),
        P("tensor", "dp"),
    )
    out_specs = (
        P("dp", "tensor", None),
        P(),
        P("dp", "tensor", None),
        P(),
        P("dp", None, "tensor"),
        P("dp", "tensor"),
        P(None, None, "tensor", "dp"),
        P("tensor", "dp"),
        P("tensor", "dp"),
        P(),
        P("dp", "tensor"),
        P("dp", "tensor"),
        P("tensor", "dp"),
    )
    return jax.shard_map(body, mesh=mesh, in_specs=in_specs, out_specs=out_specs, check_vma=False)
```
